32 devices in a mesh: bucket: 4 (over y, x), batch: 8 (over z, core).
Axes of the slice: x: 2, y: 2, z: 4, core: 2. Of those that a mesh axis runs over, the one named last changes fastest.
Arguments:
- images: float32 [8, 4, 5, 256, 256], P('batch', 'bucket'), may hold values from -6 to 6
- timesteps: int32 [8, 4, 5], P('batch', 'bucket'), may hold values from 0 to 999, as said below
- counts: int32 [8, 4], P('batch', 'bucket'), may hold values from 3 to 5, as said below
- source: int32 [8, 4], P('batch', 'bucket'), may hold values from 0 to 3, as said below
- cotangent: float32 [8, 4, 4, 256, 256], P('batch', 'bucket'), may hold values from -6 to 6
- first_gain: float32 [256], replicated, may hold values from 0.25 to 1.75
- first_shift: float32 [256], replicated, may hold values from -1.8 to 1.8
- first_conv: float32 [3, 3, 256, 256], replicated, may hold values from -0.125 to 0.125
- embed_weight: float32 [512, 256], replicated, may hold values from -0.25 to 0.25
- embed_bias: float32 [256], replicated, may hold values from -1.8 to 1.8
- second_gain: float32 [256], replicated, may hold values from 0.25 to 1.75
- second_shift: float32 [256], replicated, may hold values from -1.8 to 1.8
- second_conv: float32 [3, 3, 256, 256], replicated, may hold values from -0.125 to 0.125
- second_bias: float32 [256], replicated, may hold values from -1.8 to 1.8
- attend_gain: float32 [256], replicated, may hold values from 0.25 to 1.75
- attend_shift: float32 [256], replicated, may hold values from -1.8 to 1.8
- triple_weight: float32 [256, 768], replicated, may hold values from -0.375 to 0.375
- query_bias: float32 [256], replicated, may hold values from -1.8 to 1.8
- value_bias: float32 [256], replicated, may hold values from -1.8 to 1.8
- output_weight: float32 [256, 256], replicated, may hold values from -1.5 to 1.5
- output_bias: float32 [256], replicated, may hold values from -1.8 to 1.8
Outputs:
- output: float32 [8, 4, 4, 256, 256], P('batch', 'bucket')
- image_gradient: float32 [8, 4, 5, 256, 256], P('batch', 'bucket')
- first_gain_gradient: float32 [256], replicated
- first_shift_gradient: float32 [256], replicated
- first_conv_gradient: float32 [3, 3, 256, 256], replicated
- embed_weight_gradient: float32 [512, 256], replicated
- embed_bias_gradient: float32 [256], replicated
- second_gain_gradient: float32 [256], replicated
- second_shift_gradient: float32 [256], replicated
- second_conv_gradient: float32 [3, 3, 256, 256], replicated
- second_bias_gradient: float32 [256], replicated
- attend_gain_gradient: float32 [256], replicated
- attend_shift_gradient: float32 [256], replicated
- triple_weight_gradient: float32 [256, 768], replicated
- query_bias_gradient: float32 [256], replicated
- value_bias_gradient: float32 [256], replicated
- output_weight_gradient: float32 [256, 256], replicated
- output_bias_gradient: float32 [256], replicated
The draws below stay inside these ranges and needn't reach their ends.
Inputs may be any that keep to these rules, and one draw needn't show every extreme that they name: Each device holds 4 images, one fewer, or one more; in each batch column the counts add up to 4 times 4, as many devices hold one more as hold one fewer, and at least a third of the column's devices, rounded up, hold one more. `source`: A device holding one image fewer than 4 names a device of its batch column that holds one more, each of those named by exactly one device; every other device names its own bucket index. Images of bucket index b have timesteps from the integer part of b * 250 up to, but excluding, that of (b + 1) * 250.
All inputs are finite; a program needn't handle non-finite values.
Results may differ from the reference program's by a relative error of at most 0.014.
The reference program's roundings to bfloat16 on the way count: a program that leaves them out, or rounds other values in their place, can miss the bound.
Values sent between devices are 32-bit elements; how exact they have to be, the bound alone decides.
No kernel may reach another device: no remote copies, remote signals or barrier semaphores. Data moves between devices by JAX's collectives and lax.ppermute only.
A program may use at most 128 MiB of HBM per device.

```python
import math
import jax
import jax.numpy as jnp
from jax import lax

C = 256
TEMB = 512
GROUPS = 32
SIDE = 16
WORK = 4
STEPS = 1000
TOK = 256
SLOTS = 5
N_BUCKET = 4
N_BATCH = 8


def column_plan(key):
    key = jax.random.fold_in(key, 11)
    column_keys = jax.random.split(key, N_BATCH)

    def one_column(column_key):
        order_key, flip_key = jax.random.split(column_key)
        order = jax.random.permutation(order_key, N_BUCKET).astype(jnp.int32)
        heavy = order[0::2]
        light = order[1::2]
        pairs = jnp.arange(N_BUCKET // 2)
        forced = (N_BUCKET + 2) // 3
        coins = jax.random.randint(flip_key, (N_BUCKET // 2,), 0, 2)
        flips = ((pairs < forced) | (coins == 1)).astype(jnp.int32)
        held = jnp.full((N_BUCKET,), WORK, jnp.int32).at[heavy].add(flips).at[light].add(-flips)
        named = jnp.arange(N_BUCKET, dtype=jnp.int32).at[light].set(jnp.where(flips == 1, heavy, light))
        return (held, named)
    return jax.vmap(one_column)(column_keys)


def draw_counts(key, part):
    return column_plan(key)[0]


def draw_source(key, part):
    return column_plan(key)[1]


def draw_timesteps(key, part):
    key = jax.random.fold_in(key, 5)
    buckets = jnp.arange(N_BUCKET, dtype=jnp.int32)
    lowest = buckets * STEPS // N_BUCKET
    spans = (buckets + 1) * STEPS // N_BUCKET - lowest
    raw = jax.random.randint(key, (N_BATCH, N_BUCKET, SLOTS), 0, 1 << 20)
    return (lowest[None, :, None] + raw % spans[None, :, None]).astype(jnp.int32)


def level_of(key, shape, pieces, low, top_value):
    level, own = 1.0, jax.random.fold_in(key, 6)
    for position, blocks in pieces:
        heights = jnp.exp(jax.random.uniform(jax.random.fold_in(own, position), (blocks,), jnp.float32, low / len(pieces), top_value / len(pieces)))
        level = level * jnp.repeat(heights, shape[position] // blocks).reshape([-1 if axis == position else 1 for axis in range(len(shape))])
    return level


def centred(own_key, shape, deviation, reach, cuts=(), held_as=jnp.bfloat16):
    values = jax.random.normal(own_key, shape, jnp.float32) * deviation
    if len(cuts) > 0:
        values = level_of(own_key, shape, cuts, -0.22, 0.18) * values
    return jnp.clip(values, min=-reach, max=reach).astype(held_as)


def setup_inputs(seed: int = 0) -> dict:
    splits = jax.random.split(jax.random.key(seed), 22)
    return {
        "images": centred(splits[0], (N_BATCH, N_BUCKET, SLOTS, TOK, C), 1.0, 6.0, ((0, 8), (1, 4)), jnp.float32),
        "timesteps": draw_timesteps(jax.random.fold_in(splits[21], 71), 0),
        "counts": draw_counts(jax.random.fold_in(splits[21], 71), 0),
        "source": draw_source(jax.random.fold_in(splits[21], 71), 0),
        "cotangent": centred(splits[4], (N_BATCH, N_BUCKET, WORK, TOK, C), 1.0, 6.0, ((0, 8), (1, 4)), jnp.float32),
        "first_gain": jnp.clip(1.0 + 0.15 * jax.random.normal(splits[5], (C,), jnp.float32), 0.25, 1.75),
        "first_shift": centred(splits[6], (C,), 0.3, 1.8, (), jnp.float32),
        "first_conv": centred(splits[7], (3, 3, C, C), (9 * C) ** -0.5, 0.125, (), jnp.float32),
        "embed_weight": centred(splits[8], (TEMB, C), TEMB ** -0.5, 0.25, (), jnp.float32),
        "embed_bias": centred(splits[9], (C,), 0.3, 1.8, (), jnp.float32),
        "second_gain": jnp.clip(1.0 + 0.15 * jax.random.normal(splits[10], (C,), jnp.float32), 0.25, 1.75),
        "second_shift": centred(splits[11], (C,), 0.3, 1.8, (), jnp.float32),
        "second_conv": centred(splits[12], (3, 3, C, C), (9 * C) ** -0.5, 0.125, (), jnp.float32),
        "second_bias": centred(splits[13], (C,), 0.3, 1.8, (), jnp.float32),
        "attend_gain": jnp.clip(1.0 + 0.15 * jax.random.normal(splits[14], (C,), jnp.float32), 0.25, 1.75),
        "attend_shift": centred(splits[15], (C,), 0.3, 1.8, (), jnp.float32),
        "triple_weight": centred(splits[16], (C, 3 * C), C ** -0.5, 0.375, (), jnp.float32),
        "query_bias": centred(splits[17], (C,), 0.3, 1.8, (), jnp.float32),
        "value_bias": centred(splits[18], (C,), 0.3, 1.8, (), jnp.float32),
        "output_weight": centred(splits[19], (C, C), (C // 16) ** -0.5, 1.5, (), jnp.float32),
        "output_bias": centred(splits[20], (C,), 0.3, 1.8, (), jnp.float32),
    }


EPSILON = 1e-06
HIGHEST = lax.Precision.HIGHEST

@jax.custom_vjp
def low(v):
    return lax.optimization_barrier(v.astype(jnp.bfloat16)).astype(jnp.float32)

@jax.custom_vjp
def low_back(v):
    return v

def low_keep(v):
    return (low(v), None)

def low_pass(kept, grad):
    return (grad,)

def back_keep(v):
    return (v, None)

def back_low(kept, grad):
    return (low(grad),)
low.defvjp(low_keep, low_pass)
low_back.defvjp(back_keep, back_low)

def swish_value(values):
    return values * jax.nn.sigmoid(values)

def group_norm(values, gain, shift):
    batch_size, positions, width = values.shape
    grouped = values.reshape(batch_size, positions, GROUPS, width // GROUPS)
    center = grouped - lax.optimization_barrier(jnp.mean(grouped, axis=(1, 3), keepdims=True))
    spread = lax.optimization_barrier(jnp.mean(center * center, axis=(1, 3), keepdims=True))
    return (center * lax.rsqrt(spread + EPSILON)).reshape(values.shape) * gain + shift

def convolve(values, kernel):
    batch_size, positions, width = values.shape
    grid = values.reshape(batch_size, SIDE, SIDE, width)
    result = lax.conv_general_dilated(grid, kernel, (1, 1), 'SAME', dimension_numbers=('NHWC', 'HWIO', 'NHWC'), precision=HIGHEST)
    return result.reshape(batch_size, positions, kernel.shape[3])

def embedding(times):
    half_width = TEMB // 2
    frequency = jnp.exp(-math.log(10000.0) * jnp.arange(half_width, dtype=jnp.float32) / (half_width - 1))
    angles = times[:, None] * frequency[None, :]
    return jnp.concatenate([jnp.sin(angles), jnp.cos(angles)], axis=1)

def apply_layer(images, times, params):
    first_gain, first_shift, first_conv, embed_weight, embed_bias, second_gain, second_shift, second_conv, second_bias, attend_gain, attend_shift, triple_weight, query_bias, value_bias, output_weight, output_bias = params
    width = images.shape[2]
    first_act = low(swish_value(group_norm(images, first_gain, first_shift)))
    stepped = jnp.dot(swish_value(embedding(times)), embed_weight, precision=HIGHEST) + embed_bias
    first_out = low_back(convolve(first_act, low(first_conv))) + stepped[:, None, :]
    second_act = low(swish_value(group_norm(first_out, second_gain, second_shift)))
    middle = images + low_back(convolve(second_act, low(second_conv))) + second_bias
    normed = low(group_norm(middle, attend_gain, attend_shift))
    triple = low_back(jnp.einsum('ntc,cd->ntd', normed, low(triple_weight), precision=HIGHEST))
    queries = low(triple[:, :, :width] + query_bias)
    keys_part = low(triple[:, :, width:2 * width])
    values_part = low(triple[:, :, 2 * width:] + value_bias)
    scores = low_back(jnp.einsum('nqc,nkc->nqk', queries, keys_part, precision=HIGHEST) * (1.0 / math.sqrt(width)))
    probs = low(jax.nn.softmax(scores, axis=-1))
    mixed = low(low_back(jnp.einsum('nqk,nkc->nqc', probs, values_part, precision=HIGHEST)))
    projected = low_back(jnp.einsum('ntc,cd->ntd', mixed, low(output_weight), precision=HIGHEST))
    return middle + projected + output_bias

def reference(images, timesteps, counts, source, cotangent, first_gain, first_shift, first_conv, embed_weight, embed_bias, second_gain, second_shift, second_conv, second_bias, attend_gain, attend_shift, triple_weight, query_bias, value_bias, output_weight, output_bias):
    params = (first_gain, first_shift, first_conv, embed_weight, embed_bias, second_gain, second_shift, second_conv, second_bias, attend_gain, attend_shift, triple_weight, query_bias, value_bias, output_weight, output_bias)
    keeps = counts >= WORK
    column_count, bucket_count = counts.shape
    spare_index = jnp.broadcast_to(source[:, :, None, None].astype(jnp.int32), (column_count, bucket_count, TOK, C))
    floats = timesteps.astype(jnp.float32)
    spare_time = jnp.take_along_axis(floats[:, :, WORK], source.astype(jnp.int32), axis=1)
    last_time = jnp.where(keeps, floats[:, :, WORK - 1], spare_time)
    work_times = jnp.concatenate([floats[:, :, :WORK - 1], last_time[:, :, None]], axis=2).reshape(-1)

    def forward(slots, weights):
        spare = jnp.take_along_axis(slots[:, :, WORK], spare_index, axis=1)
        second = jnp.where(keeps[:, :, None, None], slots[:, :, WORK - 1], spare)
        work_images = jnp.concatenate([slots[:, :, :WORK - 1], second[:, :, None]], axis=2)
        flat = work_images.reshape(-1, TOK, C)
        return apply_layer(flat, work_times, weights).reshape(work_images.shape)
    output, pullback = jax.vjp(forward, images, params)
    image_gradient, grads = pullback(cotangent)
    return (output, image_gradient, grads[0], grads[1], grads[2], grads[3], grads[4], grads[5], grads[6], grads[7], grads[8], grads[9], grads[10], grads[11], grads[12], grads[13], grads[14], grads[15])
```

```python
import math

import jax
import jax.numpy as jnp
from jax import lax
from jax.experimental import pallas as pl
from jax.experimental.pallas import tpu as pltpu
from jax.sharding import PartitionSpec as P

TEMB = 512
GROUPS = 32
SIDE = 16
WORK = 4
TOK = SIDE * SIDE
C = 256
PAD = TOK + 2 * SIDE
EPSILON = 1e-06
COUNT = float(TOK * (C // GROUPS))
CHUNK = 64
F32 = jnp.float32
BF16 = jnp.bfloat16
VMEM_LIMIT = 56 * 1024 * 1024
NT = (((1,), (1,)), ((), ()))
TN = (((0,), (0,)), ((), ()))

R_OUT_BIAS, R_QUERY_BIAS, R_VALUE_BIAS, R_ATT_GAIN, R_ATT_SHIFT, R_SEC_BIAS = 0, 1, 2, 3, 4, 5
R_SEC_GAIN, R_SEC_SHIFT, R_EMB_BIAS, R_FIRST_GAIN, R_FIRST_SHIFT = 6, 7, 8, 9, 10
SUMS = 16


def dot(a, b, dims=(((1,), (0,)), ((), ()))):
    return lax.dot_general(a, b, dims, preferred_element_type=F32)


def sigmoid(v):
    return 0.5 * jnp.tanh(0.5 * v) + 0.5


def group_matrix():
    row = lax.broadcasted_iota(jnp.int32, (C, C), 0) // (C // GROUPS)
    col = lax.broadcasted_iota(jnp.int32, (C, C), 1) // (C // GROUPS)
    return (row == col).astype(F32).astype(BF16)


def group_mean(sums, same):
    high = sums.astype(BF16).astype(F32)
    rest = sums - high
    mid = rest.astype(BF16).astype(F32)
    low = rest - mid
    total = dot(jnp.concatenate([high, mid, low], axis=0).astype(BF16), same)
    return (total[0:8] + total[8:16] + total[16:24]) * (1.0 / COUNT)


def over_chunks(count, body):
    steps = TOK // CHUNK

    def step(i, carry):
        body(i // steps, pl.multiple_of((i % steps) * CHUNK, CHUNK))
        return carry

    lax.fori_loop(0, count * steps, step, 0)


def fold(v):
    return jnp.sum(v.reshape(v.shape[0] // 8, 8, v.shape[1]), axis=0)


def column_sums(count, parts, body, hold):
    hold[0 : parts * count] = jnp.zeros((parts * count, 8, C), F32)

    def step(image, row):
        for part, v in enumerate(body(image, row)):
            hold[part * count + image] += fold(v)

    over_chunks(count, step)
    return gather_sums(count, parts, hold)


def gather_sums(count, parts, hold):
    out = []
    for part in range(parts):
        rows = [jnp.sum(hold[part * count + i], axis=0, keepdims=True) for i in range(count)]
        out.append(jnp.concatenate(rows + [jnp.zeros((8 - count, C), F32)], axis=0))
    return out


def edge_masks():
    column = lax.broadcasted_iota(jnp.int32, (CHUNK, C), 0) % SIDE
    return column == 0, column == SIDE - 1


def store_shifted(ref, image, row, v, backward):
    first, last = edge_masks()
    before = jnp.where(first, 0.0, pltpu.roll(v, 1, 0)).astype(BF16)
    after = jnp.where(last, 0.0, pltpu.roll(v, CHUNK - 1, 0)).astype(BF16)
    rows = pl.ds(row + SIDE, CHUNK)
    left, right = (after, before) if backward else (before, after)
    ref[image, rows, 0:C] = left
    ref[image, rows, C : 2 * C] = v.astype(BF16)
    ref[image, rows, 2 * C : 3 * C] = right


def clear_borders(ref, count):
    for i in range(count):
        ref[i, 0:SIDE, :] = jnp.zeros((SIDE, 3 * C), BF16)
        ref[i, PAD - SIDE : PAD, :] = jnp.zeros((SIDE, 3 * C), BF16)


def window(ref, count, di):
    return ref[0:count, SIDE * di : SIDE * di + TOK, :].reshape(count * TOK, 3 * C)


def norm_stats(count, ref, hold, same):
    (sums,) = column_sums(count, 1, lambda i, r: (ref[i, pl.ds(r, CHUNK), :],), hold)
    return sums_to_stats(count, sums, ref, hold, same)


def sums_to_stats(count, sums, ref, hold, same):
    mean = group_mean(sums, same)
    hold_mean = hold.at[hold.shape[0] - 1]
    hold_mean[...] = mean

    def squares(i, r):
        d = ref[i, pl.ds(r, CHUNK), :] - hold_mean[pl.ds(i, 1), :]
        return (d * d,)

    (second,) = column_sums(count, 1, squares, hold)
    return mean, lax.rsqrt(group_mean(second, same) + EPSILON)


def front(
    count, x, cot, times, w, out, dmid, out1, act1, act2, stats, sums, g_triple, g_out,
    shifted, hold, mid, normed, triple, mixed, dmixed, dtriple, dnormed, same_ref, accumulate,
):
    same = same_ref[...]

    def vec(name):
        return w[name][...]

    mean, scale = norm_stats(count, x, hold, same)
    for i in range(count):
        stats[i, 0:1, :] = mean[i : i + 1]
        stats[i, 1:2, :] = scale[i : i + 1]
    clear_borders(shifted, count)
    gain, shift = vec("first_gain"), vec("first_shift")

    def first(i, r):
        rows = pl.ds(r, CHUNK)
        pre = (x[i, rows, :] - stats[i, 0:1, :]) * stats[i, 1:2, :] * gain + shift
        act = pre * sigmoid(pre)
        act1[i, rows, :] = act.astype(BF16)
        store_shifted(shifted, i, r, act, False)

    over_chunks(count, first)

    half = TEMB // 2
    lane = lax.broadcasted_iota(jnp.int32, (8, half), 1).astype(F32)
    row = lax.broadcasted_iota(jnp.int32, (8, half), 0)
    frequency = jnp.exp(lane * (-math.log(10000.0) / (half - 1)))
    clock = jnp.zeros((8, half), F32)
    for i in range(count):
        clock = jnp.where(row == i, times[i], clock)
    angles = clock * frequency
    waves = jnp.concatenate([jnp.sin(angles), jnp.cos(angles)], axis=1)
    waves = waves * sigmoid(waves)
    stepped = lax.dot_general(
        waves, w["embed_weight"][...], (((1,), (0,)), ((), ())),
        precision=lax.Precision.HIGHEST, preferred_element_type=F32,
    ) + vec("embed_bias")

    kernel = w["first_conv"]
    conv = None
    for di in range(3):
        part = dot(window(shifted, count, di), kernel[di].reshape(3 * C, C).astype(BF16))
        conv = part if conv is None else conv + part
    for i in range(count):
        out1[i] = conv[i * TOK : (i + 1) * TOK] + stepped[i : i + 1]

    mean, scale = norm_stats(count, out1, hold, same)
    for i in range(count):
        stats[i, 2:3, :] = mean[i : i + 1]
        stats[i, 3:4, :] = scale[i : i + 1]
    gain2, shift2 = vec("second_gain"), vec("second_shift")

    def second(i, r):
        rows = pl.ds(r, CHUNK)
        pre = (out1[i, rows, :] - stats[i, 2:3, :]) * stats[i, 3:4, :] * gain2 + shift2
        act = pre * sigmoid(pre)
        act2[i, rows, :] = act.astype(BF16)
        store_shifted(shifted, i, r, act, False)

    over_chunks(count, second)
    kernel = w["second_conv"]
    conv = None
    for di in range(3):
        part = dot(window(shifted, count, di), kernel[di].reshape(3 * C, C).astype(BF16))
        conv = part if conv is None else conv + part
    bias = vec("second_bias")
    for i in range(count):
        mid[i] = conv[i * TOK : (i + 1) * TOK] + x[i] + bias

    mean, scale = norm_stats(count, mid, hold, same)
    for i in range(count):
        stats[i, 4:5, :] = mean[i : i + 1]
        stats[i, 5:6, :] = scale[i : i + 1]
    gain3, shift3 = vec("attend_gain"), vec("attend_shift")

    def third(i, r):
        rows = pl.ds(r, CHUNK)
        pre = (mid[i, rows, :] - stats[i, 4:5, :]) * stats[i, 5:6, :] * gain3 + shift3
        normed[i, rows, :] = pre.astype(BF16)

    over_chunks(count, third)
    flat = normed[0:count].reshape(count * TOK, C)
    w_triple = w["triple_weight"][...].astype(BF16)
    w_out = w["output_weight"][...].astype(BF16)
    for part, name in enumerate(("query_bias", None, "value_bias")):
        v = dot(flat, w_triple[:, part * C : (part + 1) * C])
        if name is not None:
            v = v + vec(name)
        triple[0:count, :, part * C : (part + 1) * C] = v.astype(BF16).reshape(count, TOK, C)

    cot_low = cot[0:count].reshape(count * TOK, C).astype(BF16)
    dmixed[0:count] = dot(cot_low, w_out, NT).astype(BF16).reshape(count, TOK, C)

    factor = 1.0 / math.sqrt(C)
    query_sum = jnp.zeros((1, C), F32)
    value_sum = jnp.zeros((1, C), F32)
    for i in range(count):
        q = triple[i, :, 0:C]
        k = triple[i, :, C : 2 * C]
        v = triple[i, :, 2 * C : 3 * C]
        dm = dmixed[i]
        s = dot(q, k, NT) * factor
        e = jnp.exp(s - jnp.max(s, axis=1, keepdims=True))
        p = e * (1.0 / jnp.sum(e, axis=1, keepdims=True))
        p_low = p.astype(BF16)
        mixed[i] = dot(p_low, v).astype(BF16)
        dp = dot(dm, v, NT)
        ds = (p * (dp - jnp.sum(p * dp, axis=1, keepdims=True))).astype(BF16)
        dq = dot(ds, k) * factor
        dk = dot(ds, q, TN) * factor
        dv = dot(p_low, dm, TN)
        query_sum = query_sum + jnp.sum(dq, axis=0, keepdims=True)
        value_sum = value_sum + jnp.sum(dv, axis=0, keepdims=True)
        dtriple[i, :, 0:C] = dq.astype(BF16)
        dtriple[i, :, C : 2 * C] = dk.astype(BF16)
        dtriple[i, :, 2 * C : 3 * C] = dv.astype(BF16)

    flat_mixed = mixed[0:count].reshape(count * TOK, C)
    projected = dot(flat_mixed, w_out)
    bias = vec("output_bias")
    for i in range(count):
        out[i] = mid[i] + projected[i * TOK : (i + 1) * TOK] + bias
    flat_d = dtriple[0:count].reshape(count * TOK, 3 * C)
    gw_out = dot(flat_mixed, cot_low, TN)
    gw_triple = dot(flat, flat_d, TN)
    if accumulate is None:
        g_out[...] = gw_out
        g_triple[...] = gw_triple
    else:
        accumulate(gw_out, gw_triple)
    dn = dot(flat_d, w_triple, NT)
    dnormed[0:count] = dn.reshape(count, TOK, C)

    def sums3(i, r):
        rows = pl.ds(r, CHUNK)
        d = dnormed[i, rows, :]
        unit = (mid[i, rows, :] - stats[i, 4:5, :]) * stats[i, 5:6, :]
        return d, d * unit, cot[i, rows, :]

    sum_d, sum_du, sum_cot = column_sums(count, 3, sums3, hold)
    first_mean = group_mean(sum_d * gain3, same)
    second_mean = group_mean(sum_du * gain3, same)
    hold[hold.shape[0] - 1] = first_mean
    hold[hold.shape[0] - 2] = second_mean

    def inner3(i, r):
        rows = pl.ds(r, CHUNK)
        d = dnormed[i, rows, :] * gain3
        scaled = stats[i, 5:6, :]
        unit = (mid[i, rows, :] - stats[i, 4:5, :]) * scaled
        m1 = hold[hold.shape[0] - 1, pl.ds(i, 1), :]
        m2 = hold[hold.shape[0] - 2, pl.ds(i, 1), :]
        g = (d - m1 - unit * m2) * scaled + cot[i, rows, :]
        dmid[i, rows, :] = g
        return (g,)

    (sum_mid,) = column_sums(count, 1, inner3, hold)
    pieces = [
        jnp.sum(sum_cot, axis=0, keepdims=True), query_sum, value_sum,
        jnp.sum(sum_du, axis=0, keepdims=True), jnp.sum(sum_d, axis=0, keepdims=True),
        jnp.sum(sum_mid, axis=0, keepdims=True),
    ]
    return pieces


WEIGHTS = (
    "first_gain", "first_shift", "first_conv", "embed_weight", "embed_bias", "second_gain", "second_shift",
    "second_conv", "second_bias", "attend_gain", "attend_shift", "triple_weight", "query_bias", "value_bias",
    "output_weight", "output_bias",
)


def front_scratch(count):
    return [
        pltpu.VMEM((count, PAD, 3 * C), BF16),
        pltpu.VMEM((16, 8, C), F32),
        pltpu.VMEM((count, TOK, C), F32),
        pltpu.VMEM((count, TOK, C), BF16),
        pltpu.VMEM((count, TOK, 3 * C), BF16),
        pltpu.VMEM((count, TOK, C), BF16),
        pltpu.VMEM((count, TOK, C), BF16),
        pltpu.VMEM((count, TOK, 3 * C), BF16),
        pltpu.VMEM((count, TOK, C), F32),
        pltpu.VMEM((C, C), BF16),
    ]


def store_sums(sums, pieces, before=None):
    sums[...] = jnp.zeros((SUMS, C), F32) if before is None else before[...]
    for r, piece in enumerate(pieces):
        sums[r : r + 1, :] += piece


def kernel_one(times, x, cot, *rest):
    w = dict(zip(WEIGHTS, rest[:16]))
    out, dmid, out1, act1, act2, stats, sums, g_triple, g_out = rest[16:25]
    scratch = rest[25:]
    scratch[-1][...] = group_matrix()
    moments = [times[0, 0, i].astype(F32) for i in range(WORK - 1)]
    pieces = front(
        WORK - 1, x, cot, moments, w, out, dmid, out1, act1, act2, stats, sums, g_triple, g_out, *scratch, None
    )
    store_sums(sums, pieces)


def owner_codes(mesh_shape):
    b, t = lax.axis_index("bucket"), lax.axis_index("batch")
    x, y = b % 2, (b // 2) % 2
    core, z = t % 2, (t // 2) % 2
    return core, x * 4 + y * 2 + z, z * 4 + x * 2 + y


def scatter_unit(dst, unit, value, codes):
    core, even, odd = codes
    for block in range(16):
        half, low = divmod(block, 8)
        mine = jnp.where(core == half, 0, 1)
        code = even if half == 0 else odd
        dst[mine * 8 + (low ^ code), unit] = value[16 * block : 16 * block + 16]


def kernel_two(times, extra, counts, x, cot, *rest):
    w = dict(zip(WEIGHTS, rest[:16]))
    (mid_in, act2_in, sums_in, gt_in, go_in, _o, _a, _d, _s) = rest[16:25]
    out, dmid, out1, act1, act2, stats, sums, blocks = rest[25:33]
    scratch = rest[33:43]
    full_act, full_shift = rest[43:]
    same = scratch[-1]
    same[...] = group_matrix()
    moment = jnp.where(counts[0, 0] >= WORK, times[0, 0, WORK - 1].astype(F32), extra[0, 0])
    codes = owner_codes(None)

    def accumulate(gw_out, gw_triple):
        scatter_unit(blocks, 12, gw_out + go_in[...], codes)
        total = gw_triple + gt_in[...]
        for part in range(3):
            scatter_unit(blocks, 9 + part, total[:, part * C : (part + 1) * C], codes)

    pieces = front(
        1, x, cot, [moment], w, out, dmid, out1, act1, act2, stats, sums, None, None, *scratch, accumulate
    )
    store_sums(sums, pieces, sums_in)

    clear_borders(full_shift, WORK)

    def early(i, r):
        store_shifted(full_shift, i, r, mid_in[i, pl.ds(r, CHUNK), :], True)

    def late(i, r):
        store_shifted(full_shift, i + WORK - 1, r, dmid[i, pl.ds(r, CHUNK), :], True)

    over_chunks(WORK - 1, early)
    over_chunks(1, late)
    full_act[0 : WORK - 1] = act2_in[...]
    full_act[WORK - 1] = act2[0]
    act = full_act[...].reshape(WORK * TOK, C)
    for di in range(3):
        g = dot(act, window(full_shift, WORK, 2 - di), TN)
        for dj in range(3):
            scatter_unit(blocks, di * 3 + dj, g[:, dj * C : (dj + 1) * C], codes)


def swish_norm_backward(dact, values, base, stats, row, gain, shift, hold, same, dpre, write):
    def sums_of(i, r):
        rows = pl.ds(r, CHUNK)
        unit = (base[i, rows, :] - stats[i, row : row + 1, :]) * stats[i, row + 1 : row + 2, :]
        pre = unit * gain + shift
        s = sigmoid(pre)
        d = dact[i, rows, :] * (s * (1.0 + pre * (1.0 - s)))
        dpre[i, rows, :] = d
        return d, d * unit

    sum_d, sum_du = column_sums(WORK, 2, sums_of, hold)
    first_mean = group_mean(sum_d * gain, same)
    second_mean = group_mean(sum_du * gain, same)
    hold[hold.shape[0] - 1] = first_mean
    hold[hold.shape[0] - 2] = second_mean

    def inner(i, r):
        rows = pl.ds(r, CHUNK)
        scaled = stats[i, row + 1 : row + 2, :]
        unit = (base[i, rows, :] - stats[i, row : row + 1, :]) * scaled
        m1 = hold[hold.shape[0] - 1, pl.ds(i, 1), :]
        m2 = hold[hold.shape[0] - 2, pl.ds(i, 1), :]
        return write(i, r, (dpre[i, rows, :] * gain - m1 - unit * m2) * scaled)

    sums = column_sums(WORK, 1, inner, hold)[0]
    return sum_d, sum_du, sums


def conv_backward(shifted, kernel, dact):
    total = None
    for di in range(3):
        win = window(shifted, WORK, 2 - di)
        for dj in range(3):
            part = dot(win[:, dj * C : (dj + 1) * C], kernel[di, dj].astype(BF16), NT)
            total = part if total is None else total + part
    dact[...] = total.reshape(WORK, TOK, C)


def kernel_three(times, extra, counts, dmid, out1, act1, stats, sums_in, kernel, gain_ref, shift_ref, blocks, low, sums, rows_out,
                 shifted, hold, dact, dpre, same_ref):
    same_ref[...] = group_matrix()
    same = same_ref[...]
    codes = owner_codes(None)
    clear_borders(shifted, WORK)

    def load(i, r):
        store_shifted(shifted, i, r, dmid[i, pl.ds(r, CHUNK), :], True)

    over_chunks(WORK, load)
    conv_backward(shifted, kernel, dact)

    def write(i, r, g):
        low[i, pl.ds(r, CHUNK), :] = g.astype(BF16)
        store_shifted(shifted, i, r, g, True)
        return (g,)

    sum_d, sum_du, sum_first = swish_norm_backward(
        dact, None, out1, stats, 2, gain_ref[...], shift_ref[...], hold, same, dpre, write
    )
    act = act1[...].reshape(WORK * TOK, C)
    for di in range(3):
        g = dot(act, window(shifted, WORK, 2 - di), TN)
        for dj in range(3):
            scatter_unit(blocks, di * 3 + dj, g[:, dj * C : (dj + 1) * C], codes)
    sums[...] = sums_in[...]
    sums[R_SEC_GAIN : R_SEC_GAIN + 1, :] = jnp.sum(sum_du, axis=0, keepdims=True)
    sums[R_SEC_SHIFT : R_SEC_SHIFT + 1, :] = jnp.sum(sum_d, axis=0, keepdims=True)
    sums[R_EMB_BIAS : R_EMB_BIAS + 1, :] = jnp.sum(sum_first, axis=0, keepdims=True)
    lane = lax.broadcasted_iota(jnp.int32, (1, C), 1)
    moment = jnp.where(counts[0, 0] >= WORK, times[0, 0, WORK - 1].astype(F32), extra[0, 0])
    clock = jnp.where(lane == WORK - 1, moment, 0.0)
    for i in range(WORK - 1):
        clock = jnp.where(lane == i, times[0, 0, i].astype(F32), clock)
    rows_out[...] = sum_first
    rows_out[WORK : WORK + 1, :] = clock


def kernel_four(counts, x, spare, dmid, low, stats, sums_in, kernel, gain_ref, shift_ref, grad, back, sums,
                base, shifted, hold, dact, dpre, same_ref):
    same_ref[...] = group_matrix()
    same = same_ref[...]
    clear_borders(shifted, WORK)
    base[0 : WORK - 1] = x[...]
    base[WORK - 1] = spare[...]

    def load(i, r):
        store_shifted(shifted, i, r, low[i, pl.ds(r, CHUNK), :].astype(F32), True)

    over_chunks(WORK, load)
    conv_backward(shifted, kernel, dact)

    def write(i, r, g):
        rows = pl.ds(r, CHUNK)
        dpre[i, rows, :] = g + dmid[i, rows, :]
        return (g,)

    sum_d, sum_du, _ = swish_norm_backward(
        dact, None, base, stats, 0, gain_ref[...], shift_ref[...], hold, same, dpre, write
    )
    grad[0 : WORK - 1] = dpre[0 : WORK - 1]
    keeps = counts[0, 0] >= WORK
    grad[WORK - 1] = jnp.where(keeps, dpre[WORK - 1], 0.0)
    back[...] = jnp.where(keeps, 0.0, dpre[WORK - 1])
    sums[...] = sums_in[...]
    sums[R_FIRST_GAIN : R_FIRST_GAIN + 1, :] = jnp.sum(sum_du, axis=0, keepdims=True)
    sums[R_FIRST_SHIFT : R_FIRST_SHIFT + 1, :] = jnp.sum(sum_d, axis=0, keepdims=True)


def whole(shape):
    return pl.BlockSpec(shape, lambda *_: (0,) * len(shape), memory_space=pltpu.VMEM)


def part(shape, first):
    return pl.BlockSpec(shape, lambda *_: (first,) + (0,) * (len(shape) - 1), memory_space=pltpu.VMEM)


SMEM = pl.BlockSpec(memory_space=pltpu.SMEM)
ANY = pl.BlockSpec(memory_space=pl.ANY)


def params():
    return pltpu.CompilerParams(vmem_limit_bytes=VMEM_LIMIT)


def shape(dims, dtype=F32):
    return jax.ShapeDtypeStruct(dims, dtype)


def weight_specs(w):
    return [whole(w[name].shape) for name in WEIGHTS]


def call_one(timesteps, images, cot, w):
    n = WORK - 1
    return pl.pallas_call(
        kernel_one,
        name="front_of_own_images",
        in_specs=[SMEM, part((n, TOK, C), 0), part((n, TOK, C), 0)] + weight_specs(w),
        out_specs=[part((n, TOK, C), 0)] * 5 + [part((n, 8, C), 0), whole((SUMS, C)), whole((C, 3 * C)), whole((C, C))],
        out_shape=[
            shape((WORK, TOK, C)), shape((WORK, TOK, C)), shape((WORK, TOK, C)),
            shape((WORK, TOK, C), BF16), shape((WORK, TOK, C), BF16),
            shape((WORK, 8, C)), shape((SUMS, C)), shape((C, 3 * C)), shape((C, C)),
        ],
        scratch_shapes=front_scratch(n),
        grid=(1,),
        compiler_params=params(),
    )(timesteps, images, cot, *[w[name] for name in WEIGHTS])


def call_two(timesteps, extra, counts, last, cot, w, early):
    out, dmid, out1, act1, act2, stats, sums, g_triple, g_out = early
    n = WORK - 1
    one = part((1, TOK, C), n)
    first = 5 + 16
    return pl.pallas_call(
        kernel_two,
        name="front_of_last_image",
        in_specs=[SMEM, SMEM, SMEM, whole((1, TOK, C)), one]
        + weight_specs(w)
        + [part((n, TOK, C), 0), part((n, TOK, C), 0), whole((SUMS, C)), whole((C, 3 * C)), whole((C, C)), ANY, ANY, ANY, ANY],
        out_specs=[one] * 5 + [part((1, 8, C), n), whole((SUMS, C)), whole((16, 13, 16, C))],
        out_shape=[
            shape((WORK, TOK, C)), shape((WORK, TOK, C)), shape((WORK, TOK, C)),
            shape((WORK, TOK, C), BF16), shape((WORK, TOK, C), BF16),
            shape((WORK, 8, C)), shape((SUMS, C)), shape((16, 13, 16, C)),
        ],
        scratch_shapes=front_scratch(1) + [pltpu.VMEM((WORK, TOK, C), BF16), pltpu.VMEM((WORK, PAD, 3 * C), BF16)],
        input_output_aliases={first + 5: 0, first: 1, first + 6: 2, first + 7: 3, first + 1: 4, first + 8: 5},
        grid=(1,),
        compiler_params=params(),
    )(timesteps, extra, counts, last, cot, *[w[name] for name in WEIGHTS], dmid, act2, sums, g_triple, g_out, out, out1, act1, stats)


def back_scratch():
    return [
        pltpu.VMEM((WORK, PAD, 3 * C), BF16),
        pltpu.VMEM((16, 8, C), F32),
        pltpu.VMEM((WORK, TOK, C), F32),
        pltpu.VMEM((WORK, TOK, C), F32),
        pltpu.VMEM((C, C), BF16),
    ]


def call_three(timesteps, extra, counts, dmid, out1, act1, stats, sums, w):
    full = (WORK, TOK, C)
    return pl.pallas_call(
        kernel_three,
        name="back_to_first_out",
        in_specs=[SMEM, SMEM, SMEM, whole(full), whole(full), whole(full), whole((WORK, 8, C)), whole((SUMS, C)),
                  whole((3, 3, C, C)), whole((1, C)), whole((1, C))],
        out_specs=[whole((16, 9, 16, C)), whole(full), whole((SUMS, C)), whole((8, C))],
        out_shape=[shape((16, 9, 16, C)), shape(full, BF16), shape((SUMS, C)), shape((8, C))],
        scratch_shapes=back_scratch(),
        grid=(1,),
        compiler_params=params(),
    )(timesteps, extra, counts, dmid, out1, act1, stats, sums, w["second_conv"], w["second_gain"], w["second_shift"])


def call_four(counts, images, last, dmid, low, stats, sums, w):
    full = (WORK, TOK, C)
    return pl.pallas_call(
        kernel_four,
        name="back_to_images",
        in_specs=[SMEM, part((WORK - 1, TOK, C), 0), whole((TOK, C)), whole(full), whole(full), whole((WORK, 8, C)),
                  whole((SUMS, C)), whole((3, 3, C, C)), whole((1, C)), whole((1, C))],
        out_specs=[part(full, 0), whole((TOK, C)), whole((SUMS, C))],
        out_shape=[shape((WORK + 1, TOK, C)), shape((TOK, C)), shape((SUMS, C))],
        scratch_shapes=[pltpu.VMEM(full, F32)] + back_scratch(),
        grid=(1,),
        compiler_params=params(),
    )(counts, images, last, dmid, low, stats, sums, w["first_conv"], w["first_gain"], w["first_shift"])


def assemble_kernel(units, *refs):
    own, other = refs[0], refs[1]
    outs = refs[2:]
    core, even, odd = owner_codes(None)
    for half in range(2):
        src = own if half == 0 else other
        holder = core if half == 0 else 1 - core
        code = jnp.where(holder == 0, even, odd)
        for low in range(8):
            block = holder * 8 + (low ^ code)
            rows = pl.ds(pl.multiple_of(block * 16, 16), 16)
            for unit in range(9):
                outs[0][unit, rows, :] = src[low, unit]
            if units == 13:
                for p in range(3):
                    outs[1][rows, p * C : (p + 1) * C] = src[low, 9 + p]
                outs[2][rows, :] = src[low, 12]


def assemble(units, own, other):
    out_shape = [shape((9, C, C))]
    if units == 13:
        out_shape += [shape((C, 3 * C)), shape((C, C))]
    return pl.pallas_call(
        lambda *refs: assemble_kernel(units, *refs),
        name="assemble",
        in_specs=[whole(own.shape), whole(other.shape)],
        out_specs=[whole(s.shape) for s in out_shape],
        out_shape=out_shape,
        grid=(1,),
        compiler_params=params(),
    )(own, other)


def embed_kernel(devices, own, other, out, rows):
    core, even, odd = owner_codes(None)
    half_count = devices // 2
    for half in range(2):
        src = own if half == 0 else other
        holder = core if half == 0 else 1 - core
        code = jnp.where(holder == 0, even, odd)
        code = code * (half_count // 8) + high_code()
        for rel in range(half_count):
            place = holder * half_count + (rel ^ code)
            rows[pl.ds(pl.multiple_of(place * 8, 8), 8), :] = src[rel]
    everything = rows[...]
    half = TEMB // 2
    index = lax.broadcasted_iota(jnp.int32, (8 * devices, half), 0) % 8
    moments = jnp.zeros((8 * devices, half), F32)
    lane = lax.broadcasted_iota(jnp.int32, (8 * devices, C), 1)
    blocks = everything.reshape(devices, 8, C)
    clock_rows = jnp.broadcast_to(blocks[:, WORK : WORK + 1, :], (devices, 8, C)).reshape(8 * devices, C)
    moments = jnp.sum(jnp.where(lane == index, clock_rows, 0.0), axis=1, keepdims=True)
    frequency = jnp.exp(lax.broadcasted_iota(jnp.int32, (8 * devices, half), 1).astype(F32) * (-math.log(10000.0) / (half - 1)))
    angles = moments * frequency
    waves = jnp.concatenate([jnp.sin(angles), jnp.cos(angles)], axis=1)
    waves = waves * sigmoid(waves)
    keep = lax.broadcasted_iota(jnp.int32, (8 * devices, C), 0) % 8 < WORK
    grads = jnp.where(keep, everything, 0.0)
    out[...] = lax.dot_general(waves, grads, TN, precision=lax.Precision.HIGHEST, preferred_element_type=F32)


def high_code():
    b, t = lax.axis_index("bucket"), lax.axis_index("batch")
    nb = lax.axis_size("bucket")
    return (t // 4) * (nb // 4) + b // 4


def embed_gradient(devices, own, other):
    return pl.pallas_call(
        lambda *refs: embed_kernel(devices, *refs),
        name="embed_gradient",
        in_specs=[whole(own.shape), whole(other.shape)],
        out_specs=whole((TEMB, C)),
        out_shape=shape((TEMB, C)),
        scratch_shapes=[pltpu.VMEM((devices * 8, C), F32)],
        grid=(1,),
        compiler_params=params(),
    )(own, other)


AXES = ("bucket", "batch")


def solution(mesh):
    n_bucket, n_batch = mesh.shape["bucket"], mesh.shape["batch"]
    devices = n_bucket * n_batch

    def flips(fn):
        pairs = []
        for b in range(n_bucket):
            for t in range(n_batch):
                nb, nt = fn(b, t)
                pairs.append((b * n_batch + t, nb * n_batch + nt))
        return pairs

    def by_core(even, odd):
        def fn(b, t):
            kind, bit = even if t % 2 == 0 else odd
            return (b ^ bit, t) if kind == "b" else (b, t ^ bit)

        return flips(fn)

    x, y, z = ("b", 1), ("b", 2), ("t", 2)
    core_perm = flips(lambda b, t: (b, t ^ 1))
    stages = [by_core(x, z), by_core(y, x), by_core(z, y)]
    rest = []
    bit = 4
    while bit < n_bucket:
        rest.append(("b", bit))
        bit *= 2
    bit = 4
    while bit < n_batch:
        rest.append(("t", bit))
        bit *= 2
    rest_perms = [by_core(s, s) for s in rest]
    bucket_perms = [flips(lambda b, t, k=k: (b ^ k, t)) for k in range(1, n_bucket)]

    def send(v, perm):
        return lax.ppermute(v, AXES, perm)

    def reduce_blocks(blocks, units):
        v = blocks.reshape(2, 2, 2, 2, units * 16, C)
        r, k = send(v[1], core_perm), v[0]
        for perm in stages:
            out = k[1] + r[1]
            k = k[0] + r[0]
            r = send(out, perm)
        return k + r

    def shards(images, timesteps, counts, source, cotangent, *weights):
        w = dict(zip(WEIGHTS, weights))
        w = {k: v.reshape(1, C) if v.ndim == 1 else v for k, v in w.items()}
        slots = images[0, 0]
        cot = cotangent[0, 0]
        me = lax.axis_index("bucket")
        keeps = counts[0, 0] >= WORK
        own_offset = jnp.where(keeps, 0, source[0, 0] ^ me)

        spare = slots[WORK]
        note = jnp.concatenate(
            [timesteps[0, 0, WORK][None].astype(F32), own_offset[None].astype(F32), jnp.zeros((126,), F32)]
        ).reshape(1, 128)
        arrived = [send(spare, p) for p in bucket_perms]
        notes = [send(note, p) for p in bucket_perms]

        early = call_one(timesteps, slots, cot, w)

        taken, moment = slots[WORK - 1], note[0, 0]
        for k in range(1, n_bucket):
            taken = jnp.where(own_offset == k, arrived[k - 1], taken)
            moment = jnp.where(own_offset == k, notes[k - 1][0, 0], moment)
        extra = jnp.broadcast_to(moment, (1, 128))

        out, dmid, out1, act1, act2, stats, sums, blocks2 = call_two(timesteps, extra, counts, taken[None], cot, w, early)
        blocks1, low, sums, rows = call_three(timesteps, extra, counts, dmid, out1, act1, stats, sums, w)
        grad, back, sums = call_four(counts, slots, taken, dmid, low, stats, sums, w)

        m2 = reduce_blocks(blocks2, 13)
        for perm in rest_perms:
            m2 = m2 + send(m2, perm)
        for perm in stages[::-1]:
            m2 = jnp.stack([m2, send(m2, perm)])
        other2 = send(m2, core_perm)
        dims = (8, 13, 16, C)
        g_second, g_triple, g_out = assemble(13, m2.reshape(dims), other2.reshape(dims))

        m1 = reduce_blocks(blocks1, 9)
        n1 = 9 * 16
        carry = m1
        rows = rows[None]
        for perm in rest_perms:
            packed = jnp.concatenate([carry, sums, rows.reshape(-1, C)], axis=0)
            got = send(packed, perm)
            carry = carry + got[:n1]
            sums = sums + got[n1 : n1 + SUMS]
            rows = jnp.concatenate([rows, got[n1 + SUMS :].reshape(rows.shape)], axis=0)
        carry = carry[None]
        for perm in stages[::-1]:
            size = carry.shape[0] * n1
            packed = jnp.concatenate([carry.reshape(size, C), sums, rows.reshape(-1, C)], axis=0)
            got = send(packed, perm)
            carry = jnp.concatenate([carry, got[:size].reshape(carry.shape)], axis=0)
            sums = sums + got[size : size + SUMS]
            rows = jnp.concatenate([rows, got[size + SUMS :].reshape(rows.shape)], axis=0)
        other1, other_sums, other_rows = send(carry, core_perm), send(sums, core_perm), send(rows, core_perm)
        dims = (8, 9, 16, C)
        (g_first,) = assemble(9, carry.reshape(dims), other1.reshape(dims))
        sums = sums + other_sums
        g_embed = embed_gradient(devices, rows, other_rows)

        if n_bucket == 4:
            core = lax.axis_index("batch") % 2
            bit_a = jnp.where(core == 0, 1, 2)
            bit_b = 3 - bit_a
            first_hop, second_hop = by_core(x, y), by_core(y, x)
            offset_a = jnp.where(core == 0, notes[0][0, 1], notes[1][0, 1]).astype(jnp.int32)
            hop = send(jnp.where((own_offset & bit_a) != 0, back, 0.0), first_hop)
            onward = (offset_a & bit_a) != 0
            turn = jnp.where(onward & ((offset_a & bit_b) != 0), hop, jnp.where(own_offset == bit_b, back, 0.0))
            got = send(turn, second_hop)
            last = jnp.where(onward & ((offset_a & bit_b) == 0), hop, got)
        else:
            last = jnp.zeros_like(back)
            for k in range(1, n_bucket):
                last = last + send(jnp.where(own_offset == k, back, 0.0), bucket_perms[k - 1])
        grad = lax.dynamic_update_slice(grad, last[None], (WORK, 0, 0))

        def vec(r):
            return sums[r]

        return (
            out[None, None], grad[None, None],
            vec(R_FIRST_GAIN), vec(R_FIRST_SHIFT), g_first.reshape(3, 3, C, C), g_embed, vec(R_EMB_BIAS),
            vec(R_SEC_GAIN), vec(R_SEC_SHIFT), g_second.reshape(3, 3, C, C), vec(R_SEC_BIAS),
            vec(R_ATT_GAIN), vec(R_ATT_SHIFT), g_triple, vec(R_QUERY_BIAS), vec(R_VALUE_BIAS),
            g_out, vec(R_OUT_BIAS),
        )

    placed = (
        P("batch", "bucket", None, None, None), P("batch", "bucket", None), P("batch", "bucket"),
        P("batch", "bucket"), P("batch", "bucket", None, None, None),
    ) + (P(),) * 16
    return jax.shard_map(
        shards,
        mesh=mesh,
        in_specs=placed,
        out_specs=(P("batch", "bucket", None, None, None),) * 2 + (P(),) * 16,
        check_vma=False,
    )
```

```python
import math

import jax
import jax.numpy as jnp
from jax import lax
from jax.experimental import pallas as pl
from jax.experimental.pallas import tpu as pltpu
from jax.sharding import PartitionSpec as P

TEMB = 512
GROUPS = 32
SIDE = 16
WORK = 4
TOK = SIDE * SIDE
C = 256
PAD = TOK + 2 * SIDE
EPSILON = 1e-06
COUNT = float(TOK * (C // GROUPS))
CHUNK = 64
F32 = jnp.float32
BATCH, BUCKET = "batch", "bucket"
BF16 = jnp.bfloat16
NT = (((1,), (1,)), ((), ()))
TN = (((0,), (0,)), ((), ()))

R_OUT_BIAS, R_QUERY_BIAS, R_VALUE_BIAS, R_ATT_GAIN, R_ATT_SHIFT, R_SEC_BIAS = 0, 1, 2, 3, 4, 5
R_SEC_GAIN, R_SEC_SHIFT, R_EMB_BIAS, R_FIRST_GAIN, R_FIRST_SHIFT, R_CLOCKS = 6, 7, 8, 9, 10, 11
SUMS = 16


(W_FIRST_GAIN, W_FIRST_SHIFT, W_FIRST_CONV, W_EMBED_WEIGHT, W_EMBED_BIAS, W_SECOND_GAIN, W_SECOND_SHIFT, W_SECOND_CONV,
    W_SECOND_BIAS, W_ATTEND_GAIN, W_ATTEND_SHIFT, W_TRIPLE_WEIGHT, W_QUERY_BIAS, W_VALUE_BIAS, W_OUTPUT_WEIGHT,
    W_OUTPUT_BIAS) = WEIGHTS = range(16)
(X, COT, OUT, DMID, OUT1, ACT1, ACT2, STATS, G_TRIPLE, G_OUT, GT, GO, FULL_ACT, FULL_MID, KERNEL, GAIN, SHIFT, BASE,
    LAST, LOW, GIVE, KEEP, GIVE_C, KEEP_C, GRAD, BACK, SLOT, TO, NOTE, SMALL_ONE) = range(16, 46)


def dot(a, b, dims=(((1,), (0,)), ((), ()))):
    return lax.dot_general(a, b, dims, preferred_element_type=F32)


def sigmoid(v):
    return 0.5 * jnp.tanh(0.5 * v) + 0.5


def group_matrix():
    row = lax.broadcasted_iota(jnp.int32, (C, C), 0) // (C // GROUPS)
    col = lax.broadcasted_iota(jnp.int32, (C, C), 1) // (C // GROUPS)
    return (row == col).astype(F32).astype(BF16)


def group_mean(sums, same):
    high = sums.astype(BF16).astype(F32)
    rest = sums - high
    mid = rest.astype(BF16).astype(F32)
    low = rest - mid
    total = dot(jnp.concatenate([high, mid, low], axis=0).astype(BF16), same)
    return (total[0:8] + total[8:16] + total[16:24]) * (1.0 / COUNT)


def over_chunks(count, body):
    for image in range(count):
        for row in range(0, TOK, CHUNK):
            body(image, row)


def fold(v):
    return jnp.sum(v.reshape(v.shape[0] // 8, 8, v.shape[1]), axis=0)


def column_sums(count, parts, body, hold):
    out = [[] for _ in range(parts)]
    for image in range(count):
        totals = [None] * parts
        for row in range(0, TOK, CHUNK):
            for part, v in enumerate(body(image, row)):
                f = fold(v)
                totals[part] = f if totals[part] is None else totals[part] + f
        for part in range(parts):
            out[part].append(jnp.sum(totals[part], axis=0, keepdims=True))
    return [jnp.concatenate(rows + [jnp.zeros((8 - count, C), F32)], axis=0) for rows in out]


def edge_masks():
    column = lax.broadcasted_iota(jnp.int32, (CHUNK, C), 0) % SIDE
    return column == 0, column == SIDE - 1


def store_shifted(ref, image, row, v, backward):
    first, last = edge_masks()
    before = jnp.where(first, 0.0, pltpu.roll(v, 1, 0)).astype(BF16)
    after = jnp.where(last, 0.0, pltpu.roll(v, CHUNK - 1, 0)).astype(BF16)
    rows = pl.ds(row + SIDE, CHUNK)
    left, right = (after, before) if backward else (before, after)
    ref[image, rows, 0:C] = left
    ref[image, rows, C : 2 * C] = v.astype(BF16)
    ref[image, rows, 2 * C : 3 * C] = right


def clear_borders(ref, count):
    for i in range(count):
        ref[i, 0:SIDE, :] = jnp.zeros((SIDE, 3 * C), BF16)
        ref[i, PAD - SIDE : PAD, :] = jnp.zeros((SIDE, 3 * C), BF16)


def window(ref, count, di):
    return ref[0:count, SIDE * di : SIDE * di + TOK, :].reshape(count * TOK, 3 * C)


def convolve(shifted, image, kernel):
    total = None
    for di in range(3):
        part = dot(shifted[image, SIDE * di : SIDE * di + TOK, :], kernel[di])
        total = part if total is None else total + part
    return total


def norm_stats(count, ref, hold, same):
    (sums,) = column_sums(count, 1, lambda i, r: (ref[i, pl.ds(r, CHUNK), :],), hold)
    return sums_to_stats(count, sums, ref, hold, same)


def sums_to_stats(count, sums, ref, hold, same):
    mean = group_mean(sums, same)

    def squares(i, r):
        d = ref[i, pl.ds(r, CHUNK), :] - mean[i : i + 1, :]
        return (d * d,)

    (second,) = column_sums(count, 1, squares, hold)
    return mean, lax.rsqrt(group_mean(second, same) + EPSILON)


def front(
    count, x, cot, times, w, out, dmid, out1, act1, act2, stats, sums, g_triple, g_out,
    shifted, hold, mid, normed, triple, mixed, dmixed, dtriple, dnormed, same_ref, accumulate, need, ready,
):
    same = same_ref[...]

    def vec(name):
        return w[name][...]

    need(X)
    mean, scale = norm_stats(count, x, hold, same)
    for i in range(count):
        stats[i, 0:1, :] = mean[i : i + 1]
        stats[i, 1:2, :] = scale[i : i + 1]
    clear_borders(shifted, count)
    gain, shift = vec(W_FIRST_GAIN), vec(W_FIRST_SHIFT)

    def first(i, r):
        rows = pl.ds(r, CHUNK)
        pre = (x[i, rows, :] - stats[i, 0:1, :]) * stats[i, 1:2, :] * gain + shift
        act = pre * sigmoid(pre)
        act1[i, rows, :] = act.astype(BF16)
        store_shifted(shifted, i, r, act, False)

    over_chunks(count, first)
    ready(ACT1)

    half = TEMB // 2
    lane = lax.broadcasted_iota(jnp.int32, (8, half), 1).astype(F32)
    row = lax.broadcasted_iota(jnp.int32, (8, half), 0)
    frequency = jnp.exp(lane * (-math.log(10000.0) / (half - 1)))
    clock = jnp.zeros((8, half), F32)
    for i in range(count):
        clock = jnp.where(row == i, times[i], clock)
    angles = clock * frequency
    waves = jnp.concatenate([jnp.sin(angles), jnp.cos(angles)], axis=1)
    waves = waves * sigmoid(waves)
    need(W_EMBED_WEIGHT)
    stepped = lax.dot_general(
        waves, w[W_EMBED_WEIGHT][...], (((1,), (0,)), ((), ())),
        precision=lax.Precision.HIGHEST, preferred_element_type=F32,
    ) + vec(W_EMBED_BIAS)

    need(W_FIRST_CONV)
    kernel = w[W_FIRST_CONV]
    low = [kernel[di].reshape(3 * C, C).astype(BF16) for di in range(3)]
    for i in range(count):
        out1[i] = convolve(shifted, i, low) + stepped[i : i + 1]
    ready(OUT1)

    mean, scale = norm_stats(count, out1, hold, same)
    for i in range(count):
        stats[i, 2:3, :] = mean[i : i + 1]
        stats[i, 3:4, :] = scale[i : i + 1]
    gain2, shift2 = vec(W_SECOND_GAIN), vec(W_SECOND_SHIFT)

    def second(i, r):
        rows = pl.ds(r, CHUNK)
        pre = (out1[i, rows, :] - stats[i, 2:3, :]) * stats[i, 3:4, :] * gain2 + shift2
        act = pre * sigmoid(pre)
        act2[i, rows, :] = act.astype(BF16)
        store_shifted(shifted, i, r, act, False)

    over_chunks(count, second)
    ready(ACT2)
    need(W_SECOND_CONV)
    kernel = w[W_SECOND_CONV]
    low = [kernel[di].reshape(3 * C, C).astype(BF16) for di in range(3)]
    bias = vec(W_SECOND_BIAS)
    for i in range(count):
        mid[i] = convolve(shifted, i, low) + (x[i] + bias)

    mean, scale = norm_stats(count, mid, hold, same)
    for i in range(count):
        stats[i, 4:5, :] = mean[i : i + 1]
        stats[i, 5:6, :] = scale[i : i + 1]
        stats[i, 6:8, :] = jnp.zeros((2, C), F32)
    ready(STATS)
    gain3, shift3 = vec(W_ATTEND_GAIN), vec(W_ATTEND_SHIFT)

    def third(i, r):
        rows = pl.ds(r, CHUNK)
        pre = (mid[i, rows, :] - stats[i, 4:5, :]) * stats[i, 5:6, :] * gain3 + shift3
        normed[i, rows, :] = pre.astype(BF16)

    over_chunks(count, third)
    flat = normed[0:count].reshape(count * TOK, C)
    need(W_TRIPLE_WEIGHT)
    need(W_OUTPUT_WEIGHT)
    w_triple = w[W_TRIPLE_WEIGHT][...].astype(BF16)
    w_out = w[W_OUTPUT_WEIGHT][...].astype(BF16)
    for i in range(count):
        for part, name in enumerate((W_QUERY_BIAS, None, W_VALUE_BIAS)):
            v = dot(normed[i], w_triple[:, part * C : (part + 1) * C])
            if name is not None:
                v = v + vec(name)
            triple[i, :, part * C : (part + 1) * C] = v.astype(BF16)

    need(COT)
    cot_low = cot[0:count].reshape(count * TOK, C).astype(BF16)
    for i in range(count):
        dmixed[i] = dot(cot[i].astype(BF16), w_out, NT).astype(BF16)

    factor = 1.0 / math.sqrt(C)
    query_sum = jnp.zeros((1, C), F32)
    value_sum = jnp.zeros((1, C), F32)
    for i in range(count):
        q = triple[i, :, 0:C]
        k = triple[i, :, C : 2 * C]
        v = triple[i, :, 2 * C : 3 * C]
        dm = dmixed[i]
        s = dot(q, k, NT) * factor
        e = jnp.exp(s - jnp.max(s, axis=1, keepdims=True))
        p = e * (1.0 / jnp.sum(e, axis=1, keepdims=True))
        p_low = p.astype(BF16)
        mixed[i] = dot(p_low, v).astype(BF16)
        dp = dot(dm, v, NT)
        ds = (p * (dp - jnp.sum(p * dp, axis=1, keepdims=True))).astype(BF16)
        dq = dot(ds, k) * factor
        dk = dot(ds, q, TN) * factor
        dv = dot(p_low, dm, TN)
        query_sum = query_sum + jnp.sum(dq, axis=0, keepdims=True)
        value_sum = value_sum + jnp.sum(dv, axis=0, keepdims=True)
        dtriple[i, :, 0:C] = dq.astype(BF16)
        dtriple[i, :, C : 2 * C] = dk.astype(BF16)
        dtriple[i, :, 2 * C : 3 * C] = dv.astype(BF16)

    flat_mixed = mixed[0:count].reshape(count * TOK, C)
    bias = vec(W_OUTPUT_BIAS)
    for i in range(count):
        out[i] = dot(mixed[i], w_out) + (mid[i] + bias)
    ready(OUT)
    flat_d = dtriple[0:count].reshape(count * TOK, 3 * C)
    gw_out = dot(flat_mixed, cot_low, TN)
    gw_triple = dot(flat, flat_d, TN)
    if accumulate is None:
        g_out[...] = gw_out
        g_triple[...] = gw_triple
        ready(G_OUT)
        ready(G_TRIPLE)
    else:
        accumulate(gw_out, gw_triple)
    for i in range(count):
        dnormed[i] = dot(dtriple[i], w_triple, NT)

    def sums3(i, r):
        rows = pl.ds(r, CHUNK)
        d = dnormed[i, rows, :]
        unit = (mid[i, rows, :] - stats[i, 4:5, :]) * stats[i, 5:6, :]
        return d, d * unit, cot[i, rows, :]

    sum_d, sum_du, sum_cot = column_sums(count, 3, sums3, hold)
    first_mean = group_mean(sum_d * gain3, same)
    second_mean = group_mean(sum_du * gain3, same)

    def inner3(i, r):
        rows = pl.ds(r, CHUNK)
        d = dnormed[i, rows, :] * gain3
        scaled = stats[i, 5:6, :]
        unit = (mid[i, rows, :] - stats[i, 4:5, :]) * scaled
        m1 = first_mean[i : i + 1, :]
        m2 = second_mean[i : i + 1, :]
        g = (d - m1 - unit * m2) * scaled + cot[i, rows, :]
        dmid[i, rows, :] = g
        return (g,)

    (sum_mid,) = column_sums(count, 1, inner3, hold)
    ready(DMID)
    pieces = [
        jnp.sum(sum_cot, axis=0, keepdims=True), query_sum, value_sum,
        jnp.sum(sum_du, axis=0, keepdims=True), jnp.sum(sum_d, axis=0, keepdims=True),
        jnp.sum(sum_mid, axis=0, keepdims=True),
    ]
    return pieces


BIG = {
    W_FIRST_CONV: (3, 3, C, C), W_EMBED_WEIGHT: (TEMB, C), W_SECOND_CONV: (3, 3, C, C),
    W_TRIPLE_WEIGHT: (C, 3 * C), W_OUTPUT_WEIGHT: (C, C),
}
SMALL = tuple(name for name in WEIGHTS if name not in BIG)


def front_scratch(count):
    return [
        pltpu.VMEM((count, PAD, 3 * C), BF16),
        pltpu.VMEM((16, 8, C), F32),
        pltpu.VMEM((count, TOK, C), F32),
        pltpu.VMEM((count, TOK, C), BF16),
        pltpu.VMEM((count, TOK, 3 * C), BF16),
        pltpu.VMEM((count, TOK, C), BF16),
        pltpu.VMEM((count, TOK, C), BF16),
        pltpu.VMEM((count, TOK, 3 * C), BF16),
        pltpu.VMEM((count, TOK, C), F32),
        pltpu.VMEM((C, C), BF16),
    ]


def held(count):
    return [pltpu.VMEM(BIG[name], F32) for name in BIG] + [
        pltpu.VMEM((count, TOK, C), F32),
        pltpu.VMEM((count, TOK, C), F32),
        pltpu.VMEM((count, TOK, C), F32),
        pltpu.VMEM((count, TOK, C), F32),
        pltpu.VMEM((count, TOK, C), F32),
        pltpu.VMEM((count, TOK, C), BF16),
        pltpu.VMEM((count, TOK, C), BF16),
        pltpu.VMEM((count, 8, C), F32),
    ]


def small_copies(copies, small, held_small):
    for r, name in enumerate(SMALL):
        copies.start((SMALL_ONE, name), small[name], held_small.at[r])
    return {name: held_small.at[r] for r, name in enumerate(SMALL)}


HELD = tuple(BIG) + (X, COT, OUT, DMID, OUT1, ACT1, ACT2, STATS)


class Copies:
    def __init__(self, sems):
        self.sems = sems
        self.count = 0
        self.by_name = {}
        self.open = []

    def add(self, name, src, dst):
        copy = pltpu.make_async_copy(src, dst, self.sems.at[self.count])
        self.count += 1
        self.by_name[name] = copy
        return copy

    def start(self, name, src, dst):
        self.add(name, src, dst).start()
        self.open.append(name)

    def need(self, name):
        if name in self.open:
            self.open.remove(name)
            self.by_name[name].wait()

    def finish(self):
        for name in list(self.open):
            self.need(name)


def store_sums(sums, pieces, before=None):
    sums[...] = jnp.zeros((SUMS, C), F32) if before is None else before[...]
    for r, piece in enumerate(pieces):
        sums[r : r + 1, :] += piece


FRONT_SEMS = 48


def kernel_one(times, images, cotangent, *rest):
    small = dict(zip(SMALL, rest[: len(SMALL)]))
    rest = rest[len(SMALL) :]
    big = dict(zip(BIG, rest[: len(BIG)]))
    rest = rest[len(BIG) :]
    out, dmid, out1, act1, act2, stats, g_triple, g_out, sums = rest[:9]
    rest = rest[9:]
    scratch, rest = rest[:10], rest[10:]
    kept = dict(zip(HELD, rest[: len(HELD)]))
    v_triple, v_out, held_small, sems = rest[len(HELD) :]
    n = WORK - 1
    copies = Copies(sems)
    copies.start(X, images.at[0:n], kept[X])
    small = small_copies(copies, small, held_small)
    for name in (W_EMBED_WEIGHT, W_FIRST_CONV):
        copies.start(name, big[name], kept[name])
    scratch[-1][...] = group_matrix()
    moments = [times[0, 0, i].astype(F32) for i in range(n)]
    targets = {
        OUT: out.at[0:n], DMID: dmid.at[0:n], OUT1: out1.at[0:n], ACT1: act1.at[0:n], ACT2: act2.at[0:n],
        STATS: stats.at[0:n], G_TRIPLE: g_triple, G_OUT: g_out,
    }
    sources = {**kept, G_TRIPLE: v_triple, G_OUT: v_out}

    def need(name):
        if name == X:
            for first in [X, W_EMBED_WEIGHT, W_FIRST_CONV] + [(SMALL_ONE, v) for v in SMALL]:
                copies.need(first)
            for later in (W_SECOND_CONV, W_TRIPLE_WEIGHT, W_OUTPUT_WEIGHT):
                copies.start(later, big[later], kept[later])
            copies.start(COT, cotangent.at[0:n], kept[COT])
        if name == W_SECOND_CONV:
            for later in (W_SECOND_CONV, W_TRIPLE_WEIGHT, W_OUTPUT_WEIGHT, COT):
                copies.need(later)

    def ready(name):
        for v in {ACT2: (OUT1, ACT1, ACT2), DMID: (OUT, DMID, STATS, G_TRIPLE, G_OUT)}.get(name, ()):
            copies.start((TO, v), sources[v], targets[v])

    w = {**small, **{name: kept[name] for name in BIG}}
    pieces = front(
        n, kept[X], kept[COT], moments, w, kept[OUT], kept[DMID], kept[OUT1], kept[ACT1], kept[ACT2],
        kept[STATS], None, v_triple, v_out, *scratch, None, need, ready,
    )
    store_sums(sums, pieces)
    copies.finish()


ORDERS = (("xyz", "zxy"), ("yzx", "zxy"), ("yxz", "xyz"))
CHUNK_A, CHUNK_B, CHUNK_C = ORDERS[0], ORDERS[1], ORDERS[2]


def chip_bits():
    b, t = lax.axis_index(BUCKET), lax.axis_index(BATCH)
    return {"x": b % 2, "y": (b // 2) % 2, "z": (t // 2) % 2}


def owner_codes(order):
    bits = chip_bits()
    even, odd = (bits[o[0]] * 4 + bits[o[1]] * 2 + bits[o[2]] for o in order)
    return lax.axis_index(BATCH) % 2, even, odd


def scatter_unit(dst, unit, value, codes):
    core, even, odd = codes
    for block in range(16):
        half, low = divmod(block, 8)
        mine = jnp.where(core == half, 0, 1)
        code = even if half == 0 else odd
        dst[mine * 8 + (low ^ code), unit] = value[16 * block : 16 * block + 16]


def place_offset(counts, source):
    keeps = counts[0, 0] >= WORK
    return keeps, jnp.where(keeps, 0, source[0, 0] ^ lax.axis_index(BUCKET))


def kernel_two(n_bucket, times, counts, source, images, cotangent, *rest):
    arrived, rest = rest[: n_bucket - 1], rest[n_bucket - 1 :]
    small = dict(zip(SMALL, rest[: len(SMALL)]))
    rest = rest[len(SMALL) :]
    big = dict(zip(BIG, rest[: len(BIG)]))
    rest = rest[len(BIG) :]
    sums_in, gt_in, go_in, dmid_in, act2_in = rest[:5]
    rest = rest[9:]
    out, dmid, out1, act1, act2, stats, sums, give, keep, give_c, keep_c, last, notes = rest[:13]
    rest = rest[13:]
    scratch, rest = rest[:10], rest[10:]
    kept = dict(zip(HELD, rest[: len(HELD)]))
    full_act, full_shift, full_mid, blocks, blocks_c, v_triple, v_out, note, held_small, sems = rest[len(HELD) :]
    n = WORK - 1
    copies = Copies(sems)
    keeps, offset = place_offset(counts, source)

    def rows_of(k):
        return arrived[k - 1].at[0:TOK]

    choose = copies.add(X, images.at[n], kept[X].at[0])
    pl.when(keeps)(lambda: choose.start())
    pl.when(jnp.logical_not(keeps) & (offset == 0))(
        lambda: pltpu.make_async_copy(images.at[WORK], kept[X].at[0], sems.at[0]).start()
    )
    for k in range(1, n_bucket):
        pl.when(offset == k)(
            lambda k=k: pltpu.make_async_copy(rows_of(k), kept[X].at[0], sems.at[0]).start()
        )
    copies.open.append(X)
    copies.start(W_FIRST_CONV, big[W_FIRST_CONV], kept[W_FIRST_CONV])
    for k in range(1, n_bucket):
        copies.start((NOTE, k), arrived[k - 1].at[TOK : TOK + 8], note.at[k])
    small = small_copies(copies, small, held_small)
    copies.start(W_EMBED_WEIGHT, big[W_EMBED_WEIGHT], kept[W_EMBED_WEIGHT])
    same = scratch[-1]
    same[...] = group_matrix()
    codes, codes_c = owner_codes(CHUNK_A), owner_codes(CHUNK_C)
    first_wave = [X, W_EMBED_WEIGHT, W_FIRST_CONV] + [(SMALL_ONE, v) for v in SMALL]
    for name in first_wave + [(NOTE, k) for k in range(1, n_bucket)]:
        copies.need(name)
    for name in (W_SECOND_CONV, W_TRIPLE_WEIGHT, W_OUTPUT_WEIGHT):
        copies.start(name, big[name], kept[name])
    copies.start(COT, cotangent.at[n : n + 1], kept[COT])
    copies.start(GT, gt_in, v_triple)
    copies.start(GO, go_in, v_out)
    copies.start(FULL_ACT, act2_in.at[0:n], full_act.at[0:n])
    copies.start(FULL_MID, dmid_in.at[0:n], full_mid)
    moment = jnp.where(keeps, times[0, 0, n], times[0, 0, WORK]).astype(F32)
    moment = jnp.full((1, 1), moment, F32)
    for k in range(1, n_bucket):
        moment = jnp.where(offset == k, note[k, 0:1, 0:1], moment)

    lane = lax.broadcasted_iota(jnp.int32, (1, C), 1)
    clock = jnp.where(lane == n, moment, 0.0)
    for i in range(n):
        clock = jnp.where(lane == i, times[0, 0, i].astype(F32), clock)
    notes[...] = jnp.zeros(notes.shape, F32)
    notes[0:1, :] = clock
    if n_bucket == 4:
        even = codes[0] == 0
        neighbour = jnp.where(even, note[1, 0:1, 1:2], note[2, 0:1, 1:2])
        first = jnp.where(even, 1.0, 2.0)
        notes[1:2, :] = jnp.broadcast_to(jnp.where(neighbour == 3.0, 1.0, 0.0), (1, C))
        notes[2:3, :] = jnp.broadcast_to(jnp.where(neighbour == first, 1.0, 0.0), (1, C))

    def accumulate(gw_out, gw_triple):
        scatter_unit(blocks_c, 3, gw_out + v_out[...], codes_c)
        total = gw_triple + v_triple[...]
        for part in range(3):
            scatter_unit(blocks_c, part, total[:, part * C : (part + 1) * C], codes_c)

    targets = {
        OUT: out.at[n:WORK], DMID: dmid.at[n:WORK], OUT1: out1.at[n:WORK], ACT1: act1.at[n:WORK],
        ACT2: act2.at[n:WORK], STATS: stats.at[n:WORK],
    }
    def need(name):
        if name == W_SECOND_CONV:
            for later in (W_SECOND_CONV, W_TRIPLE_WEIGHT, W_OUTPUT_WEIGHT, COT, GT, GO, FULL_ACT, FULL_MID):
                copies.need(later)

    def ready(name):
        if name == DMID:
            for v in targets:
                copies.start((TO, v), kept[v], targets[v])
            copies.start((TO, LAST), kept[X].at[0], last)
            copies.start((TO, GIVE_C), blocks_c.at[8:16], give_c)
            copies.start((TO, KEEP_C), blocks_c.at[0:8], keep_c)

    w = {**small, **{name: kept[name] for name in BIG}}
    pieces = front(
        1, kept[X], kept[COT], [moment], w, kept[OUT], kept[DMID], kept[OUT1], kept[ACT1], kept[ACT2],
        kept[STATS], None, None, None, *scratch, accumulate, need, ready,
    )
    store_sums(sums, pieces, sums_in)

    clear_borders(full_shift, WORK)

    def early(i, r):
        store_shifted(full_shift, i, r, full_mid[i, pl.ds(r, CHUNK), :], True)

    def late(i, r):
        store_shifted(full_shift, i + n, r, kept[DMID][i, pl.ds(r, CHUNK), :], True)

    over_chunks(n, early)
    over_chunks(1, late)
    full_act[n] = kept[ACT2][0]
    act = full_act[...].reshape(WORK * TOK, C)
    for di in range(3):
        g = dot(act, window(full_shift, WORK, 2 - di), TN)
        for dj in range(3):
            scatter_unit(blocks, di * 3 + dj, g[:, dj * C : (dj + 1) * C], codes)
    copies.start((TO, GIVE), blocks.at[8:16], give)
    copies.start((TO, KEEP), blocks.at[0:8], keep)
    copies.finish()


def swish_norm_backward(dact, values, base, stats, row, gain, shift, hold, same, dpre, write):
    def sums_of(i, r):
        rows = pl.ds(r, CHUNK)
        unit = (base[i, rows, :] - stats[i, row : row + 1, :]) * stats[i, row + 1 : row + 2, :]
        pre = unit * gain + shift
        s = sigmoid(pre)
        d = dact[i, rows, :] * (s * (1.0 + pre * (1.0 - s)))
        dpre[i, rows, :] = d
        return d, d * unit

    sum_d, sum_du = column_sums(WORK, 2, sums_of, hold)
    first_mean = group_mean(sum_d * gain, same)
    second_mean = group_mean(sum_du * gain, same)

    def inner(i, r):
        rows = pl.ds(r, CHUNK)
        scaled = stats[i, row + 1 : row + 2, :]
        unit = (base[i, rows, :] - stats[i, row : row + 1, :]) * scaled
        m1 = first_mean[i : i + 1, :]
        m2 = second_mean[i : i + 1, :]
        return write(i, r, (dpre[i, rows, :] * gain - m1 - unit * m2) * scaled)

    sums = column_sums(WORK, 1, inner, hold)[0]
    return sum_d, sum_du, sums


def conv_backward(shifted, kernel, dact):
    low = [jnp.concatenate([kernel[di, dj].astype(BF16) for dj in range(3)], axis=1) for di in range(3)]
    for i in range(WORK):
        total = None
        for di in range(3):
            part = dot(shifted[i, SIDE * (2 - di) : SIDE * (2 - di) + TOK, :], low[di], NT)
            total = part if total is None else total + part
        dact[i] = total


def kernel_three(notes, dmid_in, out1_in, act1_in, stats, sums_in, kernel_in, gain_ref, shift_ref,
                 give, keep, low, sums, rows_out,
                 shifted, hold, dact, dpre, same_ref, dmid, out1, act1, kernel, blocks, v_low, v_small, sems):
    copies = Copies(sems)
    copies.start(GAIN, gain_ref, v_small.at[0])
    copies.start(SHIFT, shift_ref, v_small.at[1])
    gain_ref, shift_ref = v_small.at[0], v_small.at[1]
    copies.start(DMID, dmid_in, dmid)
    copies.start(KERNEL, kernel_in, kernel)
    copies.start(OUT1, out1_in, out1)
    copies.start(ACT1, act1_in, act1)
    same_ref[...] = group_matrix()
    same = same_ref[...]
    codes = owner_codes(CHUNK_B)
    clear_borders(shifted, WORK)
    copies.need(DMID)

    def load(i, r):
        store_shifted(shifted, i, r, dmid[i, pl.ds(r, CHUNK), :], True)

    over_chunks(WORK, load)
    copies.need(KERNEL)
    conv_backward(shifted, kernel, dact)
    for name in (OUT1, ACT1, GAIN, SHIFT):
        copies.need(name)

    def write(i, r, g):
        v_low[i, pl.ds(r, CHUNK), :] = g.astype(BF16)
        store_shifted(shifted, i, r, g, True)
        return (g,)

    sum_d, sum_du, sum_first = swish_norm_backward(
        dact, None, out1, stats, 2, gain_ref[...], shift_ref[...], hold, same, dpre, write
    )
    copies.start((TO, LOW), v_low, low)

    def tap(di, carry):
        rows = pl.ds(pl.multiple_of(SIDE * (2 - di), SIDE), TOK)
        g = dot(act1[...].reshape(WORK * TOK, C), shifted[:, rows, :].reshape(WORK * TOK, 3 * C), TN)
        for dj in range(3):
            scatter_unit(blocks, di * 3 + dj, g[:, dj * C : (dj + 1) * C], codes)
        return carry

    lax.fori_loop(0, 3, tap, 0)
    copies.start((TO, GIVE), blocks.at[8:16], give)
    copies.start((TO, KEEP), blocks.at[0:8], keep)
    sums[...] = sums_in[...]
    sums[R_SEC_GAIN : R_SEC_GAIN + 1, :] = jnp.sum(sum_du, axis=0, keepdims=True)
    sums[R_SEC_SHIFT : R_SEC_SHIFT + 1, :] = jnp.sum(sum_d, axis=0, keepdims=True)
    sums[R_EMB_BIAS : R_EMB_BIAS + 1, :] = jnp.sum(sum_first, axis=0, keepdims=True)
    core = lax.axis_index(BATCH) % 2
    place = chip_place() * 2 + core
    spots = lax.broadcasted_iota(jnp.int32, (4, C), 0) * C + lax.broadcasted_iota(jnp.int32, (4, C), 1)
    clocks = jnp.zeros((4, C), F32)
    for i in range(WORK):
        clocks = jnp.where(spots == place * WORK + i, notes[0:1, i : i + 1], clocks)
    sums[R_CLOCKS : R_CLOCKS + 4, :] = clocks
    four = sum_first[0:WORK]
    both = jnp.concatenate([four, four], axis=0)
    half = lax.broadcasted_iota(jnp.int32, (8, C), 0) // WORK
    rows_out[...] = jnp.where(half == core, both, 0.0)
    copies.finish()


def kernel_four(n_bucket, counts, source, images, last, dmid_in, low_in, stats, sums_in, rows_in, kernel_in, gain_ref, shift_ref,
                grad, back, sums,
                shifted, hold, dact, dpre, same_ref, dmid, base, low, kernel, v_back, v_small, sems):
    n = WORK - 1
    copies = Copies(sems)
    copies.start(GAIN, gain_ref, v_small.at[0])
    copies.start(SHIFT, shift_ref, v_small.at[1])
    gain_ref, shift_ref = v_small.at[0], v_small.at[1]
    copies.start(LOW, low_in, low)
    copies.start(KERNEL, kernel_in, kernel)
    copies.start(BASE, images.at[0:n], base.at[0:n])
    copies.start(LAST, last, base.at[n])
    copies.start(DMID, dmid_in, dmid)
    same_ref[...] = group_matrix()
    same = same_ref[...]
    clear_borders(shifted, WORK)
    copies.need(LOW)

    def load(i, r):
        store_shifted(shifted, i, r, low[i, pl.ds(r, CHUNK), :].astype(F32), True)

    over_chunks(WORK, load)
    copies.need(KERNEL)
    conv_backward(shifted, kernel, dact)
    for name in (BASE, LAST, DMID, GAIN, SHIFT):
        copies.need(name)

    def write(i, r, g):
        rows = pl.ds(r, CHUNK)
        dpre[i, rows, :] = g + dmid[i, rows, :]
        return (g,)

    sum_d, sum_du, _ = swish_norm_backward(
        dact, None, base, stats, 0, gain_ref[...], shift_ref[...], hold, same, dpre, write
    )
    copies.start((TO, GRAD), dpre.at[0:n], grad.at[0:n])
    keeps, offset = place_offset(counts, source)
    if n_bucket == 4:
        even = lax.axis_index(BATCH) % 2 == 0
        first = jnp.where(even, 1, 2)
        v_back[0] = jnp.where((offset & first) != 0, dpre[n], 0.0)
        v_back[1] = jnp.where(offset == 3 - first, dpre[n], 0.0)
    else:
        for k in range(1, n_bucket):
            v_back[k - 1] = jnp.where(offset == k, dpre[n], 0.0)
    copies.start((TO, BACK), v_back, back)
    dmid[n] = jnp.where(keeps, dpre[n], 0.0)
    copies.start((TO, SLOT), dmid.at[n], grad.at[n])
    sums[0:SUMS] = sums_in[...]
    sums[SUMS : SUMS + 8] = rows_in[...]
    sums[R_FIRST_GAIN : R_FIRST_GAIN + 1, :] = jnp.sum(sum_du, axis=0, keepdims=True)
    sums[R_FIRST_SHIFT : R_FIRST_SHIFT + 1, :] = jnp.sum(sum_d, axis=0, keepdims=True)
    copies.finish()


def kernel_pack(times, counts, source, images, out, sem):
    copy = pltpu.make_async_copy(images.at[WORK], out.at[0:TOK], sem)
    copy.start()
    _, offset = place_offset(counts, source)
    lane = lax.broadcasted_iota(jnp.int32, (8, C), 1)
    moment = times[0, 0, WORK].astype(F32)
    out[TOK : TOK + 8] = jnp.where(lane == 0, moment, jnp.where(lane == 1, offset.astype(F32), 0.0))
    copy.wait()


def whole(shape):
    return pl.BlockSpec(shape, lambda *_: (0,) * len(shape), memory_space=pltpu.VMEM)


def part(shape, first):
    return pl.BlockSpec(shape, lambda *_: (first,) + (0,) * (len(shape) - 1), memory_space=pltpu.VMEM)


SMEM = pl.BlockSpec(memory_space=pltpu.SMEM)
ANY = pl.BlockSpec(memory_space=pl.ANY)
HBM = pl.BlockSpec(memory_space=pltpu.HBM)


def params(mebibytes=26):
    return pltpu.CompilerParams(vmem_limit_bytes=mebibytes * 1024 * 1024)


def shape(dims, dtype=F32):
    return jax.ShapeDtypeStruct(dims, dtype)


def weight_specs(w):
    return [whole(w[name].shape) for name in WEIGHTS]


def call_pack(timesteps, counts, source, images):
    return pl.pallas_call(
        kernel_pack,
        name="pack_spare",
        in_specs=[SMEM, SMEM, SMEM, ANY],
        out_specs=pl.BlockSpec(memory_space=pltpu.VMEM),
        out_shape=shape((TOK + 8, C)),
        scratch_shapes=[pltpu.SemaphoreType.DMA],
        cost_estimate=pl.CostEstimate(flops=20_000_000_000, bytes_accessed=1_000_000, transcendentals=0),
        compiler_params=params(),
    )(timesteps, counts, source, images)


VMEM = pl.BlockSpec(memory_space=pltpu.VMEM)
IMAGE_ARRAYS = (
    ((WORK, TOK, C), F32), ((WORK, TOK, C), F32), ((WORK, TOK, C), F32), ((WORK, TOK, C), BF16), ((WORK, TOK, C), BF16),
    ((WORK, 8, C), F32),
)


def call_one(timesteps, images, cot, w):
    n = WORK - 1
    return pl.pallas_call(
        kernel_one,
        name="front_of_own_images",
        in_specs=[SMEM, HBM, HBM] + [HBM] * (len(SMALL) + len(BIG)),
        out_specs=[ANY] * 8 + [VMEM],
        out_shape=[shape(*s) for s in IMAGE_ARRAYS] + [shape((C, 3 * C)), shape((C, C)), shape((SUMS, C))],
        scratch_shapes=front_scratch(n) + held(n)
        + [pltpu.VMEM((C, 3 * C), F32), pltpu.VMEM((C, C), F32), pltpu.VMEM((len(SMALL), 1, C), F32),
           pltpu.SemaphoreType.DMA((FRONT_SEMS,))],
        cost_estimate=pl.CostEstimate(flops=20_000_000_000, bytes_accessed=1_000_000, transcendentals=0),
        compiler_params=params(),
    )(timesteps, images, cot, *[w[name] for name in SMALL], *[w[name] for name in BIG])


def call_two(timesteps, counts, source, images, cot, arrived, w, early):
    out, dmid, out1, act1, act2, stats, g_triple, g_out, sums = early
    n_bucket = len(arrived) + 1
    first = 5 + len(arrived) + len(SMALL) + len(BIG)
    half, half_c = (8, 9, 16, C), (8, 4, 16, C)
    return pl.pallas_call(
        lambda *refs: kernel_two(n_bucket, *refs),
        name="front_of_last_image",
        in_specs=[SMEM, SMEM, SMEM, HBM, HBM] + [ANY] * len(arrived) + [HBM] * (len(SMALL) + len(BIG))
        + [VMEM] + [ANY] * 8,
        out_specs=[ANY] * 6 + [VMEM] + [ANY] * 5 + [VMEM],
        out_shape=[shape(*s) for s in IMAGE_ARRAYS]
        + [shape((SUMS, C)), shape(half), shape(half), shape(half_c), shape(half_c), shape((TOK, C)), shape((8, C))],
        scratch_shapes=front_scratch(1) + held(1)
        + [
            pltpu.VMEM((WORK, TOK, C), BF16), pltpu.VMEM((WORK, PAD, 3 * C), BF16), pltpu.VMEM((WORK - 1, TOK, C), F32),
            pltpu.VMEM((16, 9, 16, C), F32), pltpu.VMEM((16, 4, 16, C), F32), pltpu.VMEM((C, 3 * C), F32), pltpu.VMEM((C, C), F32),
            pltpu.VMEM((n_bucket, 8, C), F32), pltpu.VMEM((len(SMALL), 1, C), F32),
            pltpu.SemaphoreType.DMA((FRONT_SEMS + n_bucket,)),
        ],
        input_output_aliases={first + 5: 0, first + 3: 1, first + 6: 2, first + 7: 3, first + 4: 4, first + 8: 5},
        cost_estimate=pl.CostEstimate(flops=20_000_000_000, bytes_accessed=1_000_000, transcendentals=0),
        compiler_params=params(),
    )(
        timesteps, counts, source, images, cot, *arrived, *[w[name] for name in SMALL], *[w[name] for name in BIG],
        sums, g_triple, g_out, dmid, act2, out, out1, act1, stats,
    )


def back_scratch():
    return [
        pltpu.VMEM((WORK, PAD, 3 * C), BF16),
        pltpu.VMEM((16, 8, C), F32),
        pltpu.VMEM((WORK, TOK, C), F32),
        pltpu.VMEM((WORK, TOK, C), F32),
        pltpu.VMEM((C, C), BF16),
    ]


def call_three(notes, dmid, out1, act1, stats, sums, w):
    full = (WORK, TOK, C)
    half = (8, 9, 16, C)
    return pl.pallas_call(
        kernel_three,
        name="back_to_first_out",
        in_specs=[VMEM, ANY, ANY, ANY, VMEM, VMEM, HBM, HBM, HBM],
        out_specs=[ANY, ANY, ANY, VMEM, VMEM],
        out_shape=[shape(half), shape(half), shape(full, BF16), shape((SUMS, C)), shape((8, C))],
        scratch_shapes=back_scratch()
        + [
            pltpu.VMEM(full, F32), pltpu.VMEM(full, F32), pltpu.VMEM(full, BF16), pltpu.VMEM((3, 3, C, C), F32),
            pltpu.VMEM((16, 9, 16, C), F32), pltpu.VMEM(full, BF16), pltpu.VMEM((2, 1, C), F32),
            pltpu.SemaphoreType.DMA((12,)),
        ],
        compiler_params=params(),
    )(notes, dmid, out1, act1, stats, sums, w[W_SECOND_CONV], w[W_SECOND_GAIN], w[W_SECOND_SHIFT])


def call_four(n_bucket, counts, source, images, last, dmid, low, stats, sums, rows, w):
    full = (WORK, TOK, C)
    backs = 2 if n_bucket == 4 else n_bucket - 1
    return pl.pallas_call(
        lambda *refs: kernel_four(n_bucket, *refs),
        name="back_to_images",
        in_specs=[SMEM, SMEM, HBM, ANY, ANY, ANY, VMEM, VMEM, VMEM, HBM, HBM, HBM],
        out_specs=[ANY, ANY, VMEM],
        out_shape=[shape((WORK + 1, TOK, C)), shape((backs, TOK, C)), shape((SUMS + 8, C))],
        scratch_shapes=back_scratch()
        + [
            pltpu.VMEM(full, F32), pltpu.VMEM(full, F32), pltpu.VMEM(full, BF16), pltpu.VMEM((3, 3, C, C), F32),
            pltpu.VMEM((backs, TOK, C), F32), pltpu.VMEM((2, 1, C), F32), pltpu.SemaphoreType.DMA((12,)),
        ],
        compiler_params=params(),
    )(counts, source, images, last, dmid, low, stats, sums, rows, w[W_FIRST_CONV], w[W_FIRST_GAIN], w[W_FIRST_SHIFT])


def assemble_kernel(*refs):
    first, second, triple, out = refs[6:10]
    copies = Copies(refs[-1])
    for n, order in enumerate((CHUNK_A, CHUNK_C, CHUNK_B)):
        core, even, odd = owner_codes(order)
        for half in range(2):
            src = refs[2 * n + half]
            holder = core if half == 0 else 1 - core
            code = jnp.where(holder == 0, even, odd)
            for low in range(8):
                block = holder * 8 + (low ^ code)
                rows = pl.ds(pl.multiple_of(block * 16, 16), 16)
                if n != 1:
                    copies.start((n, half, low), src.at[low], (second if n == 0 else first).at[:, rows, :])
                    continue
                for p in range(3):
                    copies.start((n, half, low, p), src.at[low, p], triple.at[rows, p * C : (p + 1) * C])
                copies.start((n, half, low), src.at[low, 3], out.at[rows, :])
    copies.finish()


def assemble(*halves):
    return pl.pallas_call(
        assemble_kernel,
        name="assemble",
        in_specs=[ANY] * 6,
        out_specs=[ANY] * 4,
        out_shape=[shape((9, C, C)), shape((9, C, C)), shape((C, 3 * C)), shape((C, C))],
        scratch_shapes=[pltpu.SemaphoreType.DMA((16 + 16 + 16 * 4,))],
        cost_estimate=pl.CostEstimate(flops=1, bytes_accessed=1, transcendentals=0),
        compiler_params=params(2),
    )(*halves)


def high_code():
    b, t = lax.axis_index(BUCKET), lax.axis_index(BATCH)
    return (t // 4) * (lax.axis_size(BUCKET) // 4) + b // 4


def chip_place():
    bits = chip_bits()
    many = lax.axis_size(BUCKET) * lax.axis_size(BATCH) // 16
    return (bits["x"] * 4 + bits["y"] * 2 + bits["z"]) * many + high_code()


def embed_kernel(devices, order, gathered, sums, out, rows):
    core = lax.axis_index(BATCH) % 2
    bits = chip_bits()
    mine = bits["x"] * 4 + bits["y"] * 2 + bits["z"]
    high = high_code()
    many = devices // 16
    weight = {"x": 4, "y": 2, "z": 1}
    for place in range(devices // 2):
        rest, code = place % many, place // many
        turned = [
            sum(((code >> (2 - n)) & 1) * weight[o[n]] for n in range(3)) for o in order
        ]
        code = jnp.where(core == 0, turned[0], turned[1]) ^ mine
        rows[code * many + (rest ^ high)] = gathered[place]
    count = WORK * devices
    grads = rows[...].reshape(count, C)
    half = TEMB // 2
    moments = []
    for n in range(0, count, C):
        size = min(C, count)
        row = lax.broadcasted_iota(jnp.int32, (size, C), 0)
        lane = lax.broadcasted_iota(jnp.int32, (size, C), 1)
        clocks = sums[R_CLOCKS + n // C : R_CLOCKS + n // C + 1, :]
        moments.append(jnp.sum(jnp.where(row == lane, clocks, 0.0), axis=1, keepdims=True))
    moments = jnp.concatenate(moments, axis=0) if len(moments) > 1 else moments[0]
    frequency = jnp.exp(
        lax.broadcasted_iota(jnp.int32, (count, half), 1).astype(F32) * (-math.log(10000.0) / (half - 1))
    )
    angles = moments * frequency
    waves = jnp.concatenate([jnp.sin(angles), jnp.cos(angles)], axis=1)
    waves = waves * sigmoid(waves)
    out[...] = lax.dot_general(waves, grads, TN, precision=lax.Precision.HIGHEST, preferred_element_type=F32)


def embed_gradient(devices, order, gathered, sums):
    return pl.pallas_call(
        lambda *refs: embed_kernel(devices, order, *refs),
        name="embed_gradient",
        in_specs=[VMEM, VMEM],
        out_specs=VMEM,
        out_shape=shape((TEMB, C)),
        scratch_shapes=[pltpu.VMEM((devices // 2, 8, C), F32)],
        cost_estimate=pl.CostEstimate(flops=1, bytes_accessed=1, transcendentals=0),
        compiler_params=params(),
    )(gathered, sums)


AXES = (BUCKET, BATCH)


def solution(mesh):
    n_bucket, n_batch = mesh.shape[BUCKET], mesh.shape[BATCH]
    devices = n_bucket * n_batch

    def flips(fn):
        pairs = []
        for b in range(n_bucket):
            for t in range(n_batch):
                nb, nt = fn(b, t)
                pairs.append((b * n_batch + t, nb * n_batch + nt))
        return pairs

    def by_core(even, odd):
        def fn(b, t):
            kind, bit = even if t % 2 == 0 else odd
            return (b ^ bit, t) if kind == 0 else (b, t ^ bit)

        return flips(fn)

    x, y, z = (0, 1), (0, 2), (1, 2)
    core_perm = flips(lambda b, t: (b, t ^ 1))
    links = {"x": x, "y": y, "z": z}
    rest = []
    bit = 4
    while bit < n_bucket:
        rest.append((0, bit))
        bit *= 2
    bit = 4
    while bit < n_batch:
        rest.append((1, bit))
        bit *= 2
    rest_perms = [by_core(s, s) for s in rest]
    bucket_perms = [flips(lambda b, t, k=k: (b ^ k, t)) for k in range(1, n_bucket)]

    def send(v, perm):
        return lax.ppermute(v, AXES, perm)

    def after(v, *others):
        return lax.optimization_barrier((v,) + others)[0]

    def held_by(v, other):
        row = other.reshape(-1, C)[0:1]
        return v + 0.0 * row.reshape((1,) * (v.ndim - 1) + (C,))

    class Chunk:
        def __init__(self, order, give, keep, units):
            self.perms = [by_core(links[p], links[q]) for p, q in zip(*order)]
            self.rows = units * 16
            self.stage = 0
            self.size = give.shape
            self.keep = keep.reshape(2, 2, 2, self.rows, C)
            self.got = send(give, core_perm).reshape(2, 2, 2, self.rows, C)
            self.extra = None

        def step(self, *deps, late=None):
            n_rest = len(rest_perms)
            k = self.stage
            self.stage += 1
            if k < 3:
                out, self.keep = self.keep[1] + self.got[1], self.keep[0] + self.got[0]
                perm = self.perms[k]
            else:
                self.take()
                if k < 3 + n_rest:
                    perm = rest_perms[k - 3]
                else:
                    if k == 3 + n_rest:
                        self.keep = self.keep[None]
                    j = k - 3 - n_rest
                    perm = self.perms[2 - j] if j < 3 else core_perm
                out = self.keep
                if self.extra is not None and perm is not core_perm:
                    sums, rows = self.extra
                    out = jnp.concatenate([out.reshape(-1, C), sums, rows.reshape(-1, C)], axis=0)
            if late is not None:
                out = held_by(out, late)
            out = after(out, *deps)
            self.got = send(out, perm)
            return out

        def take(self):
            n_rest = len(rest_perms)
            k = self.stage - 1
            got = self.got
            if k == 3:
                self.keep = self.keep + got
                return
            if self.extra is not None:
                sums, rows = self.extra
                size = self.keep.size // C
                rows = jnp.concatenate([rows, got[size + SUMS :].reshape(rows.shape)], axis=0)
                self.extra = sums + got[size : size + SUMS], rows
                got = got[:size]
            got = got.reshape(self.keep.shape)
            if k <= 3 + n_rest:
                self.keep = self.keep + got
            else:
                self.keep = jnp.concatenate([self.keep, got], axis=0)

        def halves(self):
            dims = (8, self.rows // 16, 16, C)
            return self.keep.reshape(dims), self.got.reshape(dims)

    def shards(images, timesteps, counts, source, cotangent, *weights):
        w = dict(zip(WEIGHTS, weights))
        w = {k: v.reshape(1, C) if v.ndim == 1 else v for k, v in w.items()}
        slots = images[0, 0]
        cot = cotangent[0, 0]

        spare = call_pack(timesteps, counts, source, slots)
        arrived = [send(spare, p) for p in bucket_perms]
        early = call_one(timesteps, slots, cot, w)
        out, dmid, out1, act1, act2, stats, sums, give_a, keep_a, give_c, keep_c, last, notes = call_two(
            timesteps, counts, source, slots, cot, arrived, w, early
        )
        chunk_a = Chunk(CHUNK_A, give_a, keep_a, 9)
        chunk_c = Chunk(CHUNK_C, give_c, keep_c, 4)
        give_b, keep_b, low, sums, rows = call_three(notes, dmid, out1, act1, stats, sums, w)
        chunk_b = Chunk(CHUNK_B, give_b, keep_b, 9)

        tie = chunk_a.step()
        tie = chunk_c.step(tie)
        tie = chunk_b.step(tie)
        grad, back, extra = call_four(n_bucket, counts, source, slots, last, dmid, after(low, tie), stats, sums, rows, w)
        extra = extra + send(extra, core_perm)
        total = 3 + len(rest_perms) + 3
        home = None
        for k in range(1, total):
            if k == 3:
                chunk_c.extra = extra[:SUMS], extra[None, SUMS:]
            tie = chunk_a.step(tie)
            tie = chunk_c.step(tie)
            tie = chunk_b.step(tie, late=home if k == 4 else None)
            if n_bucket == 4:
                if k == 1:
                    hop = send(after(back[0], tie), by_core(x, y))
                if k == 2:
                    turn = after(jnp.where(notes[1:2] != 0.0, hop, back[1]), tie)
                    got = send(turn, by_core(y, x))
                if k == 3:
                    home = jnp.where(notes[2:3] != 0.0, hop, got)
                    grad = lax.dynamic_update_slice(grad, home[None], (WORK, 0, 0))
            elif k == 1:
                home = send(back[0], bucket_perms[0])
                for n in range(2, n_bucket):
                    home = home + send(back[n - 1], bucket_perms[n - 1])
                grad = lax.dynamic_update_slice(grad, home[None], (WORK, 0, 0))
        tie = chunk_a.step(tie)
        tie = chunk_c.step(tie)
        tie = chunk_b.step(tie)
        sums, rows = chunk_c.extra
        g_embed = embed_gradient(devices, CHUNK_C, rows, sums)
        g_first, g_second, g_triple, g_out = assemble(*chunk_a.halves(), *chunk_c.halves(), *chunk_b.halves())

        def vec(r):
            return sums[r]

        return (
            out[None, None], grad[None, None],
            vec(R_FIRST_GAIN), vec(R_FIRST_SHIFT), g_first.reshape(3, 3, C, C), g_embed, vec(R_EMB_BIAS),
            vec(R_SEC_GAIN), vec(R_SEC_SHIFT), g_second.reshape(3, 3, C, C), vec(R_SEC_BIAS),
            vec(R_ATT_GAIN), vec(R_ATT_SHIFT), g_triple, vec(R_QUERY_BIAS), vec(R_VALUE_BIAS),
            g_out, vec(R_OUT_BIAS),
        )

    placed = (
        P(BATCH, BUCKET, None, None, None), P(BATCH, BUCKET, None), P(BATCH, BUCKET),
        P(BATCH, BUCKET), P(BATCH, BUCKET, None, None, None),
    ) + (P(),) * 16
    return jax.shard_map(
        shards,
        mesh=mesh,
        in_specs=placed,
        out_specs=(P(BATCH, BUCKET, None, None, None),) * 2 + (P(),) * 16,
        check_vma=False,
    )
```

```python
import math

import jax
import jax.numpy as jnp
from jax import lax
from jax.experimental import pallas as pl
from jax.experimental.pallas import tpu as pltpu
from jax.sharding import PartitionSpec as P

TEMB = 512
GROUPS = 32
SIDE = 16
WORK = 4
TOK = SIDE * SIDE
C = 256
PAD = TOK + 2 * SIDE
EPSILON = 1e-06
COUNT = float(TOK * (C // GROUPS))
CHUNK = 64
F32 = jnp.float32
BATCH, BUCKET = "batch", "bucket"
BF16 = jnp.bfloat16
NT = (((1,), (1,)), ((), ()))
TN = (((0,), (0,)), ((), ()))

R_OUT_BIAS, R_QUERY_BIAS, R_VALUE_BIAS, R_ATT_GAIN, R_ATT_SHIFT, R_SEC_BIAS = 0, 1, 2, 3, 4, 5
R_SEC_GAIN, R_SEC_SHIFT, R_EMB_BIAS, R_FIRST_GAIN, R_FIRST_SHIFT, R_CLOCKS = 6, 7, 8, 9, 10, 11
SUMS = 16


(W_FIRST_GAIN, W_FIRST_SHIFT, W_FIRST_CONV, W_EMBED_WEIGHT, W_EMBED_BIAS, W_SECOND_GAIN, W_SECOND_SHIFT, W_SECOND_CONV,
    W_SECOND_BIAS, W_ATTEND_GAIN, W_ATTEND_SHIFT, W_TRIPLE_WEIGHT, W_QUERY_BIAS, W_VALUE_BIAS, W_OUTPUT_WEIGHT,
    W_OUTPUT_BIAS) = WEIGHTS = range(16)
(X, COT, OUT, DMID, OUT1, ACT1, ACT2, STATS, G_TRIPLE, G_OUT, GT, GO, FULL_ACT, FULL_MID, KERNEL, GAIN, SHIFT, BASE,
    LAST, LOW, GIVE, KEEP, GIVE_C, KEEP_C, GRAD, BACK, SLOT, TO, NOTE, SMALL_ONE) = range(16, 46)


def dot(a, b, dims=(((1,), (0,)), ((), ()))):
    return lax.dot_general(a, b, dims, preferred_element_type=F32)


def sigmoid(v):
    return 0.5 * jnp.tanh(0.5 * v) + 0.5


def group_matrix():
    row = lax.broadcasted_iota(jnp.int32, (C, C), 0) // (C // GROUPS)
    col = lax.broadcasted_iota(jnp.int32, (C, C), 1) // (C // GROUPS)
    return (row == col).astype(F32).astype(BF16)


def group_mean(sums, same):
    high = sums.astype(BF16).astype(F32)
    rest = sums - high
    mid = rest.astype(BF16).astype(F32)
    low = rest - mid
    total = dot(jnp.concatenate([high, mid, low], axis=0).astype(BF16), same)
    return (total[0:8] + total[8:16] + total[16:24]) * (1.0 / COUNT)


def over_chunks(count, body):
    for image in range(count):
        for row in range(0, TOK, CHUNK):
            body(image, row)


def fold(v):
    return jnp.sum(v.reshape(v.shape[0] // 8, 8, v.shape[1]), axis=0)


def column_sums(count, parts, body, hold):
    out = [[] for _ in range(parts)]
    for image in range(count):
        totals = [None] * parts
        for row in range(0, TOK, CHUNK):
            for part, v in enumerate(body(image, row)):
                f = fold(v)
                totals[part] = f if totals[part] is None else totals[part] + f
        for part in range(parts):
            out[part].append(jnp.sum(totals[part], axis=0, keepdims=True))
    return [jnp.concatenate(rows + [jnp.zeros((8 - count, C), F32)], axis=0) for rows in out]


def edge_masks():
    column = lax.broadcasted_iota(jnp.int32, (CHUNK, C), 0) % SIDE
    return column == 0, column == SIDE - 1


def store_shifted(ref, image, row, v, backward):
    first, last = edge_masks()
    before = jnp.where(first, 0.0, pltpu.roll(v, 1, 0)).astype(BF16)
    after = jnp.where(last, 0.0, pltpu.roll(v, CHUNK - 1, 0)).astype(BF16)
    rows = pl.ds(row + SIDE, CHUNK)
    left, right = (after, before) if backward else (before, after)
    ref[image, rows, 0:C] = left
    ref[image, rows, C : 2 * C] = v.astype(BF16)
    ref[image, rows, 2 * C : 3 * C] = right


def clear_borders(ref, count):
    for i in range(count):
        ref[i, 0:SIDE, :] = jnp.zeros((SIDE, 3 * C), BF16)
        ref[i, PAD - SIDE : PAD, :] = jnp.zeros((SIDE, 3 * C), BF16)


def window(ref, count, di):
    return ref[0:count, SIDE * di : SIDE * di + TOK, :].reshape(count * TOK, 3 * C)


def convolve(shifted, image, kernel):
    total = None
    for di in range(3):
        part = dot(shifted[image, SIDE * di : SIDE * di + TOK, :], kernel[di])
        total = part if total is None else total + part
    return total


def norm_stats(count, ref, hold, same):
    (sums,) = column_sums(count, 1, lambda i, r: (ref[i, pl.ds(r, CHUNK), :],), hold)
    return sums_to_stats(count, sums, ref, hold, same)


def sums_to_stats(count, sums, ref, hold, same):
    mean = group_mean(sums, same)

    def squares(i, r):
        d = ref[i, pl.ds(r, CHUNK), :] - mean[i : i + 1, :]
        return (d * d,)

    (second,) = column_sums(count, 1, squares, hold)
    return mean, lax.rsqrt(group_mean(second, same) + EPSILON)


def front(
    count, x, cot, times, w, out, dmid, out1, act1, act2, stats, sums, g_triple, g_out,
    shifted, hold, mid, normed, triple, mixed, dmixed, dtriple, dnormed, same_ref, accumulate, need, ready,
):
    same = same_ref[...]

    def vec(name):
        return w[name][...]

    need(X)
    mean, scale = norm_stats(count, x, hold, same)
    for i in range(count):
        stats[i, 0:1, :] = mean[i : i + 1]
        stats[i, 1:2, :] = scale[i : i + 1]
    clear_borders(shifted, count)
    gain, shift = vec(W_FIRST_GAIN), vec(W_FIRST_SHIFT)

    def first(i, r):
        rows = pl.ds(r, CHUNK)
        pre = (x[i, rows, :] - stats[i, 0:1, :]) * stats[i, 1:2, :] * gain + shift
        act = pre * sigmoid(pre)
        act1[i, rows, :] = act.astype(BF16)
        store_shifted(shifted, i, r, act, False)

    over_chunks(count, first)
    ready(ACT1)

    half = TEMB // 2
    lane = lax.broadcasted_iota(jnp.int32, (8, half), 1).astype(F32)
    row = lax.broadcasted_iota(jnp.int32, (8, half), 0)
    frequency = jnp.exp(lane * (-math.log(10000.0) / (half - 1)))
    clock = jnp.zeros((8, half), F32)
    for i in range(count):
        clock = jnp.where(row == i, times[i], clock)
    angles = clock * frequency
    waves = jnp.concatenate([jnp.sin(angles), jnp.cos(angles)], axis=1)
    waves = waves * sigmoid(waves)
    need(W_EMBED_WEIGHT)
    stepped = lax.dot_general(
        waves, w[W_EMBED_WEIGHT][...], (((1,), (0,)), ((), ())),
        precision=lax.Precision.HIGHEST, preferred_element_type=F32,
    ) + vec(W_EMBED_BIAS)

    need(W_FIRST_CONV)
    kernel = w[W_FIRST_CONV]
    low = [kernel[di].reshape(3 * C, C).astype(BF16) for di in range(3)]
    for i in range(count):
        out1[i] = convolve(shifted, i, low) + stepped[i : i + 1]
    ready(OUT1)

    mean, scale = norm_stats(count, out1, hold, same)
    for i in range(count):
        stats[i, 2:3, :] = mean[i : i + 1]
        stats[i, 3:4, :] = scale[i : i + 1]
    gain2, shift2 = vec(W_SECOND_GAIN), vec(W_SECOND_SHIFT)

    def second(i, r):
        rows = pl.ds(r, CHUNK)
        pre = (out1[i, rows, :] - stats[i, 2:3, :]) * stats[i, 3:4, :] * gain2 + shift2
        act = pre * sigmoid(pre)
        act2[i, rows, :] = act.astype(BF16)
        store_shifted(shifted, i, r, act, False)

    over_chunks(count, second)
    ready(ACT2)
    need(W_SECOND_CONV)
    kernel = w[W_SECOND_CONV]
    low = [kernel[di].reshape(3 * C, C).astype(BF16) for di in range(3)]
    bias = vec(W_SECOND_BIAS)
    for i in range(count):
        mid[i] = convolve(shifted, i, low) + (x[i] + bias)

    mean, scale = norm_stats(count, mid, hold, same)
    for i in range(count):
        stats[i, 4:5, :] = mean[i : i + 1]
        stats[i, 5:6, :] = scale[i : i + 1]
        stats[i, 6:8, :] = jnp.zeros((2, C), F32)
    ready(STATS)
    gain3, shift3 = vec(W_ATTEND_GAIN), vec(W_ATTEND_SHIFT)

    def third(i, r):
        rows = pl.ds(r, CHUNK)
        pre = (mid[i, rows, :] - stats[i, 4:5, :]) * stats[i, 5:6, :] * gain3 + shift3
        normed[i, rows, :] = pre.astype(BF16)

    over_chunks(count, third)
    flat = normed[0:count].reshape(count * TOK, C)
    need(W_TRIPLE_WEIGHT)
    need(W_OUTPUT_WEIGHT)
    w_triple = w[W_TRIPLE_WEIGHT][...].astype(BF16)
    w_out = w[W_OUTPUT_WEIGHT][...].astype(BF16)
    for i in range(count):
        for part, name in enumerate((W_QUERY_BIAS, None, W_VALUE_BIAS)):
            v = dot(normed[i], w_triple[:, part * C : (part + 1) * C])
            if name is not None:
                v = v + vec(name)
            triple[i, :, part * C : (part + 1) * C] = v.astype(BF16)

    need(COT)
    cot_low = cot[0:count].reshape(count * TOK, C).astype(BF16)
    for i in range(count):
        dmixed[i] = dot(cot[i].astype(BF16), w_out, NT).astype(BF16)

    factor = 1.0 / math.sqrt(C)
    query_sum = jnp.zeros((1, C), F32)
    value_sum = jnp.zeros((1, C), F32)
    for i in range(count):
        q = triple[i, :, 0:C]
        k = triple[i, :, C : 2 * C]
        v = triple[i, :, 2 * C : 3 * C]
        dm = dmixed[i]
        s = dot(q, k, NT) * factor
        e = jnp.exp(s - jnp.max(s, axis=1, keepdims=True))
        p = e * (1.0 / jnp.sum(e, axis=1, keepdims=True))
        p_low = p.astype(BF16)
        mixed[i] = dot(p_low, v).astype(BF16)
        dp = dot(dm, v, NT)
        ds = (p * (dp - jnp.sum(p * dp, axis=1, keepdims=True))).astype(BF16)
        dq = dot(ds, k) * factor
        dk = dot(ds, q, TN) * factor
        dv = dot(p_low, dm, TN)
        query_sum = query_sum + jnp.sum(dq, axis=0, keepdims=True)
        value_sum = value_sum + jnp.sum(dv, axis=0, keepdims=True)
        dtriple[i, :, 0:C] = dq.astype(BF16)
        dtriple[i, :, C : 2 * C] = dk.astype(BF16)
        dtriple[i, :, 2 * C : 3 * C] = dv.astype(BF16)

    flat_mixed = mixed[0:count].reshape(count * TOK, C)
    bias = vec(W_OUTPUT_BIAS)
    for i in range(count):
        out[i] = dot(mixed[i], w_out) + (mid[i] + bias)
    ready(OUT)
    flat_d = dtriple[0:count].reshape(count * TOK, 3 * C)
    gw_out = dot(flat_mixed, cot_low, TN)
    gw_triple = dot(flat, flat_d, TN)
    if accumulate is None:
        g_out[...] = gw_out
        g_triple[...] = gw_triple
        ready(G_OUT)
        ready(G_TRIPLE)
    else:
        accumulate(gw_out, gw_triple)
    for i in range(count):
        dnormed[i] = dot(dtriple[i], w_triple, NT)

    def sums3(i, r):
        rows = pl.ds(r, CHUNK)
        d = dnormed[i, rows, :]
        unit = (mid[i, rows, :] - stats[i, 4:5, :]) * stats[i, 5:6, :]
        return d, d * unit, cot[i, rows, :]

    sum_d, sum_du, sum_cot = column_sums(count, 3, sums3, hold)
    first_mean = group_mean(sum_d * gain3, same)
    second_mean = group_mean(sum_du * gain3, same)

    def inner3(i, r):
        rows = pl.ds(r, CHUNK)
        d = dnormed[i, rows, :] * gain3
        scaled = stats[i, 5:6, :]
        unit = (mid[i, rows, :] - stats[i, 4:5, :]) * scaled
        m1 = first_mean[i : i + 1, :]
        m2 = second_mean[i : i + 1, :]
        g = (d - m1 - unit * m2) * scaled + cot[i, rows, :]
        dmid[i, rows, :] = g
        return (g,)

    (sum_mid,) = column_sums(count, 1, inner3, hold)
    ready(DMID)
    pieces = [
        jnp.sum(sum_cot, axis=0, keepdims=True), query_sum, value_sum,
        jnp.sum(sum_du, axis=0, keepdims=True), jnp.sum(sum_d, axis=0, keepdims=True),
        jnp.sum(sum_mid, axis=0, keepdims=True),
    ]
    return pieces


BIG = {
    W_FIRST_CONV: (3, 3, C, C), W_EMBED_WEIGHT: (TEMB, C), W_SECOND_CONV: (3, 3, C, C),
    W_TRIPLE_WEIGHT: (C, 3 * C), W_OUTPUT_WEIGHT: (C, C),
}
SMALL = tuple(name for name in WEIGHTS if name not in BIG)


def front_scratch(count):
    return [
        pltpu.VMEM((count, PAD, 3 * C), BF16),
        pltpu.VMEM((16, 8, C), F32),
        pltpu.VMEM((count, TOK, C), F32),
        pltpu.VMEM((count, TOK, C), BF16),
        pltpu.VMEM((count, TOK, 3 * C), BF16),
        pltpu.VMEM((count, TOK, C), BF16),
        pltpu.VMEM((count, TOK, C), BF16),
        pltpu.VMEM((count, TOK, 3 * C), BF16),
        pltpu.VMEM((count, TOK, C), F32),
        pltpu.VMEM((C, C), BF16),
    ]


def held(count):
    return [pltpu.VMEM(BIG[name], F32) for name in BIG] + [
        pltpu.VMEM((count, TOK, C), F32),
        pltpu.VMEM((count, TOK, C), F32),
        pltpu.VMEM((count, TOK, C), F32),
        pltpu.VMEM((count, TOK, C), F32),
        pltpu.VMEM((count, TOK, C), F32),
        pltpu.VMEM((count, TOK, C), BF16),
        pltpu.VMEM((count, TOK, C), BF16),
        pltpu.VMEM((count, 8, C), F32),
    ]


def small_copies(copies, small, held_small):
    for r, name in enumerate(SMALL):
        copies.start((SMALL_ONE, name), small[name], held_small.at[r])
    return {name: held_small.at[r] for r, name in enumerate(SMALL)}


HELD = tuple(BIG) + (X, COT, OUT, DMID, OUT1, ACT1, ACT2, STATS)


class Copies:
    def __init__(self, sems):
        self.sems = sems
        self.count = 0
        self.by_name = {}
        self.open = []

    def add(self, name, src, dst):
        copy = pltpu.make_async_copy(src, dst, self.sems.at[self.count])
        self.count += 1
        self.by_name[name] = copy
        return copy

    def start(self, name, src, dst):
        self.add(name, src, dst).start()
        self.open.append(name)

    def need(self, name):
        if name in self.open:
            self.open.remove(name)
            self.by_name[name].wait()

    def finish(self):
        for name in list(self.open):
            self.need(name)


def store_sums(sums, pieces, before=None):
    sums[...] = jnp.zeros((SUMS, C), F32) if before is None else before[...]
    for r, piece in enumerate(pieces):
        sums[r : r + 1, :] += piece


FRONT_SEMS = 48


def kernel_one(times, images, cotangent, *rest):
    small = dict(zip(SMALL, rest[: len(SMALL)]))
    rest = rest[len(SMALL) :]
    big = dict(zip(BIG, rest[: len(BIG)]))
    rest = rest[len(BIG) :]
    out, dmid, out1, act1, act2, stats, g_triple, g_out, sums = rest[:9]
    rest = rest[9:]
    scratch, rest = rest[:10], rest[10:]
    kept = dict(zip(HELD, rest[: len(HELD)]))
    v_triple, v_out, held_small, sems = rest[len(HELD) :]
    n = WORK - 1
    copies = Copies(sems)
    copies.start(X, images.at[0:n], kept[X])
    small = small_copies(copies, small, held_small)
    for name in (W_EMBED_WEIGHT, W_FIRST_CONV):
        copies.start(name, big[name], kept[name])
    scratch[-1][...] = group_matrix()
    moments = [times[0, 0, i].astype(F32) for i in range(n)]
    targets = {
        OUT: out.at[0:n], DMID: dmid.at[0:n], OUT1: out1.at[0:n], ACT1: act1.at[0:n], ACT2: act2.at[0:n],
        STATS: stats.at[0:n], G_TRIPLE: g_triple, G_OUT: g_out,
    }
    sources = {**kept, G_TRIPLE: v_triple, G_OUT: v_out}

    def need(name):
        if name == X:
            for first in [X, W_EMBED_WEIGHT, W_FIRST_CONV] + [(SMALL_ONE, v) for v in SMALL]:
                copies.need(first)
            for later in (W_SECOND_CONV, W_TRIPLE_WEIGHT, W_OUTPUT_WEIGHT):
                copies.start(later, big[later], kept[later])
            copies.start(COT, cotangent.at[0:n], kept[COT])
        if name == W_SECOND_CONV:
            for later in (W_SECOND_CONV, W_TRIPLE_WEIGHT, W_OUTPUT_WEIGHT, COT):
                copies.need(later)

    def ready(name):
        for v in {ACT2: (OUT1, ACT1, ACT2), DMID: (OUT, DMID, STATS, G_TRIPLE, G_OUT)}.get(name, ()):
            copies.start((TO, v), sources[v], targets[v])

    w = {**small, **{name: kept[name] for name in BIG}}
    pieces = front(
        n, kept[X], kept[COT], moments, w, kept[OUT], kept[DMID], kept[OUT1], kept[ACT1], kept[ACT2],
        kept[STATS], None, v_triple, v_out, *scratch, None, need, ready,
    )
    store_sums(sums, pieces)
    copies.finish()


ORDERS = (("xyz", "zxy"), ("yzx", "zxy"), ("yxz", "xyz"))
CHUNK_A, CHUNK_B, CHUNK_C = ORDERS[0], ORDERS[1], ORDERS[2]


def chip_bits():
    b, t = lax.axis_index(BUCKET), lax.axis_index(BATCH)
    return {"x": b % 2, "y": (b // 2) % 2, "z": (t // 2) % 2}


def owner_codes(order):
    bits = chip_bits()
    even, odd = (bits[o[0]] * 4 + bits[o[1]] * 2 + bits[o[2]] for o in order)
    return lax.axis_index(BATCH) % 2, even, odd


def scatter_unit(dst, unit, value, codes):
    core, even, odd = codes
    for block in range(16):
        half, low = divmod(block, 8)
        mine = jnp.where(core == half, 0, 1)
        code = even if half == 0 else odd
        dst[mine * 8 + (low ^ code), unit] = value[16 * block : 16 * block + 16]


def place_offset(counts, source):
    keeps = counts[0, 0] >= WORK
    return keeps, jnp.where(keeps, 0, source[0, 0] ^ lax.axis_index(BUCKET))


def kernel_two(n_bucket, times, counts, source, images, cotangent, *rest):
    arrived, rest = rest[: n_bucket - 1], rest[n_bucket - 1 :]
    small = dict(zip(SMALL, rest[: len(SMALL)]))
    rest = rest[len(SMALL) :]
    big = dict(zip(BIG, rest[: len(BIG)]))
    rest = rest[len(BIG) :]
    sums_in, gt_in, go_in, dmid_in, act2_in = rest[:5]
    rest = rest[9:]
    out, dmid, out1, act1, act2, stats, sums, give, keep, give_c, keep_c, last, notes = rest[:13]
    rest = rest[13:]
    scratch, rest = rest[:10], rest[10:]
    kept = dict(zip(HELD, rest[: len(HELD)]))
    full_act, full_shift, full_mid, blocks, blocks_c, v_triple, v_out, note, held_small, sems = rest[len(HELD) :]
    n = WORK - 1
    copies = Copies(sems)
    keeps, offset = place_offset(counts, source)

    def rows_of(k):
        return arrived[k - 1].at[0:TOK]

    choose = copies.add(X, images.at[n], kept[X].at[0])
    pl.when(keeps)(lambda: choose.start())
    pl.when(jnp.logical_not(keeps) & (offset == 0))(
        lambda: pltpu.make_async_copy(images.at[WORK], kept[X].at[0], sems.at[0]).start()
    )
    for k in range(1, n_bucket):
        pl.when(offset == k)(
            lambda k=k: pltpu.make_async_copy(rows_of(k), kept[X].at[0], sems.at[0]).start()
        )
    copies.open.append(X)
    copies.start(W_FIRST_CONV, big[W_FIRST_CONV], kept[W_FIRST_CONV])
    for k in range(1, n_bucket):
        copies.start((NOTE, k), arrived[k - 1].at[TOK : TOK + 8], note.at[k])
    small = small_copies(copies, small, held_small)
    copies.start(W_EMBED_WEIGHT, big[W_EMBED_WEIGHT], kept[W_EMBED_WEIGHT])
    same = scratch[-1]
    same[...] = group_matrix()
    codes, codes_c = owner_codes(CHUNK_A), owner_codes(CHUNK_C)
    first_wave = [X, W_EMBED_WEIGHT, W_FIRST_CONV] + [(SMALL_ONE, v) for v in SMALL]
    for name in first_wave + [(NOTE, k) for k in range(1, n_bucket)]:
        copies.need(name)
    for name in (W_SECOND_CONV, W_TRIPLE_WEIGHT, W_OUTPUT_WEIGHT):
        copies.start(name, big[name], kept[name])
    copies.start(COT, cotangent.at[n : n + 1], kept[COT])
    copies.start(GT, gt_in, v_triple)
    copies.start(GO, go_in, v_out)
    copies.start(FULL_ACT, act2_in.at[0:n], full_act.at[0:n])
    copies.start(FULL_MID, dmid_in.at[0:n], full_mid)
    moment = jnp.where(keeps, times[0, 0, n], times[0, 0, WORK]).astype(F32)
    moment = jnp.full((1, 1), moment, F32)
    for k in range(1, n_bucket):
        moment = jnp.where(offset == k, note[k, 0:1, 0:1], moment)

    lane = lax.broadcasted_iota(jnp.int32, (1, C), 1)
    clock = jnp.where(lane == n, moment, 0.0)
    for i in range(n):
        clock = jnp.where(lane == i, times[0, 0, i].astype(F32), clock)
    notes[...] = jnp.zeros(notes.shape, F32)
    notes[0:1, :] = clock
    if n_bucket == 4:
        even = codes[0] == 0
        neighbour = jnp.where(even, note[1, 0:1, 1:2], note[2, 0:1, 1:2])
        first = jnp.where(even, 1.0, 2.0)
        notes[1:2, :] = jnp.broadcast_to(jnp.where(neighbour == 3.0, 1.0, 0.0), (1, C))
        notes[2:3, :] = jnp.broadcast_to(jnp.where(neighbour == first, 1.0, 0.0), (1, C))

    def accumulate(gw_out, gw_triple):
        scatter_unit(blocks_c, 3, gw_out + v_out[...], codes_c)
        total = gw_triple + v_triple[...]
        for part in range(3):
            scatter_unit(blocks_c, part, total[:, part * C : (part + 1) * C], codes_c)

    targets = {
        OUT: out.at[n:WORK], DMID: dmid.at[n:WORK], OUT1: out1.at[n:WORK], ACT1: act1.at[n:WORK],
        ACT2: act2.at[n:WORK], STATS: stats.at[n:WORK],
    }
    def need(name):
        if name == W_SECOND_CONV:
            for later in (W_SECOND_CONV, W_TRIPLE_WEIGHT, W_OUTPUT_WEIGHT, COT, GT, GO, FULL_ACT, FULL_MID):
                copies.need(later)

    def ready(name):
        if name == DMID:
            for v in targets:
                copies.start((TO, v), kept[v], targets[v])
            copies.start((TO, LAST), kept[X].at[0], last)
            copies.start((TO, GIVE_C), blocks_c.at[8:16], give_c)
            copies.start((TO, KEEP_C), blocks_c.at[0:8], keep_c)

    w = {**small, **{name: kept[name] for name in BIG}}
    pieces = front(
        1, kept[X], kept[COT], [moment], w, kept[OUT], kept[DMID], kept[OUT1], kept[ACT1], kept[ACT2],
        kept[STATS], None, None, None, *scratch, accumulate, need, ready,
    )
    store_sums(sums, pieces, sums_in)

    clear_borders(full_shift, WORK)

    def early(i, r):
        store_shifted(full_shift, i, r, full_mid[i, pl.ds(r, CHUNK), :], True)

    def late(i, r):
        store_shifted(full_shift, i + n, r, kept[DMID][i, pl.ds(r, CHUNK), :], True)

    over_chunks(n, early)
    over_chunks(1, late)
    full_act[n] = kept[ACT2][0]
    act = full_act[...].reshape(WORK * TOK, C)
    for di in range(3):
        g = dot(act, window(full_shift, WORK, 2 - di), TN)
        for dj in range(3):
            scatter_unit(blocks, di * 3 + dj, g[:, dj * C : (dj + 1) * C], codes)
    copies.start((TO, GIVE), blocks.at[8:16], give)
    copies.start((TO, KEEP), blocks.at[0:8], keep)
    copies.finish()


def swish_norm_backward(dact, values, base, stats, row, gain, shift, hold, same, dpre, write):
    def sums_of(i, r):
        rows = pl.ds(r, CHUNK)
        unit = (base[i, rows, :] - stats[i, row : row + 1, :]) * stats[i, row + 1 : row + 2, :]
        pre = unit * gain + shift
        s = sigmoid(pre)
        d = dact[i, rows, :] * (s * (1.0 + pre * (1.0 - s)))
        dpre[i, rows, :] = d
        return d, d * unit

    sum_d, sum_du = column_sums(WORK, 2, sums_of, hold)
    first_mean = group_mean(sum_d * gain, same)
    second_mean = group_mean(sum_du * gain, same)

    def inner(i, r):
        rows = pl.ds(r, CHUNK)
        scaled = stats[i, row + 1 : row + 2, :]
        unit = (base[i, rows, :] - stats[i, row : row + 1, :]) * scaled
        m1 = first_mean[i : i + 1, :]
        m2 = second_mean[i : i + 1, :]
        return write(i, r, (dpre[i, rows, :] * gain - m1 - unit * m2) * scaled)

    sums = column_sums(WORK, 1, inner, hold)[0]
    return sum_d, sum_du, sums


def conv_backward(shifted, kernel, dact):
    low = [jnp.concatenate([kernel[di, dj].astype(BF16) for dj in range(3)], axis=1) for di in range(3)]
    for i in range(WORK):
        total = None
        for di in range(3):
            part = dot(shifted[i, SIDE * (2 - di) : SIDE * (2 - di) + TOK, :], low[di], NT)
            total = part if total is None else total + part
        dact[i] = total


def kernel_three(notes, dmid_in, out1_in, act1_in, stats, sums_in, kernel_in, gain_ref, shift_ref,
                 give, keep, low, sums, rows_out,
                 shifted, hold, dact, dpre, same_ref, dmid, out1, act1, kernel, blocks, v_low, v_small, sems):
    copies = Copies(sems)
    copies.start(GAIN, gain_ref, v_small.at[0])
    copies.start(SHIFT, shift_ref, v_small.at[1])
    gain_ref, shift_ref = v_small.at[0], v_small.at[1]
    copies.start(DMID, dmid_in, dmid)
    copies.start(KERNEL, kernel_in, kernel)
    copies.start(OUT1, out1_in, out1)
    copies.start(ACT1, act1_in, act1)
    same_ref[...] = group_matrix()
    same = same_ref[...]
    codes = owner_codes(CHUNK_B)
    clear_borders(shifted, WORK)
    copies.need(DMID)

    def load(i, r):
        store_shifted(shifted, i, r, dmid[i, pl.ds(r, CHUNK), :], True)

    over_chunks(WORK, load)
    copies.need(KERNEL)
    conv_backward(shifted, kernel, dact)
    for name in (OUT1, ACT1, GAIN, SHIFT):
        copies.need(name)

    def write(i, r, g):
        v_low[i, pl.ds(r, CHUNK), :] = g.astype(BF16)
        store_shifted(shifted, i, r, g, True)
        return (g,)

    sum_d, sum_du, sum_first = swish_norm_backward(
        dact, None, out1, stats, 2, gain_ref[...], shift_ref[...], hold, same, dpre, write
    )
    copies.start((TO, LOW), v_low, low)

    def tap(di, carry):
        rows = pl.ds(pl.multiple_of(SIDE * (2 - di), SIDE), TOK)
        g = dot(act1[...].reshape(WORK * TOK, C), shifted[:, rows, :].reshape(WORK * TOK, 3 * C), TN)
        for dj in range(3):
            scatter_unit(blocks, di * 3 + dj, g[:, dj * C : (dj + 1) * C], codes)
        return carry

    lax.fori_loop(0, 3, tap, 0)
    copies.start((TO, GIVE), blocks.at[8:16], give)
    copies.start((TO, KEEP), blocks.at[0:8], keep)
    sums[...] = sums_in[...]
    sums[R_SEC_GAIN : R_SEC_GAIN + 1, :] = jnp.sum(sum_du, axis=0, keepdims=True)
    sums[R_SEC_SHIFT : R_SEC_SHIFT + 1, :] = jnp.sum(sum_d, axis=0, keepdims=True)
    sums[R_EMB_BIAS : R_EMB_BIAS + 1, :] = jnp.sum(sum_first, axis=0, keepdims=True)
    core = lax.axis_index(BATCH) % 2
    place = chip_place() * 2 + core
    spots = lax.broadcasted_iota(jnp.int32, (4, C), 0) * C + lax.broadcasted_iota(jnp.int32, (4, C), 1)
    clocks = jnp.zeros((4, C), F32)
    for i in range(WORK):
        clocks = jnp.where(spots == place * WORK + i, notes[0:1, i : i + 1], clocks)
    sums[R_CLOCKS : R_CLOCKS + 4, :] = clocks
    four = sum_first[0:WORK]
    both = jnp.concatenate([four, four], axis=0)
    half = lax.broadcasted_iota(jnp.int32, (8, C), 0) // WORK
    rows_out[...] = jnp.where(half == core, both, 0.0)
    copies.finish()


def kernel_four(n_bucket, counts, source, images, last, dmid_in, low_in, stats, sums_in, rows_in, kernel_in, gain_ref, shift_ref,
                grad, back, sums,
                shifted, hold, dact, dpre, same_ref, dmid, base, low, kernel, v_back, v_small, sems):
    n = WORK - 1
    copies = Copies(sems)
    copies.start(GAIN, gain_ref, v_small.at[0])
    copies.start(SHIFT, shift_ref, v_small.at[1])
    gain_ref, shift_ref = v_small.at[0], v_small.at[1]
    copies.start(LOW, low_in, low)
    copies.start(KERNEL, kernel_in, kernel)
    copies.start(BASE, images.at[0:n], base.at[0:n])
    copies.start(LAST, last, base.at[n])
    copies.start(DMID, dmid_in, dmid)
    same_ref[...] = group_matrix()
    same = same_ref[...]
    clear_borders(shifted, WORK)
    copies.need(LOW)

    def load(i, r):
        store_shifted(shifted, i, r, low[i, pl.ds(r, CHUNK), :].astype(F32), True)

    over_chunks(WORK, load)
    copies.need(KERNEL)
    conv_backward(shifted, kernel, dact)
    for name in (BASE, LAST, DMID, GAIN, SHIFT):
        copies.need(name)

    def write(i, r, g):
        rows = pl.ds(r, CHUNK)
        dpre[i, rows, :] = g + dmid[i, rows, :]
        return (g,)

    sum_d, sum_du, _ = swish_norm_backward(
        dact, None, base, stats, 0, gain_ref[...], shift_ref[...], hold, same, dpre, write
    )
    copies.start((TO, GRAD), dpre.at[0:n], grad.at[0:n])
    keeps, offset = place_offset(counts, source)
    if n_bucket == 4:
        even = lax.axis_index(BATCH) % 2 == 0
        first = jnp.where(even, 1, 2)
        v_back[0] = jnp.where((offset & first) != 0, dpre[n], 0.0)
        v_back[1] = jnp.where(offset == 3 - first, dpre[n], 0.0)
    else:
        for k in range(1, n_bucket):
            v_back[k - 1] = jnp.where(offset == k, dpre[n], 0.0)
    copies.start((TO, BACK), v_back, back)
    dmid[n] = jnp.where(keeps, dpre[n], 0.0)
    copies.start((TO, SLOT), dmid.at[n], grad.at[n])
    sums[0:SUMS] = sums_in[...]
    sums[SUMS : SUMS + 8] = rows_in[...]
    sums[R_FIRST_GAIN : R_FIRST_GAIN + 1, :] = jnp.sum(sum_du, axis=0, keepdims=True)
    sums[R_FIRST_SHIFT : R_FIRST_SHIFT + 1, :] = jnp.sum(sum_d, axis=0, keepdims=True)
    copies.finish()


def kernel_pack(times, counts, source, images, out, sem):
    copy = pltpu.make_async_copy(images.at[WORK], out.at[0:TOK], sem)
    copy.start()
    _, offset = place_offset(counts, source)
    lane = lax.broadcasted_iota(jnp.int32, (8, C), 1)
    moment = times[0, 0, WORK].astype(F32)
    out[TOK : TOK + 8] = jnp.where(lane == 0, moment, jnp.where(lane == 1, offset.astype(F32), 0.0))
    copy.wait()


def whole(shape):
    return pl.BlockSpec(shape, lambda *_: (0,) * len(shape), memory_space=pltpu.VMEM)


def part(shape, first):
    return pl.BlockSpec(shape, lambda *_: (first,) + (0,) * (len(shape) - 1), memory_space=pltpu.VMEM)


SMEM = pl.BlockSpec(memory_space=pltpu.SMEM)
ANY = pl.BlockSpec(memory_space=pl.ANY)
HBM = pl.BlockSpec(memory_space=pltpu.HBM)


def params(mebibytes=26):
    return pltpu.CompilerParams(vmem_limit_bytes=mebibytes * 1024 * 1024)


def shape(dims, dtype=F32):
    return jax.ShapeDtypeStruct(dims, dtype)


def weight_specs(w):
    return [whole(w[name].shape) for name in WEIGHTS]


def call_pack(timesteps, counts, source, images):
    return pl.pallas_call(
        kernel_pack,
        name="pack_spare",
        in_specs=[SMEM, SMEM, SMEM, ANY],
        out_specs=pl.BlockSpec(memory_space=pltpu.VMEM),
        out_shape=shape((TOK + 8, C)),
        scratch_shapes=[pltpu.SemaphoreType.DMA],
        cost_estimate=pl.CostEstimate(flops=20_000_000_000, bytes_accessed=1_000_000, transcendentals=0),
        compiler_params=params(),
    )(timesteps, counts, source, images)


VMEM = pl.BlockSpec(memory_space=pltpu.VMEM)
IMAGE_ARRAYS = (
    ((WORK, TOK, C), F32), ((WORK, TOK, C), F32), ((WORK, TOK, C), F32), ((WORK, TOK, C), BF16), ((WORK, TOK, C), BF16),
    ((WORK, 8, C), F32),
)


def call_one(timesteps, images, cot, w):
    n = WORK - 1
    return pl.pallas_call(
        kernel_one,
        name="front_of_own_images",
        in_specs=[SMEM, HBM, HBM] + [HBM] * (len(SMALL) + len(BIG)),
        out_specs=[ANY] * 8 + [VMEM],
        out_shape=[shape(*s) for s in IMAGE_ARRAYS] + [shape((C, 3 * C)), shape((C, C)), shape((SUMS, C))],
        scratch_shapes=front_scratch(n) + held(n)
        + [pltpu.VMEM((C, 3 * C), F32), pltpu.VMEM((C, C), F32), pltpu.VMEM((len(SMALL), 1, C), F32),
           pltpu.SemaphoreType.DMA((FRONT_SEMS,))],
        cost_estimate=pl.CostEstimate(flops=20_000_000_000, bytes_accessed=1_000_000, transcendentals=0),
        compiler_params=params(),
    )(timesteps, images, cot, *[w[name] for name in SMALL], *[w[name] for name in BIG])


def call_two(timesteps, counts, source, images, cot, arrived, w, early):
    out, dmid, out1, act1, act2, stats, g_triple, g_out, sums = early
    n_bucket = len(arrived) + 1
    first = 5 + len(arrived) + len(SMALL) + len(BIG)
    half, half_c = (8, 9, 16, C), (8, 4, 16, C)
    return pl.pallas_call(
        lambda *refs: kernel_two(n_bucket, *refs),
        name="front_of_last_image",
        in_specs=[SMEM, SMEM, SMEM, HBM, HBM] + [ANY] * len(arrived) + [HBM] * (len(SMALL) + len(BIG))
        + [VMEM] + [ANY] * 8,
        out_specs=[ANY] * 6 + [VMEM] + [ANY] * 5 + [VMEM],
        out_shape=[shape(*s) for s in IMAGE_ARRAYS]
        + [shape((SUMS, C)), shape(half), shape(half), shape(half_c), shape(half_c), shape((TOK, C)), shape((8, C))],
        scratch_shapes=front_scratch(1) + held(1)
        + [
            pltpu.VMEM((WORK, TOK, C), BF16), pltpu.VMEM((WORK, PAD, 3 * C), BF16), pltpu.VMEM((WORK - 1, TOK, C), F32),
            pltpu.VMEM((16, 9, 16, C), F32), pltpu.VMEM((16, 4, 16, C), F32), pltpu.VMEM((C, 3 * C), F32), pltpu.VMEM((C, C), F32),
            pltpu.VMEM((n_bucket, 8, C), F32), pltpu.VMEM((len(SMALL), 1, C), F32),
            pltpu.SemaphoreType.DMA((FRONT_SEMS + n_bucket,)),
        ],
        input_output_aliases={first + 5: 0, first + 3: 1, first + 6: 2, first + 7: 3, first + 4: 4, first + 8: 5},
        cost_estimate=pl.CostEstimate(flops=20_000_000_000, bytes_accessed=1_000_000, transcendentals=0),
        compiler_params=params(),
    )(
        timesteps, counts, source, images, cot, *arrived, *[w[name] for name in SMALL], *[w[name] for name in BIG],
        sums, g_triple, g_out, dmid, act2, out, out1, act1, stats,
    )


def back_scratch():
    return [
        pltpu.VMEM((WORK, PAD, 3 * C), BF16),
        pltpu.VMEM((16, 8, C), F32),
        pltpu.VMEM((WORK, TOK, C), F32),
        pltpu.VMEM((WORK, TOK, C), F32),
        pltpu.VMEM((C, C), BF16),
    ]


def call_three(notes, dmid, out1, act1, stats, sums, w):
    full = (WORK, TOK, C)
    half = (8, 9, 16, C)
    return pl.pallas_call(
        kernel_three,
        name="back_to_first_out",
        in_specs=[VMEM, ANY, ANY, ANY, VMEM, VMEM, HBM, HBM, HBM],
        out_specs=[ANY, ANY, ANY, VMEM, VMEM],
        out_shape=[shape(half), shape(half), shape(full, BF16), shape((SUMS, C)), shape((8, C))],
        scratch_shapes=back_scratch()
        + [
            pltpu.VMEM(full, F32), pltpu.VMEM(full, F32), pltpu.VMEM(full, BF16), pltpu.VMEM((3, 3, C, C), F32),
            pltpu.VMEM((16, 9, 16, C), F32), pltpu.VMEM(full, BF16), pltpu.VMEM((2, 1, C), F32),
            pltpu.SemaphoreType.DMA((12,)),
        ],
        compiler_params=params(),
    )(notes, dmid, out1, act1, stats, sums, w[W_SECOND_CONV], w[W_SECOND_GAIN], w[W_SECOND_SHIFT])


def call_four(n_bucket, counts, source, images, last, dmid, low, stats, sums, rows, w):
    full = (WORK, TOK, C)
    backs = 2 if n_bucket == 4 else n_bucket - 1
    return pl.pallas_call(
        lambda *refs: kernel_four(n_bucket, *refs),
        name="back_to_images",
        in_specs=[SMEM, SMEM, HBM, ANY, ANY, ANY, VMEM, VMEM, VMEM, HBM, HBM, HBM],
        out_specs=[ANY, ANY, VMEM],
        out_shape=[shape((WORK + 1, TOK, C)), shape((backs, TOK, C)), shape((SUMS + 8, C))],
        scratch_shapes=back_scratch()
        + [
            pltpu.VMEM(full, F32), pltpu.VMEM(full, F32), pltpu.VMEM(full, BF16), pltpu.VMEM((3, 3, C, C), F32),
            pltpu.VMEM((backs, TOK, C), F32), pltpu.VMEM((2, 1, C), F32), pltpu.SemaphoreType.DMA((12,)),
        ],
        compiler_params=params(),
    )(counts, source, images, last, dmid, low, stats, sums, rows, w[W_FIRST_CONV], w[W_FIRST_GAIN], w[W_FIRST_SHIFT])


def assemble_kernel(*refs):
    first, second, triple, out = refs[6:10]
    copies = Copies(refs[-1])
    for n, order in enumerate((CHUNK_A, CHUNK_C, CHUNK_B)):
        core, even, odd = owner_codes(order)
        for half in range(2):
            src = refs[2 * n + half]
            holder = core if half == 0 else 1 - core
            code = jnp.where(holder == 0, even, odd)
            for low in range(8):
                block = holder * 8 + (low ^ code)
                rows = pl.ds(pl.multiple_of(block * 16, 16), 16)
                if n != 1:
                    copies.start((n, half, low), src.at[low], (second if n == 0 else first).at[:, rows, :])
                    continue
                for p in range(3):
                    copies.start((n, half, low, p), src.at[low, p], triple.at[rows, p * C : (p + 1) * C])
                copies.start((n, half, low), src.at[low, 3], out.at[rows, :])
    copies.finish()


def assemble(*halves):
    return pl.pallas_call(
        assemble_kernel,
        name="assemble",
        in_specs=[ANY] * 6,
        out_specs=[ANY] * 4,
        out_shape=[shape((9, C, C)), shape((9, C, C)), shape((C, 3 * C)), shape((C, C))],
        scratch_shapes=[pltpu.SemaphoreType.DMA((16 + 16 + 16 * 4,))],
        cost_estimate=pl.CostEstimate(flops=1, bytes_accessed=1, transcendentals=0),
        compiler_params=params(2),
    )(*halves)


def high_code():
    b, t = lax.axis_index(BUCKET), lax.axis_index(BATCH)
    return (t // 4) * (lax.axis_size(BUCKET) // 4) + b // 4


def chip_place():
    bits = chip_bits()
    many = lax.axis_size(BUCKET) * lax.axis_size(BATCH) // 16
    return (bits["x"] * 4 + bits["y"] * 2 + bits["z"]) * many + high_code()


def embed_kernel(devices, order, gathered, sums, out, rows):
    core = lax.axis_index(BATCH) % 2
    bits = chip_bits()
    mine = bits["x"] * 4 + bits["y"] * 2 + bits["z"]
    high = high_code()
    many = devices // 16
    weight = {"x": 4, "y": 2, "z": 1}
    for place in range(devices // 2):
        rest, code = place % many, place // many
        turned = [
            sum(((code >> (2 - n)) & 1) * weight[o[n]] for n in range(3)) for o in order
        ]
        code = jnp.where(core == 0, turned[0], turned[1]) ^ mine
        rows[code * many + (rest ^ high)] = gathered[place]
    count = WORK * devices
    grads = rows[...].reshape(count, C)
    half = TEMB // 2
    moments = []
    for n in range(0, count, C):
        size = min(C, count)
        row = lax.broadcasted_iota(jnp.int32, (size, C), 0)
        lane = lax.broadcasted_iota(jnp.int32, (size, C), 1)
        clocks = sums[R_CLOCKS + n // C : R_CLOCKS + n // C + 1, :]
        moments.append(jnp.sum(jnp.where(row == lane, clocks, 0.0), axis=1, keepdims=True))
    moments = jnp.concatenate(moments, axis=0) if len(moments) > 1 else moments[0]
    frequency = jnp.exp(
        lax.broadcasted_iota(jnp.int32, (count, half), 1).astype(F32) * (-math.log(10000.0) / (half - 1))
    )
    angles = moments * frequency
    waves = jnp.concatenate([jnp.sin(angles), jnp.cos(angles)], axis=1)
    waves = waves * sigmoid(waves)
    out[...] = lax.dot_general(waves, grads, TN, precision=lax.Precision.HIGHEST, preferred_element_type=F32)


def embed_gradient(devices, order, gathered, sums):
    return pl.pallas_call(
        lambda *refs: embed_kernel(devices, order, *refs),
        name="embed_gradient",
        in_specs=[VMEM, VMEM],
        out_specs=VMEM,
        out_shape=shape((TEMB, C)),
        scratch_shapes=[pltpu.VMEM((devices // 2, 8, C), F32)],
        cost_estimate=pl.CostEstimate(flops=1, bytes_accessed=1, transcendentals=0),
        compiler_params=params(),
    )(gathered, sums)


AXES = (BUCKET, BATCH)


def solution(mesh):
    n_bucket, n_batch = mesh.shape[BUCKET], mesh.shape[BATCH]
    devices = n_bucket * n_batch

    def flips(fn):
        pairs = []
        for b in range(n_bucket):
            for t in range(n_batch):
                nb, nt = fn(b, t)
                pairs.append((b * n_batch + t, nb * n_batch + nt))
        return pairs

    def by_core(even, odd):
        def fn(b, t):
            kind, bit = even if t % 2 == 0 else odd
            return (b ^ bit, t) if kind == 0 else (b, t ^ bit)

        return flips(fn)

    x, y, z = (0, 1), (0, 2), (1, 2)
    core_perm = flips(lambda b, t: (b, t ^ 1))
    links = {"x": x, "y": y, "z": z}
    rest = []
    bit = 4
    while bit < n_bucket:
        rest.append((0, bit))
        bit *= 2
    bit = 4
    while bit < n_batch:
        rest.append((1, bit))
        bit *= 2
    rest_perms = [by_core(s, s) for s in rest]
    bucket_perms = [flips(lambda b, t, k=k: (b ^ k, t)) for k in range(1, n_bucket)]

    def send(v, perm):
        return lax.ppermute(v, AXES, perm)

    def after(v, *others):
        return lax.optimization_barrier((v,) + others)[0]

    def held_by(v, other):
        row = other.reshape(-1, C)[0:1]
        return v + 0.0 * row.reshape((1,) * (v.ndim - 1) + (C,))

    class Chunk:
        def __init__(self, order, give, keep, units):
            self.perms = [by_core(links[p], links[q]) for p, q in zip(*order)]
            self.rows = units * 16
            self.stage = 0
            self.size = give.shape
            self.keep = keep.reshape(2, 2, 2, self.rows, C)
            self.got = send(give, core_perm).reshape(2, 2, 2, self.rows, C)
            self.extra = None

        def step(self, *deps, late=None):
            n_rest = len(rest_perms)
            k = self.stage
            self.stage += 1
            if k < 3:
                out, self.keep = self.keep[1] + self.got[1], self.keep[0] + self.got[0]
                perm = self.perms[k]
            else:
                self.take()
                if k < 3 + n_rest:
                    perm = rest_perms[k - 3]
                else:
                    if k == 3 + n_rest:
                        self.keep = self.keep[None]
                    j = k - 3 - n_rest
                    perm = self.perms[2 - j] if j < 3 else core_perm
                out = self.keep
                if self.extra is not None and perm is not core_perm:
                    sums, rows = self.extra
                    out = jnp.concatenate([out.reshape(-1, C), sums, rows.reshape(-1, C)], axis=0)
            if late is not None:
                out = held_by(out, late)
            out = after(out, *deps)
            self.got = send(out, perm)
            return out

        def take(self):
            n_rest = len(rest_perms)
            k = self.stage - 1
            got = self.got
            if k == 3:
                self.keep = self.keep + got
                return
            if self.extra is not None:
                sums, rows = self.extra
                size = self.keep.size // C
                rows = jnp.concatenate([rows, got[size + SUMS :].reshape(rows.shape)], axis=0)
                self.extra = sums + got[size : size + SUMS], rows
                got = got[:size]
            got = got.reshape(self.keep.shape)
            if k <= 3 + n_rest:
                self.keep = self.keep + got
            else:
                self.keep = jnp.concatenate([self.keep, got], axis=0)

        def halves(self):
            dims = (8, self.rows // 16, 16, C)
            return self.keep.reshape(dims), self.got.reshape(dims)

    def shards(images, timesteps, counts, source, cotangent, *weights):
        w = dict(zip(WEIGHTS, weights))
        w = {k: v.reshape(1, C) if v.ndim == 1 else v for k, v in w.items()}
        slots = images[0, 0]
        cot = cotangent[0, 0]

        spare = call_pack(timesteps, counts, source, slots)
        arrived = [send(spare, p) for p in bucket_perms]
        early = call_one(timesteps, slots, cot, w)
        out, dmid, out1, act1, act2, stats, sums, give_a, keep_a, give_c, keep_c, last, notes = call_two(
            timesteps, counts, source, slots, cot, arrived, w, early
        )
        chunk_a = Chunk(CHUNK_A, give_a, keep_a, 9)
        chunk_c = Chunk(CHUNK_C, give_c, keep_c, 4)
        give_b, keep_b, low, sums, rows = call_three(notes, dmid, out1, act1, stats, sums, w)
        chunk_b = Chunk(CHUNK_B, give_b, keep_b, 9)

        tie = chunk_a.step()
        tie = chunk_c.step(tie)
        tie = chunk_b.step(tie)
        grad, back, extra = call_four(n_bucket, counts, source, slots, last, dmid, after(low, tie), stats, sums, rows, w)
        extra = extra + send(extra, core_perm)
        total = 3 + len(rest_perms) + 3
        home = None
        for k in range(1, total):
            if k == 3:
                chunk_c.extra = extra[:SUMS], extra[None, SUMS:]
            tie = chunk_a.step(tie)
            tie = chunk_c.step(tie)
            tie = chunk_b.step(tie, late=home if k == 5 else None)
            if n_bucket == 4:
                if k == 2:
                    hop = send(after(back[0], tie), by_core(x, y))
                if k == 3:
                    turn = after(jnp.where(notes[1:2] != 0.0, hop, back[1]), tie)
                    got = send(turn, by_core(y, x))
                if k == 4:
                    home = jnp.where(notes[2:3] != 0.0, hop, got)
                    grad = lax.dynamic_update_slice(grad, home[None], (WORK, 0, 0))
            elif k == 1:
                home = send(back[0], bucket_perms[0])
                for n in range(2, n_bucket):
                    home = home + send(back[n - 1], bucket_perms[n - 1])
                grad = lax.dynamic_update_slice(grad, home[None], (WORK, 0, 0))
        tie = chunk_a.step(tie)
        tie = chunk_c.step(tie)
        tie = chunk_b.step(tie)
        sums, rows = chunk_c.extra
        g_embed = embed_gradient(devices, CHUNK_C, rows, sums)
        g_first, g_second, g_triple, g_out = assemble(*chunk_a.halves(), *chunk_c.halves(), *chunk_b.halves())

        def vec(r):
            return sums[r]

        return (
            out[None, None], grad[None, None],
            vec(R_FIRST_GAIN), vec(R_FIRST_SHIFT), g_first.reshape(3, 3, C, C), g_embed, vec(R_EMB_BIAS),
            vec(R_SEC_GAIN), vec(R_SEC_SHIFT), g_second.reshape(3, 3, C, C), vec(R_SEC_BIAS),
            vec(R_ATT_GAIN), vec(R_ATT_SHIFT), g_triple, vec(R_QUERY_BIAS), vec(R_VALUE_BIAS),
            g_out, vec(R_OUT_BIAS),
        )

    placed = (
        P(BATCH, BUCKET, None, None, None), P(BATCH, BUCKET, None), P(BATCH, BUCKET),
        P(BATCH, BUCKET), P(BATCH, BUCKET, None, None, None),
    ) + (P(),) * 16
    return jax.shard_map(
        shards,
        mesh=mesh,
        in_specs=placed,
        out_specs=(P(BATCH, BUCKET, None, None, None),) * 2 + (P(),) * 16,
        check_vma=False,
    )
```

```python
import math

import jax
import jax.numpy as jnp
from jax import lax
from jax.experimental import pallas as pl
from jax.experimental.pallas import tpu as pltpu
from jax.sharding import PartitionSpec as P

TEMB = 512
GROUPS = 32
SIDE = 16
WORK = 4
TOK = SIDE * SIDE
C = 256
PAD = TOK + 2 * SIDE
EPSILON = 1e-06
COUNT = float(TOK * (C // GROUPS))
CHUNK = 64
F32 = jnp.float32
BATCH, BUCKET = "batch", "bucket"
BF16 = jnp.bfloat16
NT = (((1,), (1,)), ((), ()))
TN = (((0,), (0,)), ((), ()))

R_OUT_BIAS, R_QUERY_BIAS, R_VALUE_BIAS, R_ATT_GAIN, R_ATT_SHIFT, R_SEC_BIAS = 0, 1, 2, 3, 4, 5
R_SEC_GAIN, R_SEC_SHIFT, R_EMB_BIAS, R_FIRST_GAIN, R_FIRST_SHIFT, R_CLOCKS = 6, 7, 8, 9, 10, 11
SUMS = 16


(W_FIRST_GAIN, W_FIRST_SHIFT, W_FIRST_CONV, W_EMBED_WEIGHT, W_EMBED_BIAS, W_SECOND_GAIN, W_SECOND_SHIFT, W_SECOND_CONV,
    W_SECOND_BIAS, W_ATTEND_GAIN, W_ATTEND_SHIFT, W_TRIPLE_WEIGHT, W_QUERY_BIAS, W_VALUE_BIAS, W_OUTPUT_WEIGHT,
    W_OUTPUT_BIAS) = WEIGHTS = range(16)
(X, COT, OUT, DMID, OUT1, ACT1, ACT2, STATS, G_TRIPLE, G_OUT, GT, GO, FULL_ACT, FULL_MID, KERNEL, GAIN, SHIFT, BASE,
    LAST, LOW, GIVE, KEEP, GIVE_C, KEEP_C, GRAD, BACK, SLOT, TO, NOTE, SMALL_ONE) = range(16, 46)


def dot(a, b, dims=(((1,), (0,)), ((), ()))):
    return lax.dot_general(a, b, dims, preferred_element_type=F32)


def sigmoid(v):
    return 0.5 * jnp.tanh(0.5 * v) + 0.5


def group_matrix():
    row = lax.broadcasted_iota(jnp.int32, (C, C), 0) // (C // GROUPS)
    col = lax.broadcasted_iota(jnp.int32, (C, C), 1) // (C // GROUPS)
    return (row == col).astype(F32).astype(BF16)


def group_mean(sums, same):
    high = sums.astype(BF16).astype(F32)
    rest = sums - high
    mid = rest.astype(BF16).astype(F32)
    low = rest - mid
    total = dot(jnp.concatenate([high, mid, low], axis=0).astype(BF16), same)
    return (total[0:8] + total[8:16] + total[16:24]) * (1.0 / COUNT)


def over_chunks(count, body):
    for image in range(count):
        for row in range(0, TOK, CHUNK):
            body(image, row)


def fold(v):
    return jnp.sum(v.reshape(v.shape[0] // 8, 8, v.shape[1]), axis=0)


def column_sums(count, parts, body, hold):
    out = [[] for _ in range(parts)]
    for image in range(count):
        totals = [None] * parts
        for row in range(0, TOK, CHUNK):
            for part, v in enumerate(body(image, row)):
                f = fold(v)
                totals[part] = f if totals[part] is None else totals[part] + f
        for part in range(parts):
            out[part].append(jnp.sum(totals[part], axis=0, keepdims=True))
    return [jnp.concatenate(rows + [jnp.zeros((8 - count, C), F32)], axis=0) for rows in out]


def edge_masks():
    column = lax.broadcasted_iota(jnp.int32, (CHUNK, C), 0) % SIDE
    return column == 0, column == SIDE - 1


def store_shifted(ref, image, row, v, backward):
    first, last = edge_masks()
    before = jnp.where(first, 0.0, pltpu.roll(v, 1, 0)).astype(BF16)
    after = jnp.where(last, 0.0, pltpu.roll(v, CHUNK - 1, 0)).astype(BF16)
    rows = pl.ds(row + SIDE, CHUNK)
    left, right = (after, before) if backward else (before, after)
    ref[image, rows, 0:C] = left
    ref[image, rows, C : 2 * C] = v.astype(BF16)
    ref[image, rows, 2 * C : 3 * C] = right


def clear_borders(ref, count):
    for i in range(count):
        ref[i, 0:SIDE, :] = jnp.zeros((SIDE, 3 * C), BF16)
        ref[i, PAD - SIDE : PAD, :] = jnp.zeros((SIDE, 3 * C), BF16)


def window(ref, count, di):
    return ref[0:count, SIDE * di : SIDE * di + TOK, :].reshape(count * TOK, 3 * C)


def convolve(shifted, image, kernel):
    total = None
    for di in range(3):
        part = dot(shifted[image, SIDE * di : SIDE * di + TOK, :], kernel[di])
        total = part if total is None else total + part
    return total


def norm_stats(count, ref, hold, same):
    (sums,) = column_sums(count, 1, lambda i, r: (ref[i, pl.ds(r, CHUNK), :],), hold)
    return sums_to_stats(count, sums, ref, hold, same)


def sums_to_stats(count, sums, ref, hold, same):
    mean = group_mean(sums, same)

    def squares(i, r):
        d = ref[i, pl.ds(r, CHUNK), :] - mean[i : i + 1, :]
        return (d * d,)

    (second,) = column_sums(count, 1, squares, hold)
    return mean, lax.rsqrt(group_mean(second, same) + EPSILON)


def front(
    count, x, cot, times, w, out, dmid, out1, act1, act2, stats, sums, g_triple, g_out,
    shifted, hold, mid, normed, triple, mixed, dmixed, dtriple, dnormed, same_ref, accumulate, need, ready,
):
    same = same_ref[...]

    def vec(name):
        return w[name][...]

    need(X)
    mean, scale = norm_stats(count, x, hold, same)
    for i in range(count):
        stats[i, 0:1, :] = mean[i : i + 1]
        stats[i, 1:2, :] = scale[i : i + 1]
    clear_borders(shifted, count)
    gain, shift = vec(W_FIRST_GAIN), vec(W_FIRST_SHIFT)

    def first(i, r):
        rows = pl.ds(r, CHUNK)
        pre = (x[i, rows, :] - stats[i, 0:1, :]) * stats[i, 1:2, :] * gain + shift
        act = pre * sigmoid(pre)
        act1[i, rows, :] = act.astype(BF16)
        store_shifted(shifted, i, r, act, False)

    over_chunks(count, first)
    ready(ACT1)

    half = TEMB // 2
    lane = lax.broadcasted_iota(jnp.int32, (8, half), 1).astype(F32)
    row = lax.broadcasted_iota(jnp.int32, (8, half), 0)
    frequency = jnp.exp(lane * (-math.log(10000.0) / (half - 1)))
    clock = jnp.zeros((8, half), F32)
    for i in range(count):
        clock = jnp.where(row == i, times[i], clock)
    angles = clock * frequency
    waves = jnp.concatenate([jnp.sin(angles), jnp.cos(angles)], axis=1)
    waves = waves * sigmoid(waves)
    need(W_EMBED_WEIGHT)
    stepped = lax.dot_general(
        waves, w[W_EMBED_WEIGHT][...], (((1,), (0,)), ((), ())),
        precision=lax.Precision.HIGHEST, preferred_element_type=F32,
    ) + vec(W_EMBED_BIAS)

    need(W_FIRST_CONV)
    kernel = w[W_FIRST_CONV]
    low = [kernel[di].reshape(3 * C, C).astype(BF16) for di in range(3)]
    for i in range(count):
        out1[i] = convolve(shifted, i, low) + stepped[i : i + 1]
    ready(OUT1)

    mean, scale = norm_stats(count, out1, hold, same)
    for i in range(count):
        stats[i, 2:3, :] = mean[i : i + 1]
        stats[i, 3:4, :] = scale[i : i + 1]
    gain2, shift2 = vec(W_SECOND_GAIN), vec(W_SECOND_SHIFT)

    def second(i, r):
        rows = pl.ds(r, CHUNK)
        pre = (out1[i, rows, :] - stats[i, 2:3, :]) * stats[i, 3:4, :] * gain2 + shift2
        act = pre * sigmoid(pre)
        act2[i, rows, :] = act.astype(BF16)
        store_shifted(shifted, i, r, act, False)

    over_chunks(count, second)
    ready(ACT2)
    need(W_SECOND_CONV)
    kernel = w[W_SECOND_CONV]
    low = [kernel[di].reshape(3 * C, C).astype(BF16) for di in range(3)]
    bias = vec(W_SECOND_BIAS)
    for i in range(count):
        mid[i] = convolve(shifted, i, low) + (x[i] + bias)

    mean, scale = norm_stats(count, mid, hold, same)
    for i in range(count):
        stats[i, 4:5, :] = mean[i : i + 1]
        stats[i, 5:6, :] = scale[i : i + 1]
        stats[i, 6:8, :] = jnp.zeros((2, C), F32)
    ready(STATS)
    gain3, shift3 = vec(W_ATTEND_GAIN), vec(W_ATTEND_SHIFT)

    def third(i, r):
        rows = pl.ds(r, CHUNK)
        pre = (mid[i, rows, :] - stats[i, 4:5, :]) * stats[i, 5:6, :] * gain3 + shift3
        normed[i, rows, :] = pre.astype(BF16)

    over_chunks(count, third)
    flat = normed[0:count].reshape(count * TOK, C)
    need(W_TRIPLE_WEIGHT)
    need(W_OUTPUT_WEIGHT)
    w_triple = w[W_TRIPLE_WEIGHT][...].astype(BF16)
    w_out = w[W_OUTPUT_WEIGHT][...].astype(BF16)
    for i in range(count):
        for part, name in enumerate((W_QUERY_BIAS, None, W_VALUE_BIAS)):
            v = dot(normed[i], w_triple[:, part * C : (part + 1) * C])
            if name is not None:
                v = v + vec(name)
            triple[i, :, part * C : (part + 1) * C] = v.astype(BF16)

    need(COT)
    cot_low = cot[0:count].reshape(count * TOK, C).astype(BF16)
    for i in range(count):
        dmixed[i] = dot(cot[i].astype(BF16), w_out, NT).astype(BF16)

    factor = 1.0 / math.sqrt(C)
    query_sum = jnp.zeros((1, C), F32)
    value_sum = jnp.zeros((1, C), F32)
    for i in range(count):
        q = triple[i, :, 0:C]
        k = triple[i, :, C : 2 * C]
        v = triple[i, :, 2 * C : 3 * C]
        dm = dmixed[i]
        s = dot(q, k, NT) * factor
        e = jnp.exp(s - jnp.max(s, axis=1, keepdims=True))
        p = e * (1.0 / jnp.sum(e, axis=1, keepdims=True))
        p_low = p.astype(BF16)
        mixed[i] = dot(p_low, v).astype(BF16)
        dp = dot(dm, v, NT)
        ds = (p * (dp - jnp.sum(p * dp, axis=1, keepdims=True))).astype(BF16)
        dq = dot(ds, k) * factor
        dk = dot(ds, q, TN) * factor
        dv = dot(p_low, dm, TN)
        query_sum = query_sum + jnp.sum(dq, axis=0, keepdims=True)
        value_sum = value_sum + jnp.sum(dv, axis=0, keepdims=True)
        dtriple[i, :, 0:C] = dq.astype(BF16)
        dtriple[i, :, C : 2 * C] = dk.astype(BF16)
        dtriple[i, :, 2 * C : 3 * C] = dv.astype(BF16)

    flat_mixed = mixed[0:count].reshape(count * TOK, C)
    bias = vec(W_OUTPUT_BIAS)
    for i in range(count):
        out[i] = dot(mixed[i], w_out) + (mid[i] + bias)
    ready(OUT)
    flat_d = dtriple[0:count].reshape(count * TOK, 3 * C)
    gw_out = dot(flat_mixed, cot_low, TN)
    gw_triple = dot(flat, flat_d, TN)
    if accumulate is None:
        g_out[...] = gw_out
        g_triple[...] = gw_triple
        ready(G_OUT)
        ready(G_TRIPLE)
    else:
        accumulate(gw_out, gw_triple)
    for i in range(count):
        dnormed[i] = dot(dtriple[i], w_triple, NT)

    def sums3(i, r):
        rows = pl.ds(r, CHUNK)
        d = dnormed[i, rows, :]
        unit = (mid[i, rows, :] - stats[i, 4:5, :]) * stats[i, 5:6, :]
        return d, d * unit, cot[i, rows, :]

    sum_d, sum_du, sum_cot = column_sums(count, 3, sums3, hold)
    first_mean = group_mean(sum_d * gain3, same)
    second_mean = group_mean(sum_du * gain3, same)

    def inner3(i, r):
        rows = pl.ds(r, CHUNK)
        d = dnormed[i, rows, :] * gain3
        scaled = stats[i, 5:6, :]
        unit = (mid[i, rows, :] - stats[i, 4:5, :]) * scaled
        m1 = first_mean[i : i + 1, :]
        m2 = second_mean[i : i + 1, :]
        g = (d - m1 - unit * m2) * scaled + cot[i, rows, :]
        dmid[i, rows, :] = g
        return (g,)

    (sum_mid,) = column_sums(count, 1, inner3, hold)
    ready(DMID)
    pieces = [
        jnp.sum(sum_cot, axis=0, keepdims=True), query_sum, value_sum,
        jnp.sum(sum_du, axis=0, keepdims=True), jnp.sum(sum_d, axis=0, keepdims=True),
        jnp.sum(sum_mid, axis=0, keepdims=True),
    ]
    return pieces


BIG = {
    W_FIRST_CONV: (3, 3, C, C), W_EMBED_WEIGHT: (TEMB, C), W_SECOND_CONV: (3, 3, C, C),
    W_TRIPLE_WEIGHT: (C, 3 * C), W_OUTPUT_WEIGHT: (C, C),
}
SMALL = tuple(name for name in WEIGHTS if name not in BIG)


def front_scratch(count):
    return [
        pltpu.VMEM((count, PAD, 3 * C), BF16),
        pltpu.VMEM((16, 8, C), F32),
        pltpu.VMEM((count, TOK, C), F32),
        pltpu.VMEM((count, TOK, C), BF16),
        pltpu.VMEM((count, TOK, 3 * C), BF16),
        pltpu.VMEM((count, TOK, C), BF16),
        pltpu.VMEM((count, TOK, C), BF16),
        pltpu.VMEM((count, TOK, 3 * C), BF16),
        pltpu.VMEM((count, TOK, C), F32),
        pltpu.VMEM((C, C), BF16),
    ]


def held(count):
    return [pltpu.VMEM(BIG[name], F32) for name in BIG] + [
        pltpu.VMEM((count, TOK, C), F32),
        pltpu.VMEM((count, TOK, C), F32),
        pltpu.VMEM((count, TOK, C), F32),
        pltpu.VMEM((count, TOK, C), F32),
        pltpu.VMEM((count, TOK, C), F32),
        pltpu.VMEM((count, TOK, C), BF16),
        pltpu.VMEM((count, TOK, C), BF16),
        pltpu.VMEM((count, 8, C), F32),
    ]


def small_copies(copies, small, held_small):
    for r, name in enumerate(SMALL):
        copies.start((SMALL_ONE, name), small[name], held_small.at[r])
    return {name: held_small.at[r] for r, name in enumerate(SMALL)}


HELD = tuple(BIG) + (X, COT, OUT, DMID, OUT1, ACT1, ACT2, STATS)


class Copies:
    def __init__(self, sems):
        self.sems = sems
        self.count = 0
        self.by_name = {}
        self.open = []

    def add(self, name, src, dst):
        copy = pltpu.make_async_copy(src, dst, self.sems.at[self.count])
        self.count += 1
        self.by_name[name] = copy
        return copy

    def start(self, name, src, dst):
        self.add(name, src, dst).start()
        self.open.append(name)

    def need(self, name):
        if name in self.open:
            self.open.remove(name)
            self.by_name[name].wait()

    def finish(self):
        for name in list(self.open):
            self.need(name)


def store_sums(sums, pieces, before=None):
    sums[...] = jnp.zeros((SUMS, C), F32) if before is None else before[...]
    for r, piece in enumerate(pieces):
        sums[r : r + 1, :] += piece


FRONT_SEMS = 48


def kernel_one(times, images, cotangent, *rest):
    small = dict(zip(SMALL, rest[: len(SMALL)]))
    rest = rest[len(SMALL) :]
    big = dict(zip(BIG, rest[: len(BIG)]))
    rest = rest[len(BIG) :]
    out, dmid, out1, act1, act2, stats, g_triple, g_out, sums = rest[:9]
    rest = rest[9:]
    scratch, rest = rest[:10], rest[10:]
    kept = dict(zip(HELD, rest[: len(HELD)]))
    v_triple, v_out, held_small, sems = rest[len(HELD) :]
    n = WORK - 1
    copies = Copies(sems)
    copies.start(X, images.at[0:n], kept[X])
    small = small_copies(copies, small, held_small)
    for name in (W_EMBED_WEIGHT, W_FIRST_CONV):
        copies.start(name, big[name], kept[name])
    scratch[-1][...] = group_matrix()
    moments = [times[0, 0, i].astype(F32) for i in range(n)]
    targets = {
        OUT: out.at[0:n], DMID: dmid.at[0:n], OUT1: out1.at[0:n], ACT1: act1.at[0:n], ACT2: act2.at[0:n],
        STATS: stats.at[0:n], G_TRIPLE: g_triple, G_OUT: g_out,
    }
    sources = {**kept, G_TRIPLE: v_triple, G_OUT: v_out}

    def need(name):
        if name == X:
            for first in [X, W_EMBED_WEIGHT, W_FIRST_CONV] + [(SMALL_ONE, v) for v in SMALL]:
                copies.need(first)
            for later in (W_SECOND_CONV, W_TRIPLE_WEIGHT, W_OUTPUT_WEIGHT):
                copies.start(later, big[later], kept[later])
            copies.start(COT, cotangent.at[0:n], kept[COT])
        if name == W_SECOND_CONV:
            for later in (W_SECOND_CONV, W_TRIPLE_WEIGHT, W_OUTPUT_WEIGHT, COT):
                copies.need(later)

    def ready(name):
        for v in {ACT2: (OUT1, ACT1, ACT2), DMID: (OUT, DMID, STATS, G_TRIPLE, G_OUT)}.get(name, ()):
            copies.start((TO, v), sources[v], targets[v])

    w = {**small, **{name: kept[name] for name in BIG}}
    pieces = front(
        n, kept[X], kept[COT], moments, w, kept[OUT], kept[DMID], kept[OUT1], kept[ACT1], kept[ACT2],
        kept[STATS], None, v_triple, v_out, *scratch, None, need, ready,
    )
    store_sums(sums, pieces)
    copies.finish()


ORDERS = (("xyz", "zxy"), ("yzx", "zxy"), ("yxz", "yzx"))
CHUNK_A, CHUNK_B, CHUNK_C = ORDERS[0], ORDERS[1], ORDERS[2]


def chip_bits():
    b, t = lax.axis_index(BUCKET), lax.axis_index(BATCH)
    return {"x": b % 2, "y": (b // 2) % 2, "z": (t // 2) % 2}


def owner_codes(order):
    bits = chip_bits()
    even, odd = (bits[o[0]] * 4 + bits[o[1]] * 2 + bits[o[2]] for o in order)
    return lax.axis_index(BATCH) % 2, even, odd


def scatter_unit(dst, unit, value, codes):
    core, even, odd = codes
    for block in range(16):
        half, low = divmod(block, 8)
        mine = jnp.where(core == half, 0, 1)
        code = even if half == 0 else odd
        dst[mine * 8 + (low ^ code), unit] = value[16 * block : 16 * block + 16]


def place_offset(counts, source):
    keeps = counts[0, 0] >= WORK
    return keeps, jnp.where(keeps, 0, source[0, 0] ^ lax.axis_index(BUCKET))


def kernel_two(n_bucket, times, counts, source, images, cotangent, *rest):
    arrived, rest = rest[: n_bucket - 1], rest[n_bucket - 1 :]
    small = dict(zip(SMALL, rest[: len(SMALL)]))
    rest = rest[len(SMALL) :]
    big = dict(zip(BIG, rest[: len(BIG)]))
    rest = rest[len(BIG) :]
    sums_in, gt_in, go_in, dmid_in, act2_in = rest[:5]
    rest = rest[9:]
    out, dmid, out1, act1, act2, stats, sums, give, keep, give_c, keep_c, last, notes = rest[:13]
    rest = rest[13:]
    scratch, rest = rest[:10], rest[10:]
    kept = dict(zip(HELD, rest[: len(HELD)]))
    full_act, full_shift, full_mid, blocks, blocks_c, v_triple, v_out, note, held_small, sems = rest[len(HELD) :]
    n = WORK - 1
    copies = Copies(sems)
    keeps, offset = place_offset(counts, source)

    def rows_of(k):
        return arrived[k - 1].at[0:TOK]

    choose = copies.add(X, images.at[n], kept[X].at[0])
    pl.when(keeps)(lambda: choose.start())
    pl.when(jnp.logical_not(keeps) & (offset == 0))(
        lambda: pltpu.make_async_copy(images.at[WORK], kept[X].at[0], sems.at[0]).start()
    )
    for k in range(1, n_bucket):
        pl.when(offset == k)(
            lambda k=k: pltpu.make_async_copy(rows_of(k), kept[X].at[0], sems.at[0]).start()
        )
    copies.open.append(X)
    copies.start(W_FIRST_CONV, big[W_FIRST_CONV], kept[W_FIRST_CONV])
    for k in range(1, n_bucket):
        copies.start((NOTE, k), arrived[k - 1].at[TOK : TOK + 8], note.at[k])
    small = small_copies(copies, small, held_small)
    copies.start(W_EMBED_WEIGHT, big[W_EMBED_WEIGHT], kept[W_EMBED_WEIGHT])
    same = scratch[-1]
    same[...] = group_matrix()
    codes, codes_c = owner_codes(CHUNK_A), owner_codes(CHUNK_C)
    first_wave = [X, W_EMBED_WEIGHT, W_FIRST_CONV] + [(SMALL_ONE, v) for v in SMALL]
    for name in first_wave + [(NOTE, k) for k in range(1, n_bucket)]:
        copies.need(name)
    for name in (W_SECOND_CONV, W_TRIPLE_WEIGHT, W_OUTPUT_WEIGHT):
        copies.start(name, big[name], kept[name])
    copies.start(COT, cotangent.at[n : n + 1], kept[COT])
    copies.start(GT, gt_in, v_triple)
    copies.start(GO, go_in, v_out)
    copies.start(FULL_ACT, act2_in.at[0:n], full_act.at[0:n])
    copies.start(FULL_MID, dmid_in.at[0:n], full_mid)
    moment = jnp.where(keeps, times[0, 0, n], times[0, 0, WORK]).astype(F32)
    moment = jnp.full((1, 1), moment, F32)
    for k in range(1, n_bucket):
        moment = jnp.where(offset == k, note[k, 0:1, 0:1], moment)

    lane = lax.broadcasted_iota(jnp.int32, (1, C), 1)
    clock = jnp.where(lane == n, moment, 0.0)
    for i in range(n):
        clock = jnp.where(lane == i, times[0, 0, i].astype(F32), clock)
    notes[...] = jnp.zeros(notes.shape, F32)
    notes[0:1, :] = clock
    if n_bucket == 4:
        even = codes[0] == 0
        neighbour = jnp.where(even, note[1, 0:1, 1:2], note[2, 0:1, 1:2])
        first = jnp.where(even, 1.0, 2.0)
        notes[1:2, :] = jnp.broadcast_to(jnp.where(neighbour == 3.0, 1.0, 0.0), (1, C))
        notes[2:3, :] = jnp.broadcast_to(jnp.where(neighbour == first, 1.0, 0.0), (1, C))

    def accumulate(gw_out, gw_triple):
        scatter_unit(blocks_c, 3, gw_out + v_out[...], codes_c)
        total = gw_triple + v_triple[...]
        for part in range(3):
            scatter_unit(blocks_c, part, total[:, part * C : (part + 1) * C], codes_c)

    targets = {
        OUT: out.at[n:WORK], DMID: dmid.at[n:WORK], OUT1: out1.at[n:WORK], ACT1: act1.at[n:WORK],
        ACT2: act2.at[n:WORK], STATS: stats.at[n:WORK],
    }
    def need(name):
        if name == W_SECOND_CONV:
            for later in (W_SECOND_CONV, W_TRIPLE_WEIGHT, W_OUTPUT_WEIGHT, COT, GT, GO, FULL_ACT, FULL_MID):
                copies.need(later)

    def ready(name):
        if name == DMID:
            for v in targets:
                copies.start((TO, v), kept[v], targets[v])
            copies.start((TO, LAST), kept[X].at[0], last)
            copies.start((TO, GIVE_C), blocks_c.at[8:16], give_c)
            copies.start((TO, KEEP_C), blocks_c.at[0:8], keep_c)

    w = {**small, **{name: kept[name] for name in BIG}}
    pieces = front(
        1, kept[X], kept[COT], [moment], w, kept[OUT], kept[DMID], kept[OUT1], kept[ACT1], kept[ACT2],
        kept[STATS], None, None, None, *scratch, accumulate, need, ready,
    )
    store_sums(sums, pieces, sums_in)

    clear_borders(full_shift, WORK)

    def early(i, r):
        store_shifted(full_shift, i, r, full_mid[i, pl.ds(r, CHUNK), :], True)

    def late(i, r):
        store_shifted(full_shift, i + n, r, kept[DMID][i, pl.ds(r, CHUNK), :], True)

    over_chunks(n, early)
    over_chunks(1, late)
    full_act[n] = kept[ACT2][0]
    act = full_act[...].reshape(WORK * TOK, C)
    for di in range(3):
        g = dot(act, window(full_shift, WORK, 2 - di), TN)
        for dj in range(3):
            scatter_unit(blocks, di * 3 + dj, g[:, dj * C : (dj + 1) * C], codes)
    copies.start((TO, GIVE), blocks.at[8:16], give)
    copies.start((TO, KEEP), blocks.at[0:8], keep)
    copies.finish()


def swish_norm_backward(dact, values, base, stats, row, gain, shift, hold, same, dpre, write):
    def sums_of(i, r):
        rows = pl.ds(r, CHUNK)
        unit = (base[i, rows, :] - stats[i, row : row + 1, :]) * stats[i, row + 1 : row + 2, :]
        pre = unit * gain + shift
        s = sigmoid(pre)
        d = dact[i, rows, :] * (s * (1.0 + pre * (1.0 - s)))
        dpre[i, rows, :] = d
        return d, d * unit

    sum_d, sum_du = column_sums(WORK, 2, sums_of, hold)
    first_mean = group_mean(sum_d * gain, same)
    second_mean = group_mean(sum_du * gain, same)

    def inner(i, r):
        rows = pl.ds(r, CHUNK)
        scaled = stats[i, row + 1 : row + 2, :]
        unit = (base[i, rows, :] - stats[i, row : row + 1, :]) * scaled
        m1 = first_mean[i : i + 1, :]
        m2 = second_mean[i : i + 1, :]
        return write(i, r, (dpre[i, rows, :] * gain - m1 - unit * m2) * scaled)

    sums = column_sums(WORK, 1, inner, hold)[0]
    return sum_d, sum_du, sums


def conv_backward(shifted, kernel, dact):
    low = [jnp.concatenate([kernel[di, dj].astype(BF16) for dj in range(3)], axis=1) for di in range(3)]
    for i in range(WORK):
        total = None
        for di in range(3):
            part = dot(shifted[i, SIDE * (2 - di) : SIDE * (2 - di) + TOK, :], low[di], NT)
            total = part if total is None else total + part
        dact[i] = total


def kernel_three(notes, dmid_in, out1_in, act1_in, stats, sums_in, kernel_in, gain_ref, shift_ref,
                 give, keep, low, sums, rows_out,
                 shifted, hold, dact, dpre, same_ref, dmid, out1, act1, kernel, blocks, v_low, v_small, sems):
    copies = Copies(sems)
    copies.start(GAIN, gain_ref, v_small.at[0])
    copies.start(SHIFT, shift_ref, v_small.at[1])
    gain_ref, shift_ref = v_small.at[0], v_small.at[1]
    copies.start(DMID, dmid_in, dmid)
    copies.start(KERNEL, kernel_in, kernel)
    copies.start(OUT1, out1_in, out1)
    copies.start(ACT1, act1_in, act1)
    same_ref[...] = group_matrix()
    same = same_ref[...]
    codes = owner_codes(CHUNK_B)
    clear_borders(shifted, WORK)
    copies.need(DMID)

    def load(i, r):
        store_shifted(shifted, i, r, dmid[i, pl.ds(r, CHUNK), :], True)

    over_chunks(WORK, load)
    copies.need(KERNEL)
    conv_backward(shifted, kernel, dact)
    for name in (OUT1, ACT1, GAIN, SHIFT):
        copies.need(name)

    def write(i, r, g):
        v_low[i, pl.ds(r, CHUNK), :] = g.astype(BF16)
        store_shifted(shifted, i, r, g, True)
        return (g,)

    sum_d, sum_du, sum_first = swish_norm_backward(
        dact, None, out1, stats, 2, gain_ref[...], shift_ref[...], hold, same, dpre, write
    )
    copies.start((TO, LOW), v_low, low)

    def tap(di, carry):
        rows = pl.ds(pl.multiple_of(SIDE * (2 - di), SIDE), TOK)
        g = dot(act1[...].reshape(WORK * TOK, C), shifted[:, rows, :].reshape(WORK * TOK, 3 * C), TN)
        for dj in range(3):
            scatter_unit(blocks, di * 3 + dj, g[:, dj * C : (dj + 1) * C], codes)
        return carry

    lax.fori_loop(0, 3, tap, 0)
    copies.start((TO, GIVE), blocks.at[8:16], give)
    copies.start((TO, KEEP), blocks.at[0:8], keep)
    sums[...] = sums_in[...]
    sums[R_SEC_GAIN : R_SEC_GAIN + 1, :] = jnp.sum(sum_du, axis=0, keepdims=True)
    sums[R_SEC_SHIFT : R_SEC_SHIFT + 1, :] = jnp.sum(sum_d, axis=0, keepdims=True)
    sums[R_EMB_BIAS : R_EMB_BIAS + 1, :] = jnp.sum(sum_first, axis=0, keepdims=True)
    core = lax.axis_index(BATCH) % 2
    place = chip_place() * 2 + core
    spots = lax.broadcasted_iota(jnp.int32, (4, C), 0) * C + lax.broadcasted_iota(jnp.int32, (4, C), 1)
    clocks = jnp.zeros((4, C), F32)
    for i in range(WORK):
        clocks = jnp.where(spots == place * WORK + i, notes[0:1, i : i + 1], clocks)
    sums[R_CLOCKS : R_CLOCKS + 4, :] = clocks
    four = sum_first[0:WORK]
    both = jnp.concatenate([four, four], axis=0)
    half = lax.broadcasted_iota(jnp.int32, (8, C), 0) // WORK
    rows_out[...] = jnp.where(half == core, both, 0.0)
    copies.finish()


def kernel_four(n_bucket, counts, source, images, last, dmid_in, low_in, stats, sums_in, rows_in, kernel_in, gain_ref, shift_ref,
                grad, back, sums,
                shifted, hold, dact, dpre, same_ref, dmid, base, low, kernel, v_back, v_small, sems):
    n = WORK - 1
    copies = Copies(sems)
    copies.start(GAIN, gain_ref, v_small.at[0])
    copies.start(SHIFT, shift_ref, v_small.at[1])
    gain_ref, shift_ref = v_small.at[0], v_small.at[1]
    copies.start(LOW, low_in, low)
    copies.start(KERNEL, kernel_in, kernel)
    copies.start(BASE, images.at[0:n], base.at[0:n])
    copies.start(LAST, last, base.at[n])
    copies.start(DMID, dmid_in, dmid)
    same_ref[...] = group_matrix()
    same = same_ref[...]
    clear_borders(shifted, WORK)
    copies.need(LOW)

    def load(i, r):
        store_shifted(shifted, i, r, low[i, pl.ds(r, CHUNK), :].astype(F32), True)

    over_chunks(WORK, load)
    copies.need(KERNEL)
    conv_backward(shifted, kernel, dact)
    for name in (BASE, LAST, DMID, GAIN, SHIFT):
        copies.need(name)

    def write(i, r, g):
        rows = pl.ds(r, CHUNK)
        dpre[i, rows, :] = g + dmid[i, rows, :]
        return (g,)

    sum_d, sum_du, _ = swish_norm_backward(
        dact, None, base, stats, 0, gain_ref[...], shift_ref[...], hold, same, dpre, write
    )
    copies.start((TO, GRAD), dpre.at[0:n], grad.at[0:n])
    keeps, offset = place_offset(counts, source)
    if n_bucket == 4:
        even = lax.axis_index(BATCH) % 2 == 0
        first = jnp.where(even, 1, 2)
        v_back[0] = jnp.where((offset & first) != 0, dpre[n], 0.0)
        v_back[1] = jnp.where(offset == 3 - first, dpre[n], 0.0)
    else:
        for k in range(1, n_bucket):
            v_back[k - 1] = jnp.where(offset == k, dpre[n], 0.0)
    copies.start((TO, BACK), v_back, back)
    dmid[n] = jnp.where(keeps, dpre[n], 0.0)
    copies.start((TO, SLOT), dmid.at[n], grad.at[n])
    sums[0:SUMS] = sums_in[...]
    sums[SUMS : SUMS + 8] = rows_in[...]
    sums[R_FIRST_GAIN : R_FIRST_GAIN + 1, :] = jnp.sum(sum_du, axis=0, keepdims=True)
    sums[R_FIRST_SHIFT : R_FIRST_SHIFT + 1, :] = jnp.sum(sum_d, axis=0, keepdims=True)
    copies.finish()


def kernel_pack(times, counts, source, images, out, sem):
    copy = pltpu.make_async_copy(images.at[WORK], out.at[0:TOK], sem)
    copy.start()
    _, offset = place_offset(counts, source)
    lane = lax.broadcasted_iota(jnp.int32, (8, C), 1)
    moment = times[0, 0, WORK].astype(F32)
    out[TOK : TOK + 8] = jnp.where(lane == 0, moment, jnp.where(lane == 1, offset.astype(F32), 0.0))
    copy.wait()


def whole(shape):
    return pl.BlockSpec(shape, lambda *_: (0,) * len(shape), memory_space=pltpu.VMEM)


def part(shape, first):
    return pl.BlockSpec(shape, lambda *_: (first,) + (0,) * (len(shape) - 1), memory_space=pltpu.VMEM)


SMEM = pl.BlockSpec(memory_space=pltpu.SMEM)
ANY = pl.BlockSpec(memory_space=pl.ANY)
HBM = pl.BlockSpec(memory_space=pltpu.HBM)


def params(mebibytes=26):
    return pltpu.CompilerParams(vmem_limit_bytes=mebibytes * 1024 * 1024)


def shape(dims, dtype=F32):
    return jax.ShapeDtypeStruct(dims, dtype)


def weight_specs(w):
    return [whole(w[name].shape) for name in WEIGHTS]


def call_pack(timesteps, counts, source, images):
    return pl.pallas_call(
        kernel_pack,
        name="pack_spare",
        in_specs=[SMEM, SMEM, SMEM, ANY],
        out_specs=pl.BlockSpec(memory_space=pltpu.VMEM),
        out_shape=shape((TOK + 8, C)),
        scratch_shapes=[pltpu.SemaphoreType.DMA],
        cost_estimate=pl.CostEstimate(flops=20_000_000_000, bytes_accessed=1_000_000, transcendentals=0),
        compiler_params=params(),
    )(timesteps, counts, source, images)


VMEM = pl.BlockSpec(memory_space=pltpu.VMEM)
IMAGE_ARRAYS = (
    ((WORK, TOK, C), F32), ((WORK, TOK, C), F32), ((WORK, TOK, C), F32), ((WORK, TOK, C), BF16), ((WORK, TOK, C), BF16),
    ((WORK, 8, C), F32),
)


def call_one(timesteps, images, cot, w):
    n = WORK - 1
    return pl.pallas_call(
        kernel_one,
        name="front_of_own_images",
        in_specs=[SMEM, HBM, HBM] + [HBM] * (len(SMALL) + len(BIG)),
        out_specs=[ANY] * 8 + [VMEM],
        out_shape=[shape(*s) for s in IMAGE_ARRAYS] + [shape((C, 3 * C)), shape((C, C)), shape((SUMS, C))],
        scratch_shapes=front_scratch(n) + held(n)
        + [pltpu.VMEM((C, 3 * C), F32), pltpu.VMEM((C, C), F32), pltpu.VMEM((len(SMALL), 1, C), F32),
           pltpu.SemaphoreType.DMA((FRONT_SEMS,))],
        cost_estimate=pl.CostEstimate(flops=20_000_000_000, bytes_accessed=1_000_000, transcendentals=0),
        compiler_params=params(),
    )(timesteps, images, cot, *[w[name] for name in SMALL], *[w[name] for name in BIG])


def call_two(timesteps, counts, source, images, cot, arrived, w, early):
    out, dmid, out1, act1, act2, stats, g_triple, g_out, sums = early
    n_bucket = len(arrived) + 1
    first = 5 + len(arrived) + len(SMALL) + len(BIG)
    half, half_c = (8, 9, 16, C), (8, 4, 16, C)
    return pl.pallas_call(
        lambda *refs: kernel_two(n_bucket, *refs),
        name="front_of_last_image",
        in_specs=[SMEM, SMEM, SMEM, HBM, HBM] + [ANY] * len(arrived) + [HBM] * (len(SMALL) + len(BIG))
        + [VMEM] + [ANY] * 8,
        out_specs=[ANY] * 6 + [VMEM] + [ANY] * 5 + [VMEM],
        out_shape=[shape(*s) for s in IMAGE_ARRAYS]
        + [shape((SUMS, C)), shape(half), shape(half), shape(half_c), shape(half_c), shape((TOK, C)), shape((8, C))],
        scratch_shapes=front_scratch(1) + held(1)
        + [
            pltpu.VMEM((WORK, TOK, C), BF16), pltpu.VMEM((WORK, PAD, 3 * C), BF16), pltpu.VMEM((WORK - 1, TOK, C), F32),
            pltpu.VMEM((16, 9, 16, C), F32), pltpu.VMEM((16, 4, 16, C), F32), pltpu.VMEM((C, 3 * C), F32), pltpu.VMEM((C, C), F32),
            pltpu.VMEM((n_bucket, 8, C), F32), pltpu.VMEM((len(SMALL), 1, C), F32),
            pltpu.SemaphoreType.DMA((FRONT_SEMS + n_bucket,)),
        ],
        input_output_aliases={first + 5: 0, first + 3: 1, first + 6: 2, first + 7: 3, first + 4: 4, first + 8: 5},
        cost_estimate=pl.CostEstimate(flops=20_000_000_000, bytes_accessed=1_000_000, transcendentals=0),
        compiler_params=params(),
    )(
        timesteps, counts, source, images, cot, *arrived, *[w[name] for name in SMALL], *[w[name] for name in BIG],
        sums, g_triple, g_out, dmid, act2, out, out1, act1, stats,
    )


def back_scratch():
    return [
        pltpu.VMEM((WORK, PAD, 3 * C), BF16),
        pltpu.VMEM((16, 8, C), F32),
        pltpu.VMEM((WORK, TOK, C), F32),
        pltpu.VMEM((WORK, TOK, C), F32),
        pltpu.VMEM((C, C), BF16),
    ]


def call_three(notes, dmid, out1, act1, stats, sums, w):
    full = (WORK, TOK, C)
    half = (8, 9, 16, C)
    return pl.pallas_call(
        kernel_three,
        name="back_to_first_out",
        in_specs=[VMEM, ANY, ANY, ANY, VMEM, VMEM, HBM, HBM, HBM],
        out_specs=[ANY, ANY, ANY, VMEM, VMEM],
        out_shape=[shape(half), shape(half), shape(full, BF16), shape((SUMS, C)), shape((8, C))],
        scratch_shapes=back_scratch()
        + [
            pltpu.VMEM(full, F32), pltpu.VMEM(full, F32), pltpu.VMEM(full, BF16), pltpu.VMEM((3, 3, C, C), F32),
            pltpu.VMEM((16, 9, 16, C), F32), pltpu.VMEM(full, BF16), pltpu.VMEM((2, 1, C), F32),
            pltpu.SemaphoreType.DMA((12,)),
        ],
        compiler_params=params(),
    )(notes, dmid, out1, act1, stats, sums, w[W_SECOND_CONV], w[W_SECOND_GAIN], w[W_SECOND_SHIFT])


def call_four(n_bucket, counts, source, images, last, dmid, low, stats, sums, rows, w):
    full = (WORK, TOK, C)
    backs = 2 if n_bucket == 4 else n_bucket - 1
    return pl.pallas_call(
        lambda *refs: kernel_four(n_bucket, *refs),
        name="back_to_images",
        in_specs=[SMEM, SMEM, HBM, ANY, ANY, ANY, VMEM, VMEM, VMEM, HBM, HBM, HBM],
        out_specs=[ANY, ANY, VMEM],
        out_shape=[shape((WORK + 1, TOK, C)), shape((backs, TOK, C)), shape((SUMS + 8, C))],
        scratch_shapes=back_scratch()
        + [
            pltpu.VMEM(full, F32), pltpu.VMEM(full, F32), pltpu.VMEM(full, BF16), pltpu.VMEM((3, 3, C, C), F32),
            pltpu.VMEM((backs, TOK, C), F32), pltpu.VMEM((2, 1, C), F32), pltpu.SemaphoreType.DMA((12,)),
        ],
        compiler_params=params(),
    )(counts, source, images, last, dmid, low, stats, sums, rows, w[W_FIRST_CONV], w[W_FIRST_GAIN], w[W_FIRST_SHIFT])


def assemble_kernel(orders, *refs):
    outs = list(refs[2 * len(orders) : -1])
    copies = Copies(refs[-1])
    for n, order in enumerate(orders):
        core, even, odd = owner_codes(order)
        target = outs.pop(0)
        units = refs[2 * n].shape[1]
        beside = outs.pop(0) if units == 4 else None
        for half in range(2):
            src = refs[2 * n + half]
            holder = core if half == 0 else 1 - core
            code = jnp.where(holder == 0, even, odd)
            for low in range(8):
                block = holder * 8 + (low ^ code)
                rows = pl.ds(pl.multiple_of(block * 16, 16), 16)
                if units == 9:
                    copies.start((n, half, low), src.at[low], target.at[:, rows, :])
                    continue
                for p in range(3):
                    copies.start((n, half, low, p), src.at[low, p], target.at[rows, p * C : (p + 1) * C])
                copies.start((n, half, low), src.at[low, 3], beside.at[rows, :])
    copies.finish()


def assemble(orders, *halves):
    out_shape = []
    for own in halves[::2]:
        out_shape += [shape((9, C, C))] if own.shape[1] == 9 else [shape((C, 3 * C)), shape((C, C))]
    return pl.pallas_call(
        lambda *refs: assemble_kernel(orders, *refs),
        name="assemble",
        in_specs=[ANY] * len(halves),
        out_specs=[ANY] * len(out_shape),
        out_shape=out_shape,
        scratch_shapes=[pltpu.SemaphoreType.DMA((16 + 16 * 4,))],
        cost_estimate=pl.CostEstimate(flops=1, bytes_accessed=1, transcendentals=0),
        compiler_params=params(2),
    )(*halves)


def high_code():
    b, t = lax.axis_index(BUCKET), lax.axis_index(BATCH)
    return (t // 4) * (lax.axis_size(BUCKET) // 4) + b // 4


def chip_place():
    bits = chip_bits()
    many = lax.axis_size(BUCKET) * lax.axis_size(BATCH) // 16
    return (bits["x"] * 4 + bits["y"] * 2 + bits["z"]) * many + high_code()


def embed_kernel(devices, order, gathered, sums, out, rows):
    core = lax.axis_index(BATCH) % 2
    bits = chip_bits()
    mine = bits["x"] * 4 + bits["y"] * 2 + bits["z"]
    high = high_code()
    many = devices // 16
    weight = {"x": 4, "y": 2, "z": 1}
    for place in range(devices // 2):
        rest, code = place % many, place // many
        turned = [
            sum(((code >> (2 - n)) & 1) * weight[o[n]] for n in range(3)) for o in order
        ]
        code = jnp.where(core == 0, turned[0], turned[1]) ^ mine
        rows[code * many + (rest ^ high)] = gathered[place]
    count = WORK * devices
    grads = rows[...].reshape(count, C)
    half = TEMB // 2
    moments = []
    for n in range(0, count, C):
        size = min(C, count)
        row = lax.broadcasted_iota(jnp.int32, (size, C), 0)
        lane = lax.broadcasted_iota(jnp.int32, (size, C), 1)
        clocks = sums[R_CLOCKS + n // C : R_CLOCKS + n // C + 1, :]
        moments.append(jnp.sum(jnp.where(row == lane, clocks, 0.0), axis=1, keepdims=True))
    moments = jnp.concatenate(moments, axis=0) if len(moments) > 1 else moments[0]
    frequency = jnp.exp(
        lax.broadcasted_iota(jnp.int32, (count, half), 1).astype(F32) * (-math.log(10000.0) / (half - 1))
    )
    angles = moments * frequency
    waves = jnp.concatenate([jnp.sin(angles), jnp.cos(angles)], axis=1)
    waves = waves * sigmoid(waves)
    out[...] = lax.dot_general(waves, grads, TN, precision=lax.Precision.HIGHEST, preferred_element_type=F32)


def embed_gradient(devices, order, gathered, sums):
    return pl.pallas_call(
        lambda *refs: embed_kernel(devices, order, *refs),
        name="embed_gradient",
        in_specs=[VMEM, VMEM],
        out_specs=VMEM,
        out_shape=shape((TEMB, C)),
        scratch_shapes=[pltpu.VMEM((devices // 2, 8, C), F32)],
        cost_estimate=pl.CostEstimate(flops=1, bytes_accessed=1, transcendentals=0),
        compiler_params=params(),
    )(gathered, sums)


AXES = (BUCKET, BATCH)


def solution(mesh):
    n_bucket, n_batch = mesh.shape[BUCKET], mesh.shape[BATCH]
    devices = n_bucket * n_batch

    def flips(fn):
        pairs = []
        for b in range(n_bucket):
            for t in range(n_batch):
                nb, nt = fn(b, t)
                pairs.append((b * n_batch + t, nb * n_batch + nt))
        return pairs

    def by_core(even, odd):
        def fn(b, t):
            kind, bit = even if t % 2 == 0 else odd
            return (b ^ bit, t) if kind == 0 else (b, t ^ bit)

        return flips(fn)

    x, y, z = (0, 1), (0, 2), (1, 2)
    core_perm = flips(lambda b, t: (b, t ^ 1))
    links = {"x": x, "y": y, "z": z}
    rest = []
    bit = 4
    while bit < n_bucket:
        rest.append((0, bit))
        bit *= 2
    bit = 4
    while bit < n_batch:
        rest.append((1, bit))
        bit *= 2
    rest_perms = [by_core(s, s) for s in rest]
    bucket_perms = [flips(lambda b, t, k=k: (b ^ k, t)) for k in range(1, n_bucket)]

    def send(v, perm):
        return lax.ppermute(v, AXES, perm)

    def after(v, *others):
        return lax.optimization_barrier((v,) + others)[0]

    def held_by(v, other):
        row = other.reshape(-1, C)[0:1]
        return v + 0.0 * row.reshape((1,) * (v.ndim - 1) + (C,))

    class Chunk:
        def __init__(self, order, give, keep, units):
            self.perms = [by_core(links[p], links[q]) for p, q in zip(*order)]
            self.rows = units * 16
            self.stage = 0
            self.size = give.shape
            self.keep = keep.reshape(2, 2, 2, self.rows, C)
            self.got = send(give, core_perm).reshape(2, 2, 2, self.rows, C)
            self.extra = None

        def step(self, *deps, late=None):
            n_rest = len(rest_perms)
            k = self.stage
            self.stage += 1
            if k < 3:
                out, self.keep = self.keep[1] + self.got[1], self.keep[0] + self.got[0]
                perm = self.perms[k]
            else:
                self.take()
                if k < 3 + n_rest:
                    perm = rest_perms[k - 3]
                else:
                    if k == 3 + n_rest:
                        self.keep = self.keep[None]
                    j = k - 3 - n_rest
                    perm = self.perms[2 - j] if j < 3 else core_perm
                out = self.keep
                if self.extra is not None and perm is not core_perm:
                    sums, rows = self.extra
                    out = jnp.concatenate([out.reshape(-1, C), sums, rows.reshape(-1, C)], axis=0)
            if late is not None:
                out = held_by(out, late)
            out = after(out, *deps)
            self.got = send(out, perm)
            return out

        def take(self):
            n_rest = len(rest_perms)
            k = self.stage - 1
            got = self.got
            if k == 3:
                self.keep = self.keep + got
                return
            if self.extra is not None:
                sums, rows = self.extra
                size = self.keep.size // C
                rows = jnp.concatenate([rows, got[size + SUMS :].reshape(rows.shape)], axis=0)
                self.extra = sums + got[size : size + SUMS], rows
                got = got[:size]
            got = got.reshape(self.keep.shape)
            if k <= 3 + n_rest:
                self.keep = self.keep + got
            else:
                self.keep = jnp.concatenate([self.keep, got], axis=0)

        def halves(self):
            dims = (8, self.rows // 16, 16, C)
            return self.keep.reshape(dims), self.got.reshape(dims)

    def shards(images, timesteps, counts, source, cotangent, *weights):
        w = dict(zip(WEIGHTS, weights))
        w = {k: v.reshape(1, C) if v.ndim == 1 else v for k, v in w.items()}
        slots = images[0, 0]
        cot = cotangent[0, 0]

        spare = call_pack(timesteps, counts, source, slots)
        arrived = [send(spare, p) for p in bucket_perms]
        early = call_one(timesteps, slots, cot, w)
        out, dmid, out1, act1, act2, stats, sums, give_a, keep_a, give_c, keep_c, last, notes = call_two(
            timesteps, counts, source, slots, cot, arrived, w, early
        )
        chunk_a = Chunk(CHUNK_A, give_a, keep_a, 9)
        chunk_c = Chunk(CHUNK_C, give_c, keep_c, 4)
        give_b, keep_b, low, sums, rows = call_three(notes, dmid, out1, act1, stats, sums, w)
        chunk_b = Chunk(CHUNK_B, give_b, keep_b, 9)

        tie = chunk_a.step()
        tie = chunk_c.step(tie)
        tie = chunk_b.step(tie)
        grad, back, extra = call_four(n_bucket, counts, source, slots, last, dmid, after(low, tie), stats, sums, rows, w)
        extra = extra + send(extra, core_perm)
        total = 3 + len(rest_perms) + 3
        home = None
        for k in range(1, total):
            if k == 3:
                chunk_c.extra = extra[:SUMS], extra[None, SUMS:]
            tie = chunk_a.step(tie)
            tie = chunk_c.step(tie)
            tie = chunk_b.step(tie, late=home if k == 5 else None)
            if n_bucket == 4:
                if k == 2:
                    hop = send(after(back[0], tie), by_core(x, y))
                if k == 3:
                    turn = after(jnp.where(notes[1:2] != 0.0, hop, back[1]), tie)
                    got = send(turn, by_core(y, x))
                if k == 4:
                    home = jnp.where(notes[2:3] != 0.0, hop, got)
                    grad = lax.dynamic_update_slice(grad, home[None], (WORK, 0, 0))
            elif k == 1:
                home = send(back[0], bucket_perms[0])
                for n in range(2, n_bucket):
                    home = home + send(back[n - 1], bucket_perms[n - 1])
                grad = lax.dynamic_update_slice(grad, home[None], (WORK, 0, 0))
        tie = chunk_c.step(tie)
        tie = chunk_a.step(tie)
        sums, rows = chunk_c.extra
        g_embed = embed_gradient(devices, CHUNK_C, rows, sums)
        tie = chunk_b.step(tie, late=g_embed)
        (g_second,) = assemble((CHUNK_A,), *chunk_a.halves())
        g_triple, g_out, g_first = assemble((CHUNK_C, CHUNK_B), *chunk_c.halves(), *chunk_b.halves())

        def vec(r):
            return sums[r]

        return (
            out[None, None], grad[None, None],
            vec(R_FIRST_GAIN), vec(R_FIRST_SHIFT), g_first.reshape(3, 3, C, C), g_embed, vec(R_EMB_BIAS),
            vec(R_SEC_GAIN), vec(R_SEC_SHIFT), g_second.reshape(3, 3, C, C), vec(R_SEC_BIAS),
            vec(R_ATT_GAIN), vec(R_ATT_SHIFT), g_triple, vec(R_QUERY_BIAS), vec(R_VALUE_BIAS),
            g_out, vec(R_OUT_BIAS),
        )

    placed = (
        P(BATCH, BUCKET, None, None, None), P(BATCH, BUCKET, None), P(BATCH, BUCKET),
        P(BATCH, BUCKET), P(BATCH, BUCKET, None, None, None),
    ) + (P(),) * 16
    return jax.shard_map(
        shards,
        mesh=mesh,
        in_specs=placed,
        out_specs=(P(BATCH, BUCKET, None, None, None),) * 2 + (P(),) * 16,
        check_vma=False,
    )
```

```python
import math

import jax
import jax.numpy as jnp
from jax import lax
from jax.experimental import pallas as pl
from jax.experimental.pallas import tpu as pltpu
from jax.sharding import PartitionSpec as P

TEMB = 512
GROUPS = 32
SIDE = 16
WORK = 4
TOK = SIDE * SIDE
C = 256
PAD = TOK + 2 * SIDE
EPSILON = 1e-06
COUNT = float(TOK * (C // GROUPS))
CHUNK = 64
F32 = jnp.float32
BATCH, BUCKET = "batch", "bucket"
BF16 = jnp.bfloat16
NT = (((1,), (1,)), ((), ()))
TN = (((0,), (0,)), ((), ()))

R_OUT_BIAS, R_QUERY_BIAS, R_VALUE_BIAS, R_ATT_GAIN, R_ATT_SHIFT, R_SEC_BIAS = 0, 1, 2, 3, 4, 5
R_SEC_GAIN, R_SEC_SHIFT, R_EMB_BIAS, R_FIRST_GAIN, R_FIRST_SHIFT, R_CLOCKS = 6, 7, 8, 9, 10, 11
SUMS = 16


(W_FIRST_GAIN, W_FIRST_SHIFT, W_FIRST_CONV, W_EMBED_WEIGHT, W_EMBED_BIAS, W_SECOND_GAIN, W_SECOND_SHIFT, W_SECOND_CONV,
    W_SECOND_BIAS, W_ATTEND_GAIN, W_ATTEND_SHIFT, W_TRIPLE_WEIGHT, W_QUERY_BIAS, W_VALUE_BIAS, W_OUTPUT_WEIGHT,
    W_OUTPUT_BIAS) = WEIGHTS = range(16)
(X, COT, OUT, DMID, OUT1, ACT1, ACT2, STATS, G_TRIPLE, G_OUT, GT, GO, FULL_ACT, FULL_MID, KERNEL, GAIN, SHIFT, BASE,
    LAST, LOW, GIVE, KEEP, GIVE_C, KEEP_C, GRAD, BACK, SLOT, TO, NOTE, SMALL_ONE) = range(16, 46)


def dot(a, b, dims=(((1,), (0,)), ((), ()))):
    return lax.dot_general(a, b, dims, preferred_element_type=F32)


def sigmoid(v):
    return 0.5 * jnp.tanh(0.5 * v) + 0.5


def group_matrix():
    row = lax.broadcasted_iota(jnp.int32, (C, C), 0) // (C // GROUPS)
    col = lax.broadcasted_iota(jnp.int32, (C, C), 1) // (C // GROUPS)
    return (row == col).astype(F32).astype(BF16)


def group_mean(sums, same):
    high = sums.astype(BF16).astype(F32)
    rest = sums - high
    mid = rest.astype(BF16).astype(F32)
    low = rest - mid
    total = dot(jnp.concatenate([high, mid, low], axis=0).astype(BF16), same)
    return (total[0:8] + total[8:16] + total[16:24]) * (1.0 / COUNT)


def over_chunks(count, body):
    for image in range(count):
        for row in range(0, TOK, CHUNK):
            body(image, row)


def fold(v):
    return jnp.sum(v.reshape(v.shape[0] // 8, 8, v.shape[1]), axis=0)


def column_sums(count, parts, body, hold):
    out = [[] for _ in range(parts)]
    for image in range(count):
        totals = [None] * parts
        for row in range(0, TOK, CHUNK):
            for part, v in enumerate(body(image, row)):
                f = fold(v)
                totals[part] = f if totals[part] is None else totals[part] + f
        for part in range(parts):
            out[part].append(jnp.sum(totals[part], axis=0, keepdims=True))
    return [jnp.concatenate(rows + [jnp.zeros((8 - count, C), F32)], axis=0) for rows in out]


def edge_masks():
    column = lax.broadcasted_iota(jnp.int32, (CHUNK, C), 0) % SIDE
    return column == 0, column == SIDE - 1


def store_shifted(ref, image, row, v, backward):
    first, last = edge_masks()
    before = jnp.where(first, 0.0, pltpu.roll(v, 1, 0)).astype(BF16)
    after = jnp.where(last, 0.0, pltpu.roll(v, CHUNK - 1, 0)).astype(BF16)
    rows = pl.ds(row + SIDE, CHUNK)
    left, right = (after, before) if backward else (before, after)
    ref[image, rows, 0:C] = left
    ref[image, rows, C : 2 * C] = v.astype(BF16)
    ref[image, rows, 2 * C : 3 * C] = right


def clear_borders(ref, count):
    for i in range(count):
        ref[i, 0:SIDE, :] = jnp.zeros((SIDE, 3 * C), BF16)
        ref[i, PAD - SIDE : PAD, :] = jnp.zeros((SIDE, 3 * C), BF16)


def window(ref, count, di):
    return ref[0:count, SIDE * di : SIDE * di + TOK, :].reshape(count * TOK, 3 * C)


def convolve(shifted, image, kernel):
    total = None
    for di in range(3):
        part = dot(shifted[image, SIDE * di : SIDE * di + TOK, :], kernel[di])
        total = part if total is None else total + part
    return total


def norm_stats(count, ref, hold, same):
    (sums,) = column_sums(count, 1, lambda i, r: (ref[i, pl.ds(r, CHUNK), :],), hold)
    return sums_to_stats(count, sums, ref, hold, same)


def sums_to_stats(count, sums, ref, hold, same):
    mean = group_mean(sums, same)

    def squares(i, r):
        d = ref[i, pl.ds(r, CHUNK), :] - mean[i : i + 1, :]
        return (d * d,)

    (second,) = column_sums(count, 1, squares, hold)
    return mean, lax.rsqrt(group_mean(second, same) + EPSILON)


def front(
    count, x, cot, times, w, out, dmid, out1, act1, act2, stats, sums, g_triple, g_out,
    shifted, hold, mid, normed, triple, mixed, dmixed, dtriple, dnormed, same_ref, accumulate, need, ready,
):
    same = same_ref[...]

    def vec(name):
        return w[name][...]

    need(X)
    mean, scale = norm_stats(count, x, hold, same)
    for i in range(count):
        stats[i, 0:1, :] = mean[i : i + 1]
        stats[i, 1:2, :] = scale[i : i + 1]
    clear_borders(shifted, count)
    gain, shift = vec(W_FIRST_GAIN), vec(W_FIRST_SHIFT)

    def first(i, r):
        rows = pl.ds(r, CHUNK)
        pre = (x[i, rows, :] - stats[i, 0:1, :]) * stats[i, 1:2, :] * gain + shift
        act = pre * sigmoid(pre)
        act1[i, rows, :] = act.astype(BF16)
        store_shifted(shifted, i, r, act, False)

    over_chunks(count, first)
    ready(ACT1)

    half = TEMB // 2
    lane = lax.broadcasted_iota(jnp.int32, (8, half), 1).astype(F32)
    row = lax.broadcasted_iota(jnp.int32, (8, half), 0)
    frequency = jnp.exp(lane * (-math.log(10000.0) / (half - 1)))
    clock = jnp.zeros((8, half), F32)
    for i in range(count):
        clock = jnp.where(row == i, times[i], clock)
    angles = clock * frequency
    waves = jnp.concatenate([jnp.sin(angles), jnp.cos(angles)], axis=1)
    waves = waves * sigmoid(waves)
    need(W_EMBED_WEIGHT)
    stepped = lax.dot_general(
        waves, w[W_EMBED_WEIGHT][...], (((1,), (0,)), ((), ())),
        precision=lax.Precision.HIGHEST, preferred_element_type=F32,
    ) + vec(W_EMBED_BIAS)

    need(W_FIRST_CONV)
    kernel = w[W_FIRST_CONV]
    low = [kernel[di].reshape(3 * C, C).astype(BF16) for di in range(3)]
    for i in range(count):
        out1[i] = convolve(shifted, i, low) + stepped[i : i + 1]
    ready(OUT1)

    mean, scale = norm_stats(count, out1, hold, same)
    for i in range(count):
        stats[i, 2:3, :] = mean[i : i + 1]
        stats[i, 3:4, :] = scale[i : i + 1]
    gain2, shift2 = vec(W_SECOND_GAIN), vec(W_SECOND_SHIFT)

    def second(i, r):
        rows = pl.ds(r, CHUNK)
        pre = (out1[i, rows, :] - stats[i, 2:3, :]) * stats[i, 3:4, :] * gain2 + shift2
        act = pre * sigmoid(pre)
        act2[i, rows, :] = act.astype(BF16)
        store_shifted(shifted, i, r, act, False)

    over_chunks(count, second)
    ready(ACT2)
    need(W_SECOND_CONV)
    kernel = w[W_SECOND_CONV]
    low = [kernel[di].reshape(3 * C, C).astype(BF16) for di in range(3)]
    bias = vec(W_SECOND_BIAS)
    for i in range(count):
        mid[i] = convolve(shifted, i, low) + (x[i] + bias)

    mean, scale = norm_stats(count, mid, hold, same)
    for i in range(count):
        stats[i, 4:5, :] = mean[i : i + 1]
        stats[i, 5:6, :] = scale[i : i + 1]
        stats[i, 6:8, :] = jnp.zeros((2, C), F32)
    ready(STATS)
    gain3, shift3 = vec(W_ATTEND_GAIN), vec(W_ATTEND_SHIFT)

    def third(i, r):
        rows = pl.ds(r, CHUNK)
        pre = (mid[i, rows, :] - stats[i, 4:5, :]) * stats[i, 5:6, :] * gain3 + shift3
        normed[i, rows, :] = pre.astype(BF16)

    over_chunks(count, third)
    flat = normed[0:count].reshape(count * TOK, C)
    need(W_TRIPLE_WEIGHT)
    need(W_OUTPUT_WEIGHT)
    w_triple = w[W_TRIPLE_WEIGHT][...].astype(BF16)
    w_out = w[W_OUTPUT_WEIGHT][...].astype(BF16)
    for i in range(count):
        for part, name in enumerate((W_QUERY_BIAS, None, W_VALUE_BIAS)):
            v = dot(normed[i], w_triple[:, part * C : (part + 1) * C])
            if name is not None:
                v = v + vec(name)
            triple[i, :, part * C : (part + 1) * C] = v.astype(BF16)

    need(COT)
    cot_low = cot[0:count].reshape(count * TOK, C).astype(BF16)
    for i in range(count):
        dmixed[i] = dot(cot[i].astype(BF16), w_out, NT).astype(BF16)

    factor = 1.0 / math.sqrt(C)
    query_sum = jnp.zeros((1, C), F32)
    value_sum = jnp.zeros((1, C), F32)
    for i in range(count):
        q = triple[i, :, 0:C]
        k = triple[i, :, C : 2 * C]
        v = triple[i, :, 2 * C : 3 * C]
        dm = dmixed[i]
        s = dot(q, k, NT) * factor
        e = jnp.exp(s - jnp.max(s, axis=1, keepdims=True))
        p = e * (1.0 / jnp.sum(e, axis=1, keepdims=True))
        p_low = p.astype(BF16)
        mixed[i] = dot(p_low, v).astype(BF16)
        dp = dot(dm, v, NT)
        ds = (p * (dp - jnp.sum(p * dp, axis=1, keepdims=True))).astype(BF16)
        dq = dot(ds, k) * factor
        dk = dot(ds, q, TN) * factor
        dv = dot(p_low, dm, TN)
        query_sum = query_sum + jnp.sum(dq, axis=0, keepdims=True)
        value_sum = value_sum + jnp.sum(dv, axis=0, keepdims=True)
        dtriple[i, :, 0:C] = dq.astype(BF16)
        dtriple[i, :, C : 2 * C] = dk.astype(BF16)
        dtriple[i, :, 2 * C : 3 * C] = dv.astype(BF16)

    flat_mixed = mixed[0:count].reshape(count * TOK, C)
    bias = vec(W_OUTPUT_BIAS)
    for i in range(count):
        out[i] = dot(mixed[i], w_out) + (mid[i] + bias)
    ready(OUT)
    flat_d = dtriple[0:count].reshape(count * TOK, 3 * C)
    gw_out = dot(flat_mixed, cot_low, TN)
    gw_triple = dot(flat, flat_d, TN)
    if accumulate is None:
        g_out[...] = gw_out
        g_triple[...] = gw_triple
        ready(G_OUT)
        ready(G_TRIPLE)
    else:
        accumulate(gw_out, gw_triple)
    for i in range(count):
        dnormed[i] = dot(dtriple[i], w_triple, NT)

    def sums3(i, r):
        rows = pl.ds(r, CHUNK)
        d = dnormed[i, rows, :]
        unit = (mid[i, rows, :] - stats[i, 4:5, :]) * stats[i, 5:6, :]
        return d, d * unit, cot[i, rows, :]

    sum_d, sum_du, sum_cot = column_sums(count, 3, sums3, hold)
    first_mean = group_mean(sum_d * gain3, same)
    second_mean = group_mean(sum_du * gain3, same)

    def inner3(i, r):
        rows = pl.ds(r, CHUNK)
        d = dnormed[i, rows, :] * gain3
        scaled = stats[i, 5:6, :]
        unit = (mid[i, rows, :] - stats[i, 4:5, :]) * scaled
        m1 = first_mean[i : i + 1, :]
        m2 = second_mean[i : i + 1, :]
        g = (d - m1 - unit * m2) * scaled + cot[i, rows, :]
        dmid[i, rows, :] = g
        return (g,)

    (sum_mid,) = column_sums(count, 1, inner3, hold)
    ready(DMID)
    pieces = [
        jnp.sum(sum_cot, axis=0, keepdims=True), query_sum, value_sum,
        jnp.sum(sum_du, axis=0, keepdims=True), jnp.sum(sum_d, axis=0, keepdims=True),
        jnp.sum(sum_mid, axis=0, keepdims=True),
    ]
    return pieces


BIG = {
    W_FIRST_CONV: (3, 3, C, C), W_EMBED_WEIGHT: (TEMB, C), W_SECOND_CONV: (3, 3, C, C),
    W_TRIPLE_WEIGHT: (C, 3 * C), W_OUTPUT_WEIGHT: (C, C),
}
SMALL = tuple(name for name in WEIGHTS if name not in BIG)


def front_scratch(count):
    return [
        pltpu.VMEM((count, PAD, 3 * C), BF16),
        pltpu.VMEM((16, 8, C), F32),
        pltpu.VMEM((count, TOK, C), F32),
        pltpu.VMEM((count, TOK, C), BF16),
        pltpu.VMEM((count, TOK, 3 * C), BF16),
        pltpu.VMEM((count, TOK, C), BF16),
        pltpu.VMEM((count, TOK, C), BF16),
        pltpu.VMEM((count, TOK, 3 * C), BF16),
        pltpu.VMEM((count, TOK, C), F32),
        pltpu.VMEM((C, C), BF16),
    ]


def held(count):
    return [pltpu.VMEM(BIG[name], F32) for name in BIG] + [
        pltpu.VMEM((count, TOK, C), F32),
        pltpu.VMEM((count, TOK, C), F32),
        pltpu.VMEM((count, TOK, C), F32),
        pltpu.VMEM((count, TOK, C), F32),
        pltpu.VMEM((count, TOK, C), F32),
        pltpu.VMEM((count, TOK, C), BF16),
        pltpu.VMEM((count, TOK, C), BF16),
        pltpu.VMEM((count, 8, C), F32),
    ]


def small_copies(copies, small, held_small):
    for r, name in enumerate(SMALL):
        copies.start((SMALL_ONE, name), small[name], held_small.at[r])
    return {name: held_small.at[r] for r, name in enumerate(SMALL)}


HELD = tuple(BIG) + (X, COT, OUT, DMID, OUT1, ACT1, ACT2, STATS)


class Copies:
    def __init__(self, sems):
        self.sems = sems
        self.count = 0
        self.by_name = {}
        self.open = []

    def add(self, name, src, dst):
        copy = pltpu.make_async_copy(src, dst, self.sems.at[self.count])
        self.count += 1
        self.by_name[name] = copy
        return copy

    def start(self, name, src, dst):
        self.add(name, src, dst).start()
        self.open.append(name)

    def need(self, name):
        if name in self.open:
            self.open.remove(name)
            self.by_name[name].wait()

    def finish(self):
        for name in list(self.open):
            self.need(name)


def store_sums(sums, pieces, before=None):
    sums[...] = jnp.zeros((SUMS, C), F32) if before is None else before[...]
    for r, piece in enumerate(pieces):
        sums[r : r + 1, :] += piece


FRONT_SEMS = 48


def kernel_one(times, images, cotangent, *rest):
    small = dict(zip(SMALL, rest[: len(SMALL)]))
    rest = rest[len(SMALL) :]
    big = dict(zip(BIG, rest[: len(BIG)]))
    rest = rest[len(BIG) :]
    out, dmid, out1, act1, act2, stats, g_triple, g_out, sums = rest[:9]
    rest = rest[9:]
    scratch, rest = rest[:10], rest[10:]
    kept = dict(zip(HELD, rest[: len(HELD)]))
    v_triple, v_out, held_small, sems = rest[len(HELD) :]
    n = WORK - 1
    copies = Copies(sems)
    copies.start(X, images.at[0:n], kept[X])
    small = small_copies(copies, small, held_small)
    for name in (W_EMBED_WEIGHT, W_FIRST_CONV):
        copies.start(name, big[name], kept[name])
    scratch[-1][...] = group_matrix()
    moments = [times[0, 0, i].astype(F32) for i in range(n)]
    targets = {
        OUT: out.at[0:n], DMID: dmid.at[0:n], OUT1: out1.at[0:n], ACT1: act1.at[0:n], ACT2: act2.at[0:n],
        STATS: stats.at[0:n], G_TRIPLE: g_triple, G_OUT: g_out,
    }
    sources = {**kept, G_TRIPLE: v_triple, G_OUT: v_out}

    def need(name):
        if name == X:
            for first in [X, W_EMBED_WEIGHT, W_FIRST_CONV] + [(SMALL_ONE, v) for v in SMALL]:
                copies.need(first)
            for later in (W_SECOND_CONV, W_TRIPLE_WEIGHT, W_OUTPUT_WEIGHT):
                copies.start(later, big[later], kept[later])
            copies.start(COT, cotangent.at[0:n], kept[COT])
        if name == W_SECOND_CONV:
            for later in (W_SECOND_CONV, W_TRIPLE_WEIGHT, W_OUTPUT_WEIGHT, COT):
                copies.need(later)

    def ready(name):
        for v in {ACT2: (OUT1, ACT1, ACT2), DMID: (OUT, DMID, STATS, G_TRIPLE, G_OUT)}.get(name, ()):
            copies.start((TO, v), sources[v], targets[v])

    w = {**small, **{name: kept[name] for name in BIG}}
    pieces = front(
        n, kept[X], kept[COT], moments, w, kept[OUT], kept[DMID], kept[OUT1], kept[ACT1], kept[ACT2],
        kept[STATS], None, v_triple, v_out, *scratch, None, need, ready,
    )
    store_sums(sums, pieces)
    copies.finish()


ORDERS = (("xyz", "zxy"), ("yzx", "zxy"), ("yxz", "yzx"))
CHUNK_A, CHUNK_B, CHUNK_C = ORDERS[0], ORDERS[1], ORDERS[2]


def chip_bits():
    b, t = lax.axis_index(BUCKET), lax.axis_index(BATCH)
    return {"x": b % 2, "y": (b // 2) % 2, "z": (t // 2) % 2}


def owner_codes(order):
    bits = chip_bits()
    even, odd = (bits[o[0]] * 4 + bits[o[1]] * 2 + bits[o[2]] for o in order)
    return lax.axis_index(BATCH) % 2, even, odd


def scatter_unit(dst, unit, value, codes):
    core, even, odd = codes
    for block in range(16):
        half, low = divmod(block, 8)
        mine = jnp.where(core == half, 0, 1)
        code = even if half == 0 else odd
        dst[mine * 8 + (low ^ code), unit] = value[16 * block : 16 * block + 16]


def place_offset(counts, source):
    keeps = counts[0, 0] >= WORK
    return keeps, jnp.where(keeps, 0, source[0, 0] ^ lax.axis_index(BUCKET))


def kernel_two(n_bucket, times, counts, source, images, cotangent, *rest):
    arrived, rest = rest[: n_bucket - 1], rest[n_bucket - 1 :]
    small = dict(zip(SMALL, rest[: len(SMALL)]))
    rest = rest[len(SMALL) :]
    big = dict(zip(BIG, rest[: len(BIG)]))
    rest = rest[len(BIG) :]
    sums_in, gt_in, go_in, dmid_in, act2_in = rest[:5]
    rest = rest[9:]
    out, dmid, out1, act1, act2, stats, sums, give, keep, give_c, keep_c, last, notes = rest[:13]
    rest = rest[13:]
    scratch, rest = rest[:10], rest[10:]
    kept = dict(zip(HELD, rest[: len(HELD)]))
    full_act, full_shift, full_mid, blocks, blocks_c, v_triple, v_out, note, held_small, sems = rest[len(HELD) :]
    n = WORK - 1
    copies = Copies(sems)
    keeps, offset = place_offset(counts, source)

    def rows_of(k):
        return arrived[k - 1].at[0:TOK]

    choose = copies.add(X, images.at[n], kept[X].at[0])
    pl.when(keeps)(lambda: choose.start())
    pl.when(jnp.logical_not(keeps) & (offset == 0))(
        lambda: pltpu.make_async_copy(images.at[WORK], kept[X].at[0], sems.at[0]).start()
    )
    for k in range(1, n_bucket):
        pl.when(offset == k)(
            lambda k=k: pltpu.make_async_copy(rows_of(k), kept[X].at[0], sems.at[0]).start()
        )
    copies.open.append(X)
    copies.start(W_FIRST_CONV, big[W_FIRST_CONV], kept[W_FIRST_CONV])
    for k in range(1, n_bucket):
        copies.start((NOTE, k), arrived[k - 1].at[TOK : TOK + 8], note.at[k])
    small = small_copies(copies, small, held_small)
    copies.start(W_EMBED_WEIGHT, big[W_EMBED_WEIGHT], kept[W_EMBED_WEIGHT])
    same = scratch[-1]
    same[...] = group_matrix()
    codes, codes_c = owner_codes(CHUNK_A), owner_codes(CHUNK_C)
    first_wave = [X, W_EMBED_WEIGHT, W_FIRST_CONV] + [(SMALL_ONE, v) for v in SMALL]
    for name in first_wave + [(NOTE, k) for k in range(1, n_bucket)]:
        copies.need(name)
    for name in (W_SECOND_CONV, W_TRIPLE_WEIGHT, W_OUTPUT_WEIGHT):
        copies.start(name, big[name], kept[name])
    copies.start(COT, cotangent.at[n : n + 1], kept[COT])
    copies.start(GT, gt_in, v_triple)
    copies.start(GO, go_in, v_out)
    copies.start(FULL_ACT, act2_in.at[0:n], full_act.at[0:n])
    copies.start(FULL_MID, dmid_in.at[0:n], full_mid)
    moment = jnp.where(keeps, times[0, 0, n], times[0, 0, WORK]).astype(F32)
    moment = jnp.full((1, 1), moment, F32)
    for k in range(1, n_bucket):
        moment = jnp.where(offset == k, note[k, 0:1, 0:1], moment)

    lane = lax.broadcasted_iota(jnp.int32, (1, C), 1)
    clock = jnp.where(lane == n, moment, 0.0)
    for i in range(n):
        clock = jnp.where(lane == i, times[0, 0, i].astype(F32), clock)
    notes[...] = jnp.zeros(notes.shape, F32)
    notes[0:1, :] = clock
    if n_bucket == 4:
        even = codes[0] == 0
        neighbour = jnp.where(even, note[1, 0:1, 1:2], note[2, 0:1, 1:2])
        first = jnp.where(even, 1.0, 2.0)
        notes[1:2, :] = jnp.broadcast_to(jnp.where(neighbour == 3.0, 1.0, 0.0), (1, C))
        notes[2:3, :] = jnp.broadcast_to(jnp.where(neighbour == first, 1.0, 0.0), (1, C))

    def accumulate(gw_out, gw_triple):
        scatter_unit(blocks_c, 3, gw_out + v_out[...], codes_c)
        total = gw_triple + v_triple[...]
        for part in range(3):
            scatter_unit(blocks_c, part, total[:, part * C : (part + 1) * C], codes_c)

    targets = {
        OUT: out.at[n:WORK], DMID: dmid.at[n:WORK], OUT1: out1.at[n:WORK], ACT1: act1.at[n:WORK],
        ACT2: act2.at[n:WORK], STATS: stats.at[n:WORK],
    }
    def need(name):
        if name == W_SECOND_CONV:
            for later in (W_SECOND_CONV, W_TRIPLE_WEIGHT, W_OUTPUT_WEIGHT, COT, GT, GO, FULL_ACT, FULL_MID):
                copies.need(later)

    def ready(name):
        if name == DMID:
            for v in targets:
                copies.start((TO, v), kept[v], targets[v])
            copies.start((TO, LAST), kept[X].at[0], last)
            copies.start((TO, GIVE_C), blocks_c.at[8:16], give_c)
            copies.start((TO, KEEP_C), blocks_c.at[0:8], keep_c)

    w = {**small, **{name: kept[name] for name in BIG}}
    pieces = front(
        1, kept[X], kept[COT], [moment], w, kept[OUT], kept[DMID], kept[OUT1], kept[ACT1], kept[ACT2],
        kept[STATS], None, None, None, *scratch, accumulate, need, ready,
    )
    store_sums(sums, pieces, sums_in)

    clear_borders(full_shift, WORK)

    def early(i, r):
        store_shifted(full_shift, i, r, full_mid[i, pl.ds(r, CHUNK), :], True)

    def late(i, r):
        store_shifted(full_shift, i + n, r, kept[DMID][i, pl.ds(r, CHUNK), :], True)

    over_chunks(n, early)
    over_chunks(1, late)
    full_act[n] = kept[ACT2][0]
    act = full_act[...].reshape(WORK * TOK, C)
    for di in range(3):
        g = dot(act, window(full_shift, WORK, 2 - di), TN)
        for dj in range(3):
            scatter_unit(blocks, di * 3 + dj, g[:, dj * C : (dj + 1) * C], codes)
    copies.start((TO, GIVE), blocks.at[8:16], give)
    copies.start((TO, KEEP), blocks.at[0:8], keep)
    copies.finish()


def swish_norm_backward(dact, values, base, stats, row, gain, shift, hold, same, dpre, write):
    def sums_of(i, r):
        rows = pl.ds(r, CHUNK)
        unit = (base[i, rows, :] - stats[i, row : row + 1, :]) * stats[i, row + 1 : row + 2, :]
        pre = unit * gain + shift
        s = sigmoid(pre)
        d = dact[i, rows, :] * (s * (1.0 + pre * (1.0 - s)))
        dpre[i, rows, :] = d
        return d, d * unit

    sum_d, sum_du = column_sums(WORK, 2, sums_of, hold)
    first_mean = group_mean(sum_d * gain, same)
    second_mean = group_mean(sum_du * gain, same)

    def inner(i, r):
        rows = pl.ds(r, CHUNK)
        scaled = stats[i, row + 1 : row + 2, :]
        unit = (base[i, rows, :] - stats[i, row : row + 1, :]) * scaled
        m1 = first_mean[i : i + 1, :]
        m2 = second_mean[i : i + 1, :]
        return write(i, r, (dpre[i, rows, :] * gain - m1 - unit * m2) * scaled)

    sums = column_sums(WORK, 1, inner, hold)[0]
    return sum_d, sum_du, sums


def conv_backward(shifted, kernel, dact):
    low = [jnp.concatenate([kernel[di, dj].astype(BF16) for dj in range(3)], axis=1) for di in range(3)]
    for i in range(WORK):
        total = None
        for di in range(3):
            part = dot(shifted[i, SIDE * (2 - di) : SIDE * (2 - di) + TOK, :], low[di], NT)
            total = part if total is None else total + part
        dact[i] = total


def kernel_three(notes, dmid_in, out1_in, act1_in, stats, sums_in, kernel_in, gain_ref, shift_ref,
                 give, keep, low, sums, rows_out,
                 shifted, hold, dact, dpre, same_ref, dmid, out1, act1, kernel, blocks, v_low, v_small, sems):
    copies = Copies(sems)
    copies.start(GAIN, gain_ref, v_small.at[0])
    copies.start(SHIFT, shift_ref, v_small.at[1])
    gain_ref, shift_ref = v_small.at[0], v_small.at[1]
    copies.start(DMID, dmid_in, dmid)
    copies.start(KERNEL, kernel_in, kernel)
    copies.start(OUT1, out1_in, out1)
    copies.start(ACT1, act1_in, act1)
    same_ref[...] = group_matrix()
    same = same_ref[...]
    codes = owner_codes(CHUNK_B)
    clear_borders(shifted, WORK)
    copies.need(DMID)

    def load(i, r):
        store_shifted(shifted, i, r, dmid[i, pl.ds(r, CHUNK), :], True)

    over_chunks(WORK, load)
    copies.need(KERNEL)
    conv_backward(shifted, kernel, dact)
    for name in (OUT1, ACT1, GAIN, SHIFT):
        copies.need(name)

    def write(i, r, g):
        v_low[i, pl.ds(r, CHUNK), :] = g.astype(BF16)
        store_shifted(shifted, i, r, g, True)
        return (g,)

    sum_d, sum_du, sum_first = swish_norm_backward(
        dact, None, out1, stats, 2, gain_ref[...], shift_ref[...], hold, same, dpre, write
    )
    copies.start((TO, LOW), v_low, low)

    act = act1[...].reshape(WORK * TOK, C)
    for di in range(3):
        g = dot(act, window(shifted, WORK, 2 - di), TN)
        for dj in range(3):
            scatter_unit(blocks, di * 3 + dj, g[:, dj * C : (dj + 1) * C], codes)
    copies.start((TO, GIVE), blocks.at[8:16], give)
    copies.start((TO, KEEP), blocks.at[0:8], keep)
    sums[...] = sums_in[...]
    sums[R_SEC_GAIN : R_SEC_GAIN + 1, :] = jnp.sum(sum_du, axis=0, keepdims=True)
    sums[R_SEC_SHIFT : R_SEC_SHIFT + 1, :] = jnp.sum(sum_d, axis=0, keepdims=True)
    sums[R_EMB_BIAS : R_EMB_BIAS + 1, :] = jnp.sum(sum_first, axis=0, keepdims=True)
    core = lax.axis_index(BATCH) % 2
    place = chip_place() * 2 + core
    spots = lax.broadcasted_iota(jnp.int32, (4, C), 0) * C + lax.broadcasted_iota(jnp.int32, (4, C), 1)
    clocks = jnp.zeros((4, C), F32)
    for i in range(WORK):
        clocks = jnp.where(spots == place * WORK + i, notes[0:1, i : i + 1], clocks)
    sums[R_CLOCKS : R_CLOCKS + 4, :] = clocks
    four = sum_first[0:WORK]
    both = jnp.concatenate([four, four], axis=0)
    half = lax.broadcasted_iota(jnp.int32, (8, C), 0) // WORK
    rows_out[...] = jnp.where(half == core, both, 0.0)
    copies.finish()


def kernel_four(n_bucket, counts, source, images, last, dmid_in, low_in, stats, sums_in, rows_in, kernel_in, gain_ref, shift_ref,
                grad, back, sums,
                shifted, hold, dact, dpre, same_ref, dmid, base, low, kernel, v_back, v_small, sems):
    n = WORK - 1
    copies = Copies(sems)
    copies.start(GAIN, gain_ref, v_small.at[0])
    copies.start(SHIFT, shift_ref, v_small.at[1])
    gain_ref, shift_ref = v_small.at[0], v_small.at[1]
    copies.start(LOW, low_in, low)
    copies.start(KERNEL, kernel_in, kernel)
    copies.start(BASE, images.at[0:n], base.at[0:n])
    copies.start(LAST, last, base.at[n])
    copies.start(DMID, dmid_in, dmid)
    same_ref[...] = group_matrix()
    same = same_ref[...]
    clear_borders(shifted, WORK)
    copies.need(LOW)

    def load(i, r):
        store_shifted(shifted, i, r, low[i, pl.ds(r, CHUNK), :].astype(F32), True)

    over_chunks(WORK, load)
    copies.need(KERNEL)
    conv_backward(shifted, kernel, dact)
    for name in (BASE, LAST, DMID, GAIN, SHIFT):
        copies.need(name)

    def write(i, r, g):
        rows = pl.ds(r, CHUNK)
        dpre[i, rows, :] = g + dmid[i, rows, :]
        return (g,)

    sum_d, sum_du, _ = swish_norm_backward(
        dact, None, base, stats, 0, gain_ref[...], shift_ref[...], hold, same, dpre, write
    )
    copies.start((TO, GRAD), dpre.at[0:n], grad.at[0:n])
    keeps, offset = place_offset(counts, source)
    if n_bucket == 4:
        even = lax.axis_index(BATCH) % 2 == 0
        first = jnp.where(even, 1, 2)
        v_back[0] = jnp.where((offset & first) != 0, dpre[n], 0.0)
        v_back[1] = jnp.where(offset == 3 - first, dpre[n], 0.0)
    else:
        for k in range(1, n_bucket):
            v_back[k - 1] = jnp.where(offset == k, dpre[n], 0.0)
    copies.start((TO, BACK), v_back, back)
    dmid[n] = jnp.where(keeps, dpre[n], 0.0)
    copies.start((TO, SLOT), dmid.at[n], grad.at[n])
    sums[0:SUMS] = sums_in[...]
    sums[SUMS : SUMS + 8] = rows_in[...]
    sums[R_FIRST_GAIN : R_FIRST_GAIN + 1, :] = jnp.sum(sum_du, axis=0, keepdims=True)
    sums[R_FIRST_SHIFT : R_FIRST_SHIFT + 1, :] = jnp.sum(sum_d, axis=0, keepdims=True)
    copies.finish()


def kernel_pack(times, counts, source, images, out, sem):
    copy = pltpu.make_async_copy(images.at[WORK], out.at[0:TOK], sem)
    copy.start()
    _, offset = place_offset(counts, source)
    lane = lax.broadcasted_iota(jnp.int32, (8, C), 1)
    moment = times[0, 0, WORK].astype(F32)
    out[TOK : TOK + 8] = jnp.where(lane == 0, moment, jnp.where(lane == 1, offset.astype(F32), 0.0))
    copy.wait()


def whole(shape):
    return pl.BlockSpec(shape, lambda *_: (0,) * len(shape), memory_space=pltpu.VMEM)


def part(shape, first):
    return pl.BlockSpec(shape, lambda *_: (first,) + (0,) * (len(shape) - 1), memory_space=pltpu.VMEM)


SMEM = pl.BlockSpec(memory_space=pltpu.SMEM)
ANY = pl.BlockSpec(memory_space=pl.ANY)
HBM = pl.BlockSpec(memory_space=pltpu.HBM)


def params(mebibytes=26):
    return pltpu.CompilerParams(vmem_limit_bytes=mebibytes * 1024 * 1024)


def shape(dims, dtype=F32):
    return jax.ShapeDtypeStruct(dims, dtype)


def weight_specs(w):
    return [whole(w[name].shape) for name in WEIGHTS]


def call_pack(timesteps, counts, source, images):
    return pl.pallas_call(
        kernel_pack,
        name="pack_spare",
        in_specs=[SMEM, SMEM, SMEM, ANY],
        out_specs=pl.BlockSpec(memory_space=pltpu.VMEM),
        out_shape=shape((TOK + 8, C)),
        scratch_shapes=[pltpu.SemaphoreType.DMA],
        cost_estimate=pl.CostEstimate(flops=20_000_000_000, bytes_accessed=1_000_000, transcendentals=0),
        compiler_params=params(),
    )(timesteps, counts, source, images)


VMEM = pl.BlockSpec(memory_space=pltpu.VMEM)
IMAGE_ARRAYS = (
    ((WORK, TOK, C), F32), ((WORK, TOK, C), F32), ((WORK, TOK, C), F32), ((WORK, TOK, C), BF16), ((WORK, TOK, C), BF16),
    ((WORK, 8, C), F32),
)


def call_one(timesteps, images, cot, w):
    n = WORK - 1
    return pl.pallas_call(
        kernel_one,
        name="front_of_own_images",
        in_specs=[SMEM, HBM, HBM] + [HBM] * (len(SMALL) + len(BIG)),
        out_specs=[ANY] * 8 + [VMEM],
        out_shape=[shape(*s) for s in IMAGE_ARRAYS] + [shape((C, 3 * C)), shape((C, C)), shape((SUMS, C))],
        scratch_shapes=front_scratch(n) + held(n)
        + [pltpu.VMEM((C, 3 * C), F32), pltpu.VMEM((C, C), F32), pltpu.VMEM((len(SMALL), 1, C), F32),
           pltpu.SemaphoreType.DMA((FRONT_SEMS,))],
        cost_estimate=pl.CostEstimate(flops=20_000_000_000, bytes_accessed=1_000_000, transcendentals=0),
        compiler_params=params(),
    )(timesteps, images, cot, *[w[name] for name in SMALL], *[w[name] for name in BIG])


def call_two(timesteps, counts, source, images, cot, arrived, w, early):
    out, dmid, out1, act1, act2, stats, g_triple, g_out, sums = early
    n_bucket = len(arrived) + 1
    first = 5 + len(arrived) + len(SMALL) + len(BIG)
    half, half_c = (8, 9, 16, C), (8, 4, 16, C)
    return pl.pallas_call(
        lambda *refs: kernel_two(n_bucket, *refs),
        name="front_of_last_image",
        in_specs=[SMEM, SMEM, SMEM, HBM, HBM] + [ANY] * len(arrived) + [HBM] * (len(SMALL) + len(BIG))
        + [VMEM] + [ANY] * 8,
        out_specs=[ANY] * 6 + [VMEM] + [ANY] * 5 + [VMEM],
        out_shape=[shape(*s) for s in IMAGE_ARRAYS]
        + [shape((SUMS, C)), shape(half), shape(half), shape(half_c), shape(half_c), shape((TOK, C)), shape((8, C))],
        scratch_shapes=front_scratch(1) + held(1)
        + [
            pltpu.VMEM((WORK, TOK, C), BF16), pltpu.VMEM((WORK, PAD, 3 * C), BF16), pltpu.VMEM((WORK - 1, TOK, C), F32),
            pltpu.VMEM((16, 9, 16, C), F32), pltpu.VMEM((16, 4, 16, C), F32), pltpu.VMEM((C, 3 * C), F32), pltpu.VMEM((C, C), F32),
            pltpu.VMEM((n_bucket, 8, C), F32), pltpu.VMEM((len(SMALL), 1, C), F32),
            pltpu.SemaphoreType.DMA((FRONT_SEMS + n_bucket,)),
        ],
        input_output_aliases={first + 5: 0, first + 3: 1, first + 6: 2, first + 7: 3, first + 4: 4, first + 8: 5},
        cost_estimate=pl.CostEstimate(flops=20_000_000_000, bytes_accessed=1_000_000, transcendentals=0),
        compiler_params=params(),
    )(
        timesteps, counts, source, images, cot, *arrived, *[w[name] for name in SMALL], *[w[name] for name in BIG],
        sums, g_triple, g_out, dmid, act2, out, out1, act1, stats,
    )


def back_scratch():
    return [
        pltpu.VMEM((WORK, PAD, 3 * C), BF16),
        pltpu.VMEM((16, 8, C), F32),
        pltpu.VMEM((WORK, TOK, C), F32),
        pltpu.VMEM((WORK, TOK, C), F32),
        pltpu.VMEM((C, C), BF16),
    ]


def call_three(notes, dmid, out1, act1, stats, sums, w):
    full = (WORK, TOK, C)
    half = (8, 9, 16, C)
    return pl.pallas_call(
        kernel_three,
        name="back_to_first_out",
        in_specs=[VMEM, ANY, ANY, ANY, VMEM, VMEM, HBM, HBM, HBM],
        out_specs=[ANY, ANY, ANY, VMEM, VMEM],
        out_shape=[shape(half), shape(half), shape(full, BF16), shape((SUMS, C)), shape((8, C))],
        scratch_shapes=back_scratch()
        + [
            pltpu.VMEM(full, F32), pltpu.VMEM(full, F32), pltpu.VMEM(full, BF16), pltpu.VMEM((3, 3, C, C), F32),
            pltpu.VMEM((16, 9, 16, C), F32), pltpu.VMEM(full, BF16), pltpu.VMEM((2, 1, C), F32),
            pltpu.SemaphoreType.DMA((12,)),
        ],
        compiler_params=params(),
    )(notes, dmid, out1, act1, stats, sums, w[W_SECOND_CONV], w[W_SECOND_GAIN], w[W_SECOND_SHIFT])


def call_four(n_bucket, counts, source, images, last, dmid, low, stats, sums, rows, w):
    full = (WORK, TOK, C)
    backs = 2 if n_bucket == 4 else n_bucket - 1
    return pl.pallas_call(
        lambda *refs: kernel_four(n_bucket, *refs),
        name="back_to_images",
        in_specs=[SMEM, SMEM, HBM, ANY, ANY, ANY, VMEM, VMEM, VMEM, HBM, HBM, HBM],
        out_specs=[ANY, ANY, VMEM],
        out_shape=[shape((WORK + 1, TOK, C)), shape((backs, TOK, C)), shape((SUMS + 8, C))],
        scratch_shapes=back_scratch()
        + [
            pltpu.VMEM(full, F32), pltpu.VMEM(full, F32), pltpu.VMEM(full, BF16), pltpu.VMEM((3, 3, C, C), F32),
            pltpu.VMEM((backs, TOK, C), F32), pltpu.VMEM((2, 1, C), F32), pltpu.SemaphoreType.DMA((12,)),
        ],
        compiler_params=params(),
    )(counts, source, images, last, dmid, low, stats, sums, rows, w[W_FIRST_CONV], w[W_FIRST_GAIN], w[W_FIRST_SHIFT])


def assemble_kernel(orders, *refs):
    outs = list(refs[2 * len(orders) : -1])
    copies = Copies(refs[-1])
    for n, order in enumerate(orders):
        core, even, odd = owner_codes(order)
        target = outs.pop(0)
        units = refs[2 * n].shape[1]
        beside = outs.pop(0) if units == 4 else None
        for half in range(2):
            src = refs[2 * n + half]
            holder = core if half == 0 else 1 - core
            code = jnp.where(holder == 0, even, odd)
            for low in range(8):
                block = holder * 8 + (low ^ code)
                rows = pl.ds(pl.multiple_of(block * 16, 16), 16)
                if units == 9:
                    copies.start((n, half, low), src.at[low], target.at[:, rows, :])
                    continue
                for p in range(3):
                    copies.start((n, half, low, p), src.at[low, p], target.at[rows, p * C : (p + 1) * C])
                copies.start((n, half, low), src.at[low, 3], beside.at[rows, :])
    copies.finish()


def assemble(orders, *halves):
    out_shape = []
    for own in halves[::2]:
        out_shape += [shape((9, C, C))] if own.shape[1] == 9 else [shape((C, 3 * C)), shape((C, C))]
    return pl.pallas_call(
        lambda *refs: assemble_kernel(orders, *refs),
        name="assemble",
        in_specs=[ANY] * len(halves),
        out_specs=[ANY] * len(out_shape),
        out_shape=out_shape,
        scratch_shapes=[pltpu.SemaphoreType.DMA((16 + 16 * 4,))],
        cost_estimate=pl.CostEstimate(flops=1, bytes_accessed=1, transcendentals=0),
        compiler_params=params(2),
    )(*halves)


def high_code():
    b, t = lax.axis_index(BUCKET), lax.axis_index(BATCH)
    return (t // 4) * (lax.axis_size(BUCKET) // 4) + b // 4


def chip_place():
    bits = chip_bits()
    many = lax.axis_size(BUCKET) * lax.axis_size(BATCH) // 16
    return (bits["x"] * 4 + bits["y"] * 2 + bits["z"]) * many + high_code()


def embed_kernel(devices, order, gathered, sums, out, rows):
    core = lax.axis_index(BATCH) % 2
    bits = chip_bits()
    mine = bits["x"] * 4 + bits["y"] * 2 + bits["z"]
    high = high_code()
    many = devices // 16
    weight = {"x": 4, "y": 2, "z": 1}
    for place in range(devices // 2):
        rest, code = place % many, place // many
        turned = [
            sum(((code >> (2 - n)) & 1) * weight[o[n]] for n in range(3)) for o in order
        ]
        code = jnp.where(core == 0, turned[0], turned[1]) ^ mine
        rows[code * many + (rest ^ high)] = gathered[place]
    count = WORK * devices
    grads = rows[...].reshape(count, C)
    half = TEMB // 2
    moments = []
    for n in range(0, count, C):
        size = min(C, count)
        row = lax.broadcasted_iota(jnp.int32, (size, C), 0)
        lane = lax.broadcasted_iota(jnp.int32, (size, C), 1)
        clocks = sums[R_CLOCKS + n // C : R_CLOCKS + n // C + 1, :]
        moments.append(jnp.sum(jnp.where(row == lane, clocks, 0.0), axis=1, keepdims=True))
    moments = jnp.concatenate(moments, axis=0) if len(moments) > 1 else moments[0]
    frequency = jnp.exp(
        lax.broadcasted_iota(jnp.int32, (count, half), 1).astype(F32) * (-math.log(10000.0) / (half - 1))
    )
    angles = moments * frequency
    waves = jnp.concatenate([jnp.sin(angles), jnp.cos(angles)], axis=1)
    waves = waves * sigmoid(waves)
    out[...] = lax.dot_general(waves, grads, TN, precision=lax.Precision.HIGHEST, preferred_element_type=F32)


def embed_gradient(devices, order, gathered, sums):
    return pl.pallas_call(
        lambda *refs: embed_kernel(devices, order, *refs),
        name="embed_gradient",
        in_specs=[VMEM, VMEM],
        out_specs=VMEM,
        out_shape=shape((TEMB, C)),
        scratch_shapes=[pltpu.VMEM((devices // 2, 8, C), F32)],
        cost_estimate=pl.CostEstimate(flops=1, bytes_accessed=1, transcendentals=0),
        compiler_params=params(),
    )(gathered, sums)


AXES = (BUCKET, BATCH)


def solution(mesh):
    n_bucket, n_batch = mesh.shape[BUCKET], mesh.shape[BATCH]
    devices = n_bucket * n_batch

    def flips(fn):
        pairs = []
        for b in range(n_bucket):
            for t in range(n_batch):
                nb, nt = fn(b, t)
                pairs.append((b * n_batch + t, nb * n_batch + nt))
        return pairs

    def by_core(even, odd):
        def fn(b, t):
            kind, bit = even if t % 2 == 0 else odd
            return (b ^ bit, t) if kind == 0 else (b, t ^ bit)

        return flips(fn)

    x, y, z = (0, 1), (0, 2), (1, 2)
    core_perm = flips(lambda b, t: (b, t ^ 1))
    links = {"x": x, "y": y, "z": z}
    rest = []
    bit = 4
    while bit < n_bucket:
        rest.append((0, bit))
        bit *= 2
    bit = 4
    while bit < n_batch:
        rest.append((1, bit))
        bit *= 2
    rest_perms = [by_core(s, s) for s in rest]
    bucket_perms = [flips(lambda b, t, k=k: (b ^ k, t)) for k in range(1, n_bucket)]

    def send(v, perm):
        return lax.ppermute(v, AXES, perm)

    def after(v, *others):
        return lax.optimization_barrier((v,) + others)[0]

    def held_by(v, other):
        row = other.reshape(-1, C)[0:1]
        return v + 0.0 * row.reshape((1,) * (v.ndim - 1) + (C,))

    class Chunk:
        def __init__(self, order, give, keep, units):
            self.perms = [by_core(links[p], links[q]) for p, q in zip(*order)]
            self.rows = units * 16
            self.stage = 0
            self.size = give.shape
            self.keep = keep.reshape(2, 2, 2, self.rows, C)
            self.got = send(give, core_perm).reshape(2, 2, 2, self.rows, C)
            self.extra = None

        def step(self, *deps, late=None):
            n_rest = len(rest_perms)
            k = self.stage
            self.stage += 1
            if k < 3:
                out, self.keep = self.keep[1] + self.got[1], self.keep[0] + self.got[0]
                perm = self.perms[k]
            else:
                self.take()
                if k < 3 + n_rest:
                    perm = rest_perms[k - 3]
                else:
                    if k == 3 + n_rest:
                        self.keep = self.keep[None]
                    j = k - 3 - n_rest
                    perm = self.perms[2 - j] if j < 3 else core_perm
                out = self.keep
                if self.extra is not None and perm is not core_perm:
                    sums, rows = self.extra
                    out = jnp.concatenate([out.reshape(-1, C), sums, rows.reshape(-1, C)], axis=0)
            if late is not None:
                out = held_by(out, late)
            out = after(out, *deps)
            self.got = send(out, perm)
            return out

        def take(self):
            n_rest = len(rest_perms)
            k = self.stage - 1
            got = self.got
            if k == 3:
                self.keep = self.keep + got
                return
            if self.extra is not None:
                sums, rows = self.extra
                size = self.keep.size // C
                rows = jnp.concatenate([rows, got[size + SUMS :].reshape(rows.shape)], axis=0)
                self.extra = sums + got[size : size + SUMS], rows
                got = got[:size]
            got = got.reshape(self.keep.shape)
            if k <= 3 + n_rest:
                self.keep = self.keep + got
            else:
                self.keep = jnp.concatenate([self.keep, got], axis=0)

        def halves(self):
            dims = (8, self.rows // 16, 16, C)
            return self.keep.reshape(dims), self.got.reshape(dims)

    def shards(images, timesteps, counts, source, cotangent, *weights):
        w = dict(zip(WEIGHTS, weights))
        w = {k: v.reshape(1, C) if v.ndim == 1 else v for k, v in w.items()}
        slots = images[0, 0]
        cot = cotangent[0, 0]

        spare = call_pack(timesteps, counts, source, slots)
        arrived = [send(spare, p) for p in bucket_perms]
        early = call_one(timesteps, slots, cot, w)
        out, dmid, out1, act1, act2, stats, sums, give_a, keep_a, give_c, keep_c, last, notes = call_two(
            timesteps, counts, source, slots, cot, arrived, w, early
        )
        chunk_a = Chunk(CHUNK_A, give_a, keep_a, 9)
        chunk_c = Chunk(CHUNK_C, give_c, keep_c, 4)
        give_b, keep_b, low, sums, rows = call_three(notes, dmid, out1, act1, stats, sums, w)
        chunk_b = Chunk(CHUNK_B, give_b, keep_b, 9)

        tie = chunk_a.step()
        tie = chunk_c.step(tie)
        tie = chunk_b.step(tie)
        grad, back, extra = call_four(n_bucket, counts, source, slots, last, dmid, after(low, tie), stats, sums, rows, w)
        extra = extra + send(extra, core_perm)
        total = 3 + len(rest_perms) + 3
        home = None
        for k in range(1, total):
            if k == 3:
                chunk_c.extra = extra[:SUMS], extra[None, SUMS:]
            tie = chunk_a.step(tie)
            tie = chunk_c.step(tie)
            tie = chunk_b.step(tie, late=home if k == 5 else None)
            if n_bucket == 4:
                if k == 2:
                    hop = send(after(back[0], tie), by_core(x, y))
                if k == 3:
                    turn = after(jnp.where(notes[1:2] != 0.0, hop, back[1]), tie)
                    got = send(turn, by_core(y, x))
                if k == 4:
                    home = jnp.where(notes[2:3] != 0.0, hop, got)
                    grad = lax.dynamic_update_slice(grad, home[None], (WORK, 0, 0))
            elif k == 1:
                home = send(back[0], bucket_perms[0])
                for n in range(2, n_bucket):
                    home = home + send(back[n - 1], bucket_perms[n - 1])
                grad = lax.dynamic_update_slice(grad, home[None], (WORK, 0, 0))
        tie = chunk_c.step(tie)
        tie = chunk_a.step(tie)
        sums, rows = chunk_c.extra
        g_embed = embed_gradient(devices, CHUNK_C, rows, sums)
        tie = chunk_b.step(tie, late=g_embed)
        (g_second,) = assemble((CHUNK_A,), *chunk_a.halves())
        g_triple, g_out, g_first = assemble((CHUNK_C, CHUNK_B), *chunk_c.halves(), *chunk_b.halves())

        def vec(r):
            return sums[r]

        return (
            out[None, None], grad[None, None],
            vec(R_FIRST_GAIN), vec(R_FIRST_SHIFT), g_first.reshape(3, 3, C, C), g_embed, vec(R_EMB_BIAS),
            vec(R_SEC_GAIN), vec(R_SEC_SHIFT), g_second.reshape(3, 3, C, C), vec(R_SEC_BIAS),
            vec(R_ATT_GAIN), vec(R_ATT_SHIFT), g_triple, vec(R_QUERY_BIAS), vec(R_VALUE_BIAS),
            g_out, vec(R_OUT_BIAS),
        )

    placed = (
        P(BATCH, BUCKET, None, None, None), P(BATCH, BUCKET, None), P(BATCH, BUCKET),
        P(BATCH, BUCKET), P(BATCH, BUCKET, None, None, None),
    ) + (P(),) * 16
    return jax.shard_map(
        shards,
        mesh=mesh,
        in_specs=placed,
        out_specs=(P(BATCH, BUCKET, None, None, None),) * 2 + (P(),) * 16,
        check_vma=False,
    )
```
